32 devices in a mesh: dp: 8 (over y, x, core), tensor: 4 (over z).
Axes of the slice: x: 2, y: 2, z: 4, core: 2. Of those that a mesh axis runs over, the one named last changes fastest.
Arguments:
- tokens: bfloat16 [1024, 8, 1024], P('tensor', 'dp'), may hold values from -6 to 6
- cotangent: bfloat16 [1024, 8, 1024], P('tensor', 'dp'), may hold values from -6 to 6
- clip_mask: int32 [8], P('dp'), may hold values from 0 to 1, as said below
- positions: int32 [3, 8, 1024], P(None, 'dp'), may hold values from 0 to 15
- triple_weight: bfloat16 [2, 1024, 3, 1024], P(None, 'dp', None, 'tensor'), may hold values from -0.1875 to 0.1875
- triple_bias: bfloat16 [2, 3, 1024], P(None, None, 'tensor'), may hold values from -0.75 to 0.75
- exit_weight: bfloat16 [2, 1024, 1024], P(None, 'tensor', 'dp'), may hold values from -2 to 2
- expand_weight: bfloat16 [2, 1024, 4096], P(None, 'dp', 'tensor'), may hold values from -0.1875 to 0.1875
- expand_bias: bfloat16 [2, 4096], P(None, 'tensor'), may hold values from -4 to 4
- shrink_weight: bfloat16 [2, 4096, 1024], P(None, 'tensor', 'dp'), may hold values from -0.09375 to 0.09375
- norm_gain: bfloat16 [2, 2, 1024], replicated, may hold values from 0.5 to 1.5
- norm_shift: bfloat16 [2, 2, 1024], replicated, may hold values from -3 to 3
- branch_bias: bfloat16 [2, 2, 1024], replicated, may hold values from -4 to 4
Outputs:
- mixed: float32 [1024, 8, 1024], P('tensor', 'dp')
- tokens_gradient: float32 [1024, 8, 1024], P('tensor', 'dp')
- triple_gradient: float32 [2, 1024, 3, 1024], P(None, 'dp', None, 'tensor')
- triple_bias_gradient: float32 [2, 3, 1024], P(None, None, 'tensor')
- exit_gradient: float32 [2, 1024, 1024], P(None, 'tensor', 'dp')
- expand_gradient: float32 [2, 1024, 4096], P(None, 'dp', 'tensor')
- expand_bias_gradient: float32 [2, 4096], P(None, 'tensor')
- shrink_gradient: float32 [2, 4096, 1024], P(None, 'tensor', 'dp')
- gain_gradient: float32 [2, 2, 1024], replicated
- shift_gradient: float32 [2, 2, 1024], replicated
- branch_bias_gradient: float32 [2, 2, 1024], replicated
The draws below stay inside these ranges and needn't reach their ends.
Inputs may be any that keep to these rules, and one draw needn't show every extreme that they name: `clip_mask`: exactly 1 of the 8 slots hold 0.
All inputs are finite; a program needn't handle non-finite values.
Results may differ from the reference program's by a relative error of at most 0.015.
Values may be sent and summed in bfloat16 or wider, within the bound.
A program may use at most 128 MiB of HBM per device.

```python
import jax
import jax.numpy as jnp
from jax import lax

D = 1024
HEADS = 16
HEAD_DIM = 64
FF = 4096
ROT = 20
LAYERS = 2
SEQ = 1024
CLIPS = 8
EMPTY = 1
QBLOCK = 512


def draw_clip_mask(key, part):
    key = jax.random.fold_in(key, 7)
    shuffled = jax.random.permutation(key, CLIPS)
    return (shuffled >= EMPTY).astype(jnp.int32)


def touch_ends(values, own_key, least, largest):
    longest = values.shape.index(max(values.shape))
    spots = []
    for shift in (0, 1):
        where = [jax.random.randint(jax.random.fold_in(own_key, axis), (), 0, length) for axis, length in enumerate(values.shape)]
        where[longest] = (where[longest] + shift) % values.shape[longest]
        spots.append(tuple(where))
    return values.at[spots[0]].set(least).at[spots[1]].set(largest)


def steps_of(stream_key, extent, shards, smallest, largest):
    def one(axis_at, shards_of):
        draws = jax.random.uniform(jax.random.fold_in(jax.random.fold_in(stream_key, 6), axis_at), (shards_of,), jnp.float32, smallest / len(shards), largest / len(shards))
        return jnp.repeat(jnp.exp(draws), extent[axis_at] // shards_of).reshape((-1,) + (1,) * (len(extent) - axis_at - 1))

    level = one(*shards[0])
    for cut in shards[1:]:
        level = level * one(*cut)
    return level


def scatter_about(own_key, dims, spread, limit, split=(), kind=jnp.bfloat16):
    gain = steps_of(own_key, dims, split, -0.22, 0.18) if split else 1.0
    values = jax.random.normal(own_key, dims, jnp.float32) * spread * gain
    return jnp.minimum(jnp.maximum(values, -limit), limit).astype(kind)


def setup_inputs(seed: int = 0) -> dict:
    key_of = jax.random.split(jax.random.key(seed), 14)
    return {
        "tokens": scatter_about(key_of[0], (SEQ, CLIPS, D), 1.0, 6.0, ((0, 4), (1, 8))),
        "cotangent": scatter_about(key_of[1], (SEQ, CLIPS, D), 1.0, 6.0, ((0, 4), (1, 8))),
        "clip_mask": draw_clip_mask(jax.random.fold_in(key_of[13], 71), 0),
        "positions": touch_ends(jax.random.randint(key_of[3], (3, CLIPS, SEQ), 0, 16), jax.random.fold_in(key_of[3], 1), 0, 15).astype(jnp.int32),
        "triple_weight": scatter_about(key_of[4], (LAYERS, D, 3, D), D ** -0.5, 0.1875, ((1, 8), (3, 4))),
        "triple_bias": scatter_about(key_of[5], (LAYERS, 3, D), 0.05, 0.75, ((2, 4),)),
        "exit_weight": scatter_about(key_of[6], (LAYERS, D, D), (max(1, 10 * D // SEQ)) ** -0.5, 2.0, ((1, 4), (2, 8))),
        "expand_weight": scatter_about(key_of[7], (LAYERS, D, FF), D ** -0.5, 0.1875, ((1, 8), (2, 4))),
        "expand_bias": scatter_about(key_of[8], (LAYERS, FF), 0.3, 4.0, ((1, 4),)),
        "shrink_weight": scatter_about(key_of[9], (LAYERS, FF, D), FF ** -0.5, 0.09375, ((1, 4), (2, 8))),
        "norm_gain": jnp.clip(1.0 + 0.1 * jax.random.normal(key_of[10], (LAYERS, 2, D), jnp.float32), 0.5, 1.5).astype(jnp.bfloat16),
        "norm_shift": scatter_about(key_of[11], (LAYERS, 2, D), 0.2, 3.0),
        "branch_bias": scatter_about(key_of[12], (LAYERS, 2, D), 0.3, 4.0),
    }


@jax.custom_vjp
def low(v):
    return lax.optimization_barrier(v.astype(jnp.bfloat16)).astype(jnp.float32)

@jax.custom_vjp
def low_back(v):
    return v

def low_keep(v):
    return (low(v), None)

def low_pass(kept, grad):
    return (grad,)

def back_keep(v):
    return (v, None)

def back_low(kept, grad):
    return (low(grad),)
low.defvjp(low_keep, low_pass)
low_back.defvjp(back_keep, back_low)
EPSILON = 1e-06
HIGHEST = lax.Precision.HIGHEST

def rotary_tables(grid_rows):
    halfway = ROT // 2
    indices = jnp.arange(halfway, dtype=jnp.float32)
    frequency = 10000.0 ** (-indices / halfway)
    angles = grid_rows.astype(jnp.float32)[:, :, None] * frequency
    return (jnp.cos(angles)[:, :, None, :], jnp.sin(angles)[:, :, None, :])

def rotate(values, cosines, sines):
    halfway = ROT // 2
    pieces = []
    for coord_index in range(3):
        offset = coord_index * ROT
        former = values[..., offset:offset + halfway]
        latter = values[..., offset + halfway:offset + ROT]
        pieces.append(former * cosines[coord_index] - latter * sines[coord_index])
        pieces.append(latter * cosines[coord_index] + former * sines[coord_index])
    pieces.append(values[..., 3 * ROT:])
    return jnp.concatenate(pieces, axis=-1)

def normalize(values, gain_row, shift_row):
    center = values - lax.optimization_barrier(jnp.mean(values, axis=-1, keepdims=True))
    inverse = lax.rsqrt(lax.optimization_barrier(jnp.mean(center * center, axis=-1, keepdims=True)) + EPSILON)
    return center * inverse * gain_row + shift_row

def attention(queries, key_rows, values, factor):

    def one_block(query_block):
        scores = low_back(jnp.einsum('qhe,khe->hqk', query_block, key_rows, precision=HIGHEST) * factor)
        highest = lax.optimization_barrier(jnp.max(scores, axis=-1, keepdims=True))
        weights = jnp.exp(scores - highest)
        chances = low(weights / lax.optimization_barrier(jnp.sum(weights, axis=-1, keepdims=True)))
        return jnp.einsum('hqk,khe->qhe', chances, values, precision=HIGHEST)
    blocked = queries.reshape(SEQ // QBLOCK, QBLOCK, HEADS, HEAD_DIM)
    return lax.map(jax.checkpoint(one_block), blocked).reshape(SEQ, HEADS, HEAD_DIM)

def two_layers(hidden, grid_rows, params):
    cosines, sines = rotary_tables(grid_rows)
    factor = HEAD_DIM ** (-0.5)
    for layer_index in range(LAYERS):
        triple_weight, triple_bias, exit_weight, expand_weight, expand_bias, shrink_weight, gain_rows, shift_rows, biases = [array[layer_index] for array in params]
        normed = low(normalize(hidden, gain_rows[0], shift_rows[0]))
        mixed_triple = low_back(jnp.einsum('sd,dtf->stf', normed, triple_weight, precision=HIGHEST) + triple_bias)
        split_heads = mixed_triple.reshape(SEQ, 3, HEADS, HEAD_DIM)
        queries = low(rotate(split_heads[:, 0], cosines, sines))
        key_rows = low(rotate(split_heads[:, 1], cosines, sines))
        values = low(split_heads[:, 2])
        attended = low(low_back(attention(queries, key_rows, values, factor).reshape(SEQ, D)))
        hidden = hidden + low_back(jnp.dot(attended, exit_weight, precision=HIGHEST) + biases[0])
        normed = low(normalize(hidden, gain_rows[1], shift_rows[1]))
        inner_sum = low_back(jnp.dot(normed, expand_weight, precision=HIGHEST) + expand_bias)
        activated = low(jax.nn.gelu(inner_sum, approximate=False))
        hidden = hidden + low_back(jnp.dot(activated, shrink_weight, precision=HIGHEST) + biases[1])
    return hidden

def reference(tokens, cotangent, clip_mask, positions, triple_weight, triple_bias, exit_weight, expand_weight, expand_bias, shrink_weight, norm_gain, norm_shift, branch_bias):
    params = tuple((array.astype(jnp.float32) for array in (triple_weight, triple_bias, exit_weight, expand_weight, expand_bias, shrink_weight, norm_gain, norm_shift, branch_bias)))

    def per_clip(totals, pieces):
        clip_tokens, clip_grad, clip_live, grid_rows = pieces

        def forward(hidden, weights):
            return two_layers(hidden, grid_rows, weights) * clip_live.astype(jnp.float32)
        result, pullback = jax.vjp(forward, clip_tokens.astype(jnp.float32), params)
        hidden_grad, weight_grads = pullback(clip_grad.astype(jnp.float32))
        return (jax.tree.map(jnp.add, totals, weight_grads), (result, hidden_grad))
    inputs = (jnp.moveaxis(tokens, 1, 0), jnp.moveaxis(cotangent, 1, 0), clip_mask, jnp.moveaxis(positions, 1, 0))
    totals, (results, hidden_grads) = lax.scan(per_clip, jax.tree.map(jnp.zeros_like, params), inputs)
    mixed = jnp.moveaxis(results, 0, 1)
    tokens_gradient = jnp.moveaxis(hidden_grads, 0, 1)
    return (mixed, tokens_gradient, totals[0], totals[1], totals[2], totals[3], totals[4], totals[5], totals[6], totals[7], totals[8])
```

```python
import jax
import jax.numpy as jnp
from jax import lax
from jax.sharding import PartitionSpec as P

HEAD_DIM = 64
ROT = 20
LAYERS = 2
SEQ = 1024
QBLOCK = 512


DP = ("dh", "th")
TP = ("b", "tl")
SWAP = [(0, 0), (1, 2), (2, 1), (3, 3)]


def swap(array):
    return lax.ppermute(array, ("b", "th"), SWAP)


EPSILON = 1e-06
SQRT_HALF = 0.7071067811865476
ROOT_TWO_PI = 2.5066282746310002


def rotary_tables(positions):
    halfway = ROT // 2
    indices = jnp.arange(halfway, dtype=jnp.float32)
    frequency = 10000.0 ** (-indices / halfway)
    angles = jnp.transpose(positions.astype(jnp.float32), (0, 2, 1))[..., None] * frequency
    return (jnp.cos(angles)[:, :, :, None, :], jnp.sin(angles)[:, :, :, None, :])


def rotate(values, cosines, sines):
    halfway = ROT // 2
    pieces = []
    for coord_index in range(3):
        offset = coord_index * ROT
        former = values[..., offset : offset + halfway]
        latter = values[..., offset + halfway : offset + ROT]
        pieces.append(former * cosines[coord_index] - latter * sines[coord_index])
        pieces.append(latter * cosines[coord_index] + former * sines[coord_index])
    pieces.append(values[..., 3 * ROT :])
    return jnp.concatenate(pieces, axis=-1)


def normalize(values, gain_row, shift_row):
    center = values - jnp.mean(values, axis=-1, keepdims=True)
    inverse = lax.rsqrt(jnp.mean(center * center, axis=-1, keepdims=True) + EPSILON)
    scaled = center * inverse
    return (scaled * gain_row + shift_row, scaled, inverse)


def norm_back(upstream, scaled, inverse, gain_row):
    weighted = upstream * gain_row
    first_mean = jnp.mean(weighted, axis=-1, keepdims=True)
    second_mean = jnp.mean(weighted * scaled, axis=-1, keepdims=True)
    return inverse * (weighted - first_mean - scaled * second_mean)


def gelu_slope(inner_sum):
    return (
        0.5 * (1.0 + lax.erf(inner_sum * SQRT_HALF))
        + inner_sum * jnp.exp(-0.5 * inner_sum * inner_sum) / ROOT_TWO_PI
    )


def to_items(array):
    seq_length, clip_count, head_count, head_width = array.shape
    return jnp.transpose(array, (1, 2, 0, 3)).reshape(
        clip_count * head_count, seq_length, head_width
    )


def from_items(array, clip_count):
    item_count, seq_length, head_width = array.shape
    return jnp.transpose(
        array.reshape(clip_count, item_count // clip_count, seq_length, head_width), (2, 0, 1, 3)
    )


def attend(queries, key_items, values):
    factor = HEAD_DIM ** (-0.5)
    block_count = SEQ // QBLOCK

    def one_item(triple):
        query_rows, key_rows, value_rows = triple

        def one_block(query_block):
            scores = (
                jnp.einsum("qe,ke->qk", query_block, key_rows, preferred_element_type=jnp.float32)
                * factor
            )
            highest = jnp.max(scores, axis=-1, keepdims=True)
            weights = jnp.exp(scores - highest)
            summed = jnp.sum(weights, axis=-1, keepdims=True)
            chances = (weights / summed).astype(jnp.bfloat16)
            output = jnp.einsum(
                "qk,ke->qe", chances, value_rows, preferred_element_type=jnp.float32
            )
            return (output.astype(jnp.bfloat16), (highest + jnp.log(summed))[:, 0])

        outputs, logsums = lax.map(one_block, query_rows.reshape(block_count, QBLOCK, HEAD_DIM))
        return (outputs.reshape(SEQ, HEAD_DIM), logsums.reshape(SEQ))

    return lax.map(one_item, (queries, key_items, values))


def attend_back(queries, key_items, values, out_grads, logsums):
    factor = HEAD_DIM ** (-0.5)
    block_count = SEQ // QBLOCK

    def one_item(group):
        query_rows, key_rows, value_rows, grad_rows, logsum_rows = group

        def one_block(carry, blocked):
            key_total, value_total = carry
            query_block, grad_block, logsum_block = blocked
            scores = (
                jnp.einsum("qe,ke->qk", query_block, key_rows, preferred_element_type=jnp.float32)
                * factor
            )
            chances = jnp.exp(scores - logsum_block[:, None])
            value_total = value_total + jnp.einsum(
                "qk,qe->ke",
                chances.astype(jnp.bfloat16),
                grad_block,
                preferred_element_type=jnp.float32,
            )
            chance_grad = jnp.einsum(
                "qe,ke->qk", grad_block, value_rows, preferred_element_type=jnp.float32
            )
            center = jnp.sum(chances * chance_grad, axis=-1, keepdims=True)
            score_grad = (chances * (chance_grad - center)).astype(jnp.bfloat16)
            query_grad = (
                jnp.einsum("qk,ke->qe", score_grad, key_rows, preferred_element_type=jnp.float32)
                * factor
            )
            key_total = (
                key_total
                + jnp.einsum(
                    "qk,qe->ke", score_grad, query_block, preferred_element_type=jnp.float32
                )
                * factor
            )
            return ((key_total, value_total), query_grad)

        zeros = jnp.zeros((SEQ, HEAD_DIM), jnp.float32)
        blocked_rows = (
            query_rows.reshape(block_count, QBLOCK, HEAD_DIM),
            grad_rows.reshape(block_count, QBLOCK, HEAD_DIM),
            logsum_rows.reshape(block_count, QBLOCK),
        )
        (key_total, value_total), query_grads = lax.scan(one_block, (zeros, zeros), blocked_rows)
        return (query_grads.reshape(SEQ, HEAD_DIM), key_total, value_total)

    return lax.map(one_item, (queries, key_items, values, out_grads, logsums))


def shards(
    tokens,
    cotangent,
    clip_mask,
    positions,
    triple_weight,
    triple_bias,
    exit_weight,
    expand_weight,
    expand_bias,
    shrink_weight,
    norm_gain,
    norm_shift,
    branch_bias,
):
    tokens, cotangent, clip_mask, positions = [
        swap(array) for array in (tokens, cotangent, clip_mask, positions)
    ]
    triple_weight, triple_bias, exit_weight, expand_weight, expand_bias, shrink_weight = [
        swap(array)
        for array in (
            triple_weight,
            triple_bias,
            exit_weight,
            expand_weight,
            expand_bias,
            shrink_weight,
        )
    ]
    row_count = tokens.shape[0]
    clip_count = tokens.shape[1]
    local_width = triple_weight.shape[3]
    head_count = local_width // HEAD_DIM
    cosines, sines = rotary_tables(positions)
    live = clip_mask.astype(jnp.float32)[None, :, None]

    def spread_rows(normed):
        return lax.all_gather(normed, TP, axis=0, tiled=True)

    def spread_grads(upstream_low):
        return lax.all_gather(upstream_low, TP, axis=0, tiled=True)

    def collect_rows(operand, matrix, pattern):

        def partial_term(offset, row_span):
            return jnp.einsum(pattern, operand, matrix, preferred_element_type=jnp.float32)

        return lax.psum_scatter(
            partial_term(jnp.int32(0), row_count * lax.axis_size(TP)).astype(jnp.bfloat16),
            TP,
            scatter_dimension=0,
            tiled=True,
        ).astype(jnp.float32)

    def collect_grads(operand, matrix, pattern):

        def partial_term(offset, row_span):
            return jnp.einsum(pattern, operand, matrix, preferred_element_type=jnp.float32)

        return lax.psum_scatter(
            partial_term(jnp.int32(0), row_count * lax.axis_size(TP)).astype(jnp.bfloat16),
            TP,
            scatter_dimension=0,
            tiled=True,
        ).astype(jnp.float32)

    hidden = tokens.astype(jnp.float32)
    saved = []
    for layer_index in range(LAYERS):
        fetched = (
            lax.all_gather(triple_weight[layer_index], DP, axis=0, tiled=True),
            lax.all_gather(exit_weight[layer_index], DP, axis=1, tiled=True),
            lax.all_gather(expand_weight[layer_index], DP, axis=0, tiled=True),
            lax.all_gather(shrink_weight[layer_index], DP, axis=1, tiled=True),
        )
        triple_full, exit_full, expand_full, shrink_full = fetched
        gain_pair = norm_gain[layer_index].astype(jnp.float32)
        shift_pair = norm_shift[layer_index].astype(jnp.float32)
        bias_pair = branch_bias[layer_index].astype(jnp.float32)
        normed, scaled_one, inverse_one = normalize(hidden, gain_pair[0], shift_pair[0])
        gathered_one = spread_rows(normed.astype(jnp.bfloat16))
        mixed_triple = jnp.einsum(
            "scd,dtf->sctf", gathered_one, triple_full, preferred_element_type=jnp.float32
        ) + triple_bias[layer_index].astype(jnp.float32)
        split_heads = mixed_triple.reshape(SEQ, clip_count, 3, head_count, HEAD_DIM)
        query_items = to_items(rotate(split_heads[:, :, 0], cosines, sines).astype(jnp.bfloat16))
        key_items = to_items(rotate(split_heads[:, :, 1], cosines, sines).astype(jnp.bfloat16))
        value_items = to_items(split_heads[:, :, 2].astype(jnp.bfloat16))
        attended_items, logsums = attend(query_items, key_items, value_items)
        attended = from_items(attended_items, clip_count).reshape(SEQ, clip_count, local_width)
        hidden = hidden + (collect_rows(attended, exit_full, "sce,ed->scd") + bias_pair[0])
        normed, scaled_two, inverse_two = normalize(hidden, gain_pair[1], shift_pair[1])
        gathered_two = spread_rows(normed.astype(jnp.bfloat16))
        inner_sum = jnp.einsum(
            "scd,df->scf", gathered_two, expand_full, preferred_element_type=jnp.float32
        ) + expand_bias[layer_index].astype(jnp.float32)
        activated = jax.nn.gelu(inner_sum, approximate=False).astype(jnp.bfloat16)
        hidden = hidden + (collect_rows(activated, shrink_full, "scf,fd->scd") + bias_pair[1])
        saved.append(
            (
                gathered_one,
                scaled_one,
                inverse_one,
                query_items,
                key_items,
                value_items,
                logsums,
                attended,
                scaled_two,
                inverse_two,
                gathered_two,
                inner_sum,
                activated,
                fetched,
            )
        )
    mixed = hidden * live
    upstream = cotangent.astype(jnp.float32) * live
    collected = [None] * LAYERS
    gain_parts = [None] * LAYERS
    shift_parts = [None] * LAYERS
    bias_parts = [None] * LAYERS
    triple_bias_parts = [None] * LAYERS
    expand_bias_parts = [None] * LAYERS
    for layer_index in reversed(range(LAYERS)):
        (
            gathered_one,
            scaled_one,
            inverse_one,
            query_items,
            key_items,
            value_items,
            logsums,
            attended,
            scaled_two,
            inverse_two,
            gathered_two,
            inner_sum,
            activated,
            fetched,
        ) = saved[layer_index]
        triple_full, exit_full, expand_full, shrink_full = (
            lax.all_gather(triple_weight[layer_index], DP, axis=0, tiled=True),
            lax.all_gather(exit_weight[layer_index], DP, axis=1, tiled=True),
            lax.all_gather(expand_weight[layer_index], DP, axis=0, tiled=True),
            lax.all_gather(shrink_weight[layer_index], DP, axis=1, tiled=True),
        )
        gain_pair = norm_gain[layer_index].astype(jnp.float32)
        shrink_low = upstream.astype(jnp.bfloat16)
        bias_two = jnp.sum(shrink_low, axis=(0, 1), dtype=jnp.float32)
        full_grad = spread_grads(shrink_low)
        shrink_grad = jnp.einsum(
            "scf,scd->fd", activated, full_grad, preferred_element_type=jnp.float32
        )
        active_grad = jnp.einsum(
            "scd,fd->scf", full_grad, shrink_full, preferred_element_type=jnp.float32
        )
        inner_low = (active_grad * gelu_slope(inner_sum)).astype(jnp.bfloat16)
        expand_bias_parts[layer_index] = jnp.sum(inner_low, axis=(0, 1), dtype=jnp.float32)
        expand_grad = jnp.einsum(
            "scd,scf->df", gathered_two, inner_low, preferred_element_type=jnp.float32
        )
        normed_grad = collect_grads(inner_low, expand_full, "scf,df->scd")
        gain_two = jnp.sum(normed_grad * scaled_two, axis=(0, 1))
        shift_two = jnp.sum(normed_grad, axis=(0, 1))
        upstream = upstream + norm_back(normed_grad, scaled_two, inverse_two, gain_pair[1])
        branch_low = upstream.astype(jnp.bfloat16)
        bias_one = jnp.sum(branch_low, axis=(0, 1), dtype=jnp.float32)
        full_grad = spread_grads(branch_low)
        exit_grad = jnp.einsum(
            "sce,scd->ed", attended, full_grad, preferred_element_type=jnp.float32
        )
        attended_grad = jnp.einsum(
            "scd,ed->sce", full_grad, exit_full, preferred_element_type=jnp.float32
        ).astype(jnp.bfloat16)
        grad_items = to_items(attended_grad.reshape(SEQ, clip_count, head_count, HEAD_DIM))
        query_grad, key_grad, value_grad = attend_back(
            query_items, key_items, value_items, grad_items, logsums
        )
        query_back = rotate(from_items(query_grad, clip_count), cosines, -sines)
        key_back = rotate(from_items(key_grad, clip_count), cosines, -sines)
        value_back = from_items(value_grad, clip_count)
        triple_low = (
            jnp.stack([query_back, key_back, value_back], axis=2)
            .reshape(SEQ, clip_count, 3, local_width)
            .astype(jnp.bfloat16)
        )
        triple_bias_parts[layer_index] = jnp.sum(triple_low, axis=(0, 1), dtype=jnp.float32)
        triple_grad = jnp.einsum(
            "scd,sctf->dtf", gathered_one, triple_low, preferred_element_type=jnp.float32
        )
        normed_grad = collect_grads(triple_low, triple_full, "sctf,dtf->scd")
        gain_one = jnp.sum(normed_grad * scaled_one, axis=(0, 1))
        shift_one = jnp.sum(normed_grad, axis=(0, 1))
        upstream = upstream + norm_back(normed_grad, scaled_one, inverse_one, gain_pair[0])
        gain_parts[layer_index] = jnp.stack([gain_one, gain_two])
        shift_parts[layer_index] = jnp.stack([shift_one, shift_two])
        bias_parts[layer_index] = jnp.stack([bias_one, bias_two])
        collected[layer_index] = (
            lax.psum_scatter(triple_grad.astype(jnp.bfloat16), DP, scatter_dimension=0, tiled=True).astype(jnp.float32),
            lax.psum_scatter(exit_grad.astype(jnp.bfloat16), DP, scatter_dimension=1, tiled=True).astype(jnp.float32),
            lax.psum_scatter(expand_grad.astype(jnp.bfloat16), DP, scatter_dimension=0, tiled=True).astype(jnp.float32),
            lax.psum_scatter(shrink_grad.astype(jnp.bfloat16), DP, scatter_dimension=1, tiled=True).astype(jnp.float32),
        )
    stacked = [
        jnp.stack([collected[layer_index][member] for layer_index in range(LAYERS)])
        for member in range(4)
    ]
    triple_total, exit_total, expand_total, shrink_total = stacked
    gain_total, shift_total, bias_total = lax.psum(
        (jnp.stack(gain_parts), jnp.stack(shift_parts), jnp.stack(bias_parts)), DP + TP
    )
    triple_bias_total, expand_bias_total = lax.psum(
        (jnp.stack(triple_bias_parts), jnp.stack(expand_bias_parts)), DP
    )
    return (
        swap(mixed),
        swap(upstream),
        swap(triple_total),
        swap(triple_bias_total),
        swap(exit_total),
        swap(expand_total),
        swap(expand_bias_total),
        swap(shrink_total),
        gain_total,
        shift_total,
        bias_total,
    )


def solution(mesh):
    shape = (mesh.shape["dp"] // 2, 2, mesh.shape["tensor"] // 2, 2)
    fine = jax.sharding.Mesh(mesh.devices.reshape(shape), ("dh", "b", "th", "tl"))
    dp, tensor = ("dh", "b"), ("th", "tl")
    return jax.shard_map(
        shards,
        mesh=fine,
        in_specs=(
            P(tensor, dp, None),
            P(tensor, dp, None),
            P(dp),
            P(None, dp, None),
            P(None, dp, None, tensor),
            P(None, None, tensor),
            P(None, tensor, dp),
            P(None, dp, tensor),
            P(None, tensor),
            P(None, tensor, dp),
            P(),
            P(),
            P(),
        ),
        out_specs=(
            P(tensor, dp, None),
            P(tensor, dp, None),
            P(None, dp, None, tensor),
            P(None, None, tensor),
            P(None, tensor, dp),
            P(None, dp, tensor),
            P(None, tensor),
            P(None, tensor, dp),
            P(),
            P(),
            P(),
        ),
        check_vma=False,
    )
```

```python
import functools

import jax
import jax.numpy as jnp
from jax import lax
from jax.experimental import pallas as pl
from jax.experimental.pallas import tpu as pltpu
from jax.sharding import PartitionSpec as P

HEAD_DIM = 64
ROT = 20
LAYERS = 2
CHUNKS = 4
LANES = 128
EPSILON = 1e-06
LOG2E = 1.4426950408889634
LN2 = 0.6931471805599453
SCALE = HEAD_DIM ** (-0.5)
RSQRT_2PI = 0.3989422804014327
F32, BF16 = jnp.float32, jnp.bfloat16
NN = (((1,), (0,)), ((), ()))
NT = (((1,), (1,)), ((), ()))
TN = (((0,), (0,)), ((), ()))
MESH = pl.DeviceIdType.MESH
ANY = pl.BlockSpec(memory_space=pl.ANY)
VMEM = pl.BlockSpec(memory_space=pltpu.VMEM)
VMEM_LIMIT = 59 * 2**20


def dot(left, right, dims):
    return lax.dot_general(left, right, dims, preferred_element_type=F32)


def tile(index, size):
    return pl.ds(pl.multiple_of(index * size, size), size)


class Place:
    def __init__(self):
        self.dh, self.b, self.th, self.tl = [lax.axis_index(a) for a in ("dh", "b", "th", "tl")]
        self.n = lax.axis_size("dh")
        self.me = (self.dh, self.b, self.th, self.tl)
        self.sib = (self.dh, 1 - self.b, self.th, self.tl)
        self.link = (self.dh, self.b, self.th, 1 - self.tl)
        self.other = (self.dh, self.th, self.b, self.tl)
        self.mine = 2 * self.b + self.tl
        self.links = 2 * self.b + 1 - self.tl
        self.sibs = 2 * (1 - self.b) + self.tl
        self.diags = 2 * (1 - self.b) + 1 - self.tl

    def peer(self, step):
        return (lax.rem(self.dh + step, self.n), self.b, self.th, self.tl)

    def barrier(self):
        sem = pltpu.get_barrier_semaphore()
        greeted = [
            self.sib,
            self.link,
            (self.dh, self.b, 1 - self.th, self.tl),
            (self.dh, 1 - self.b, 1 - self.th, self.tl),
        ] + [self.peer(step) for step in range(1, self.n)]
        for device in greeted:
            pl.semaphore_signal(sem, inc=1, device_id=device, device_id_type=MESH)
        pl.semaphore_wait(sem, len(greeted))


def remote(src, dst, send, recv, device):
    return pltpu.make_async_remote_copy(
        src_ref=src, dst_ref=dst, send_sem=send, recv_sem=recv, device_id=device, device_id_type=MESH
    )


class Swap:
    def __init__(self, at, src, dst, sems):
        self.same = at.b == at.th
        self.far = remote(src, dst, sems.at[0], sems.at[1], at.other)
        self.near = pltpu.make_async_copy(src, dst, sems.at[2])

    def start(self):
        pl.when(self.same)(self.near.start)
        pl.when(jnp.logical_not(self.same))(self.far.start)

    def wait(self):
        pl.when(self.same)(self.near.wait)
        pl.when(jnp.logical_not(self.same))(self.far.wait)


class Gather:
    def __init__(self, at, src, full, zsems, psems):
        self.at, self.src, self.full = at, src, full
        self.zsems, self.psems = zsems, psems
        self.size = src.shape[0]
        self.same = at.b == at.th

    def slot(self, b):
        return self.full.at[tile(self.at.dh * 2 + b, self.size)]

    def block(self, dh):
        return self.full.at[tile(dh, 2 * self.size)]

    def zcopies(self):
        at = self.at
        dst = self.slot(at.b)
        far = remote(
            self.src,
            dst,
            self.zsems.at[0],
            self.zsems.at[4 + at.b],
            (at.dh, at.th, 1 - at.th, at.tl),
        )
        near = remote(self.src, dst, self.zsems.at[1], self.zsems.at[3], at.sib)
        own = pltpu.make_async_copy(self.src, dst, self.zsems.at[2])
        return far, near, own

    def zstart(self):
        far, near, own = self.zcopies()
        far.start()
        pl.when(self.same)(own.start)
        pl.when(jnp.logical_not(self.same))(near.start)

    def arrival(self, b, sem):
        return remote(self.src, self.slot(b), self.zsems.at[0], self.zsems.at[sem], self.at.sib)

    def zwait(self):
        at = self.at
        far, near, own = self.zcopies()
        far.wait_send()

        @pl.when(self.same)
        def _():
            own.wait()
            self.arrival(1 - at.b, 3).wait_recv()

        @pl.when(jnp.logical_not(self.same))
        def _():
            near.wait_send()
            self.arrival(at.b, 4 + at.b).wait_recv()
            self.arrival(1 - at.b, 5 - at.b).wait_recv()

    def pcopy(self, step, dh):
        block = self.block(dh)
        return remote(
            block, block, self.psems.at[0, step], self.psems.at[1, step], self.at.peer(step)
        )

    def pstart(self):
        for step in range(1, self.at.n):
            self.pcopy(step, self.at.dh).start()

    def pwait(self):
        for step in range(1, self.at.n):
            self.pcopy(step, self.at.dh).wait_send()
            self.pcopy(step, lax.rem(self.at.dh + self.at.n - step, self.at.n)).wait_recv()

    @staticmethod
    def scratch(n):
        return [pltpu.SemaphoreType.DMA((6,)), pltpu.SemaphoreType.DMA((2, n))]


class Scatter:
    def __init__(self, at, grad, out, got, mid, zgot, psems, zsems):
        self.at, self.grad, self.out = at, grad, out
        self.got, self.mid, self.zgot = got, mid, zgot
        self.psems, self.zsems = psems, zsems
        self.size = mid.shape[0] // 2
        self.same = at.b == at.th

    @staticmethod
    def scratch(n, rows, columns):
        size = rows // n
        return [
            pltpu.VMEM((n - 1, size, columns), BF16),
            pltpu.VMEM((size, columns), BF16),
            pltpu.VMEM((2, size // 2, columns), BF16),
            pltpu.SemaphoreType.DMA((2, n)),
            pltpu.SemaphoreType.DMA((6,)),
        ]

    def pcopy(self, step):
        block = self.grad.at[tile(lax.rem(self.at.dh + step, self.at.n), 2 * self.size)]
        return remote(
            block,
            self.got.at[step - 1],
            self.psems.at[0, step],
            self.psems.at[1, step],
            self.at.peer(step),
        )

    def pstart(self):
        for step in range(1, self.at.n):
            self.pcopy(step).start()

    def psum(self):
        total = self.grad[tile(self.at.dh, 2 * self.size), :].astype(F32)
        for step in range(1, self.at.n):
            self.pcopy(step).wait()
            total = total + self.got[step - 1].astype(F32)
        self.mid[...] = total.astype(BF16)

    def piece(self, b):
        return self.mid.at[tile(b, self.size)]

    def zcopies(self):
        at, sems = self.at, self.zsems
        dst = self.zgot.at[at.th]
        own = pltpu.make_async_copy(self.piece(at.b), dst, sems.at[0])
        near = remote(self.piece(1 - at.b), dst, sems.at[1], sems.at[4], at.sib)
        first = remote(
            self.piece(at.b), dst, sems.at[2], sems.at[5], (at.dh, at.b, 1 - at.th, at.tl)
        )
        second = remote(
            self.piece(1 - at.b), dst, sems.at[3], sems.at[5], (at.dh, 1 - at.b, 1 - at.th, at.tl)
        )
        return own, near, first, second

    def zstart(self):
        own, near, first, second = self.zcopies()

        @pl.when(self.same)
        def _():
            near.start()
            own.start()

        @pl.when(jnp.logical_not(self.same))
        def _():
            first.start()
            second.start()

    def arrival(self, th, sem):
        return remote(
            self.piece(0), self.zgot.at[th], self.zsems.at[0], self.zsems.at[sem], self.at.sib
        )

    def zsum(self):
        at = self.at
        own, near, first, second = self.zcopies()

        @pl.when(self.same)
        def _():
            near.wait_send()
            own.wait()

        @pl.when(jnp.logical_not(self.same))
        def _():
            first.wait_send()
            second.wait_send()
            self.arrival(at.th, 4).wait_recv()

        self.arrival(1 - at.th, 5).wait_recv()
        self.out[...] = self.zgot[0].astype(F32) + self.zgot[1].astype(F32)


class Rows:
    def __init__(self, at, count):
        self.at, self.R = at, count // CHUNKS

    def at_(self, chunk, owner):
        return tile(chunk * 4 + owner, self.R)

    def whole(self, chunk):
        return pl.ds(chunk * 4 * self.R, 4 * self.R)

    def own(self, chunk):
        return pl.ds(chunk * self.R, self.R)


class Spread:
    def __init__(self, at, rows, buf, sems):
        self.at, self.rows, self.buf, self.sems = at, rows, buf, sems

    @staticmethod
    def scratch(width):
        return [pltpu.SemaphoreType.DMA((6, CHUNKS))]

    def copy(self, chunk, kind, owner):
        ref = self.buf.at[self.rows.at_(chunk, owner)]
        device = self.at.link if kind == 0 else self.at.sib
        return remote(ref, ref, self.sems.at[kind, chunk], self.sems.at[3 + kind, chunk], device)

    def start(self, chunk):
        self.copy(chunk, 0, self.at.mine).start()
        self.copy(chunk, 1, self.at.mine).start()

    def forward(self, chunk):
        self.copy(chunk, 0, self.at.links).wait_recv()
        self.copy(chunk, 2, self.at.links).start()

    def wait(self, chunk):
        self.copy(chunk, 1, self.at.sibs).wait_recv()
        self.copy(chunk, 2, self.at.diags).wait_recv()

    def finish(self):
        for chunk in range(CHUNKS):
            self.copy(chunk, 0, self.at.mine).wait_send()
            self.copy(chunk, 1, self.at.mine).wait_send()
            self.copy(chunk, 2, self.at.links).wait_send()


class Collect:
    def __init__(self, at, rows, part, sent, got, sent_far, got_far, sems):
        self.at, self.R, self.part = at, rows.R, part
        self.sent, self.got, self.sent_far, self.got_far, self.sems = sent, got, sent_far, got_far, sems

    @staticmethod
    def scratch(count, width):
        R = count // CHUNKS
        return [
            pltpu.VMEM((CHUNKS, 2 * R, width), BF16),
            pltpu.VMEM((CHUNKS, 2 * R, width), BF16),
            pltpu.VMEM((CHUNKS, R, width), BF16),
            pltpu.VMEM((CHUNKS, R, width), BF16),
            pltpu.SemaphoreType.DMA((4, CHUNKS)),
        ]

    def near(self, chunk):
        return remote(
            self.sent.at[chunk],
            self.got.at[chunk],
            self.sems.at[0, chunk],
            self.sems.at[1, chunk],
            self.at.sib,
        )

    def far(self, chunk):
        return remote(
            self.sent_far.at[chunk],
            self.got_far.at[chunk],
            self.sems.at[2, chunk],
            self.sems.at[3, chunk],
            self.at.link,
        )

    def start(self, chunk):
        self.sent[chunk] = self.part[chunk, tile(1 - self.at.b, 2 * self.R), :].astype(BF16)
        self.near(chunk).start()

    def half(self, chunk, tl):
        mine = self.part[chunk, tile(2 * self.at.b + tl, self.R), :]
        return mine + self.got[chunk, tile(tl, self.R), :].astype(F32)

    def forward(self, chunk):
        self.near(chunk).wait_recv()
        self.sent_far[chunk] = self.half(chunk, 1 - self.at.tl).astype(BF16)
        self.far(chunk).start()

    def take(self, chunk):
        self.far(chunk).wait_recv()
        return self.half(chunk, self.at.tl) + self.got_far[chunk].astype(F32)

    def finish(self):
        for chunk in range(CHUNKS):
            self.near(chunk).wait_send()
            self.far(chunk).wait_send()


class Take:
    def __init__(self, refs):
        self.refs = list(refs)

    def __call__(self, count=None):
        if count is None:
            return self.refs.pop(0)
        return [self.refs.pop(0) for _ in range(count)]


class Local:
    def __init__(self, sems):
        self.sems, self.used = sems, 0

    def start(self, src, dst):
        copy = pltpu.make_async_copy(src, dst, self.sems.at[self.used])
        self.used += 1
        copy.start()
        return copy


def stats(values):
    center = values - jnp.mean(values, axis=-1, keepdims=True)
    inverse = lax.rsqrt(jnp.mean(center * center, axis=-1, keepdims=True) + EPSILON)
    return center * inverse, inverse


def norm(values, gain, shift):
    return stats(values)[0] * gain + shift


def norm_back(upstream, scaled, inverse, gain):
    weighted = upstream * gain
    first_mean = jnp.mean(weighted, axis=-1, keepdims=True)
    second_mean = jnp.mean(weighted * scaled, axis=-1, keepdims=True)
    return inverse * (weighted - first_mean - scaled * second_mean)


def lane():
    return lax.broadcasted_iota(jnp.int32, (1, LANES), 1)


def turned(values, cosines, sines):
    within = lax.rem(lane(), HEAD_DIM)
    former = lax.rem(within, ROT) < ROT // 2
    half = ROT // 2
    moved = jnp.where(former, pltpu.roll(values, LANES - half, 1), pltpu.roll(values, half, 1))
    return values * cosines + moved * sines


def of_head(values, head):
    keep = (lane() // HEAD_DIM) == head % 2
    return jnp.where(keep, values, jnp.zeros_like(values))


def gelu_and_slope(u):
    size = jnp.abs(u) * 0.7071067811865476
    t = 1.0 / (1.0 + 0.3275911 * size)
    bell = jnp.exp(-0.5 * u * u)
    poly = t * (
        0.127414796
        + t * (-0.142248368 + t * (0.7107068705 + t * (-0.7265760135 + t * 0.5307027145)))
    )
    tail = poly * bell
    phi = jnp.where(u < 0, tail, 1.0 - tail)
    return u * phi, phi + u * bell * RSQRT_2PI


def start_kernel(n, refs):
    take = Take(refs)
    tokens, small, slice_a = take(3)
    tokens_out, small_out, full_a = take(3)
    sems1, sems2, zsems, psems = take(4)
    at = Place()
    at.barrier()
    gather = Gather(at, slice_a, full_a, zsems, psems)
    swaps = [Swap(at, small, small_out, sems1), Swap(at, tokens, tokens_out, sems2)]
    gather.zstart()
    for swap in swaps:
        swap.start()
    gather.zwait()
    gather.pstart()
    gather.pwait()
    for swap in swaps:
        swap.wait()


def forward_kernel(n, following, swapping, refs):
    take = Take(refs)
    hidden, full_a, slice_b, slice_c, slice_d, small, cosines, sines = take(8)
    next_slice = take() if following else None
    swap_in = take() if swapping else None
    hidden_out, middle_out, full_b_out, full_c_out, full_d_out = take(5)
    n1_out, n2_out, qp_out, kp_out, vp_out, o_out, g_out, slope_out, lse_out = take(9)
    next_out = take() if following else None
    swap_out = take() if swapping else None
    x, wa, wb, wc, wd = take(5)
    n1, n2, qp, kp, vp, vt, o, g, slope, lse, ot = take(11)
    part = take()
    spread_one_sems, spread_two_sems = take(2)
    collect_one_scratch, collect_two_scratch = take(5), take(5)
    gather_sems = [take(2) for _ in range(4 if following else 3)]
    swap_sems = take() if swapping else None
    local_sems = take()

    at = Place()
    local = Local(local_sems)
    load_x = local.start(hidden, x)
    load_a = local.start(full_a, wa)
    at.barrier()
    rows = Rows(at, x.shape[0])
    R = rows.R
    spread_one = Spread(at, rows, n1, spread_one_sems)
    spread_two = Spread(at, rows, n2, spread_two_sems)
    collect_one = Collect(at, rows, part, *collect_one_scratch)
    collect_two = Collect(at, rows, part, *collect_two_scratch)
    gathers = [
        Gather(at, slice_b, wb, *gather_sems[0]),
        Gather(at, slice_c, wc, *gather_sems[1]),
        Gather(at, slice_d, wd, *gather_sems[2]),
    ]
    if following:
        gathers.append(Gather(at, next_slice, next_out, *gather_sems[3]))
    swap = Swap(at, swap_in, swap_out, swap_sems) if swapping else None

    load_x.wait()
    for k in range(CHUNKS):
        n1[rows.at_(k, at.mine), :] = norm(
            x[rows.own(k), :], small[0:1, :], small[2:3, :]
        ).astype(BF16)
        spread_one.start(k)
    for gather in gathers:
        gather.zstart()
    if swapping:
        swap.start()
    for k in range(CHUNKS):
        spread_one.forward(k)
    load_a.wait()

    def project(k):
        spread_one.wait(k)
        whole = rows.whole(k)
        for column in range(6):
            columns = pl.ds(column * LANES, LANES)
            t = dot(n1[whole, :], wa[:, columns], NN) + small[7:8, columns]
            pair = column % 2
            if column < 4:
                t = turned(t, cosines[whole, :], sines[whole, :])
            if column < 2:
                qp[pair, whole, :] = (t * (SCALE * LOG2E)).astype(BF16)
            elif column < 4:
                kp[pair, whole, :] = t.astype(BF16)
            else:
                vp[pair, whole, :] = t.astype(BF16)
                vt[pl.ds(pair * LANES, LANES), whole] = t.T.astype(BF16)

    for k in range(CHUNKS):
        project(k)
    saves = [local.start(*pair) for pair in ((n1, n1_out), (qp, qp_out), (kp, kp_out), (vp, vp_out))]
    for gather in gathers[:2]:
        gather.zwait()
        gather.pstart()

    def attention(k):
        whole = rows.whole(k)

        def head(h, carry):
            scores = dot(kp[h // 2], of_head(qp[h // 2, whole, :], h), NT)
            highest = jnp.max(scores, axis=0, keepdims=True)
            weights = jnp.exp2(scores - highest)
            total = jnp.sum(weights, axis=0, keepdims=True)
            spans = tile(h, HEAD_DIM)
            out = dot(vt[spans, :], weights.astype(BF16), NN) / total
            ot[spans, :] = out
            lse[pl.ds(h, 1), whole] = highest + jnp.log2(total)
            return carry

        lax.fori_loop(0, 4, head, 0)
        o[whole, :] = ot[...].T.astype(BF16)

    def leave(k):
        if k == 0:
            gathers[0].pwait()

        def columns(j, carry):
            span = tile(j, 256)
            part[k, :, span] = dot(o[rows.whole(k), :], wb[span, :], NT)
            return carry

        lax.fori_loop(0, part.shape[2] // 256, columns, 0)
        collect_one.start(k)

    def second_norm(k):
        own = rows.own(k)
        x[own, :] = x[own, :] + (collect_one.take(k) + small[4:5, :])
        n2[rows.at_(k, at.mine), :] = norm(x[own, :], small[1:2, :], small[3:4, :]).astype(BF16)
        spread_two.start(k)

    def expand(k):
        if k == 0:
            gathers[1].pwait()
            gathers[2].pwait()
        spread_two.wait(k)
        whole = rows.whole(k)

        def columns(j, carry):
            span = tile(j, 256)
            u = dot(n2[whole, :], wc[:, span], NN) + small[6:7, span]
            active, grade = gelu_and_slope(u)
            g[whole, span] = active.astype(BF16)
            slope[whole, span] = grade.astype(BF16)
            return carry

        lax.fori_loop(0, wc.shape[1] // 256, columns, 0)

        def outputs(j, carry):
            span = tile(j, 256)
            part[k, :, span] = dot(g[whole, :], wd[span, :], NT)
            return carry

        lax.fori_loop(0, part.shape[2] // 256, outputs, 0)
        collect_two.start(k)

    def end(k):
        own = rows.own(k)
        x[own, :] = x[own, :] + (collect_two.take(k) + small[5:6, :])

    attention(0)
    leave(0)
    for gather in gathers[2:]:
        gather.zwait()
        gather.pstart()
    for k in range(1, CHUNKS):
        attention(k)
        collect_one.forward(k - 1)
        leave(k)
    collect_one.forward(CHUNKS - 1)
    for k in range(CHUNKS):
        second_norm(k)
    saves.append(local.start(x, middle_out))
    saves.append(local.start(o, o_out))
    saves.append(local.start(lse, lse_out))
    for k in range(CHUNKS):
        spread_two.forward(k)
        expand(k)
        if k:
            collect_two.forward(k - 1)
    collect_two.forward(CHUNKS - 1)
    saves.append(local.start(n2, n2_out))
    saves.append(local.start(g, g_out))
    saves.append(local.start(slope, slope_out))
    saves.append(local.start(wb, full_b_out))
    saves.append(local.start(wc, full_c_out))
    saves.append(local.start(wd, full_d_out))
    saves[4].wait()
    for k in range(CHUNKS):
        end(k)
    last = local.start(x, hidden_out)
    if following:
        gathers[3].pwait()
    if swapping:
        swap.wait()
    for index, save in enumerate(saves):
        if index != 4:
            save.wait()
    last.wait()
    spread_one.finish()
    spread_two.finish()
    collect_one.finish()
    collect_two.finish()


def backward_kernel(n, following, swapping, refs):
    take = Take(refs)
    grad_in, hidden, middle, full_a, full_b, full_c, full_d = take(7)
    n1_in, n2_in, qp_in, kp_in, vp_in, o_in, g_in, slope_in, lse_in = take(9)
    small, cosines, sines = take(3)
    next_exit, next_triple = take(2) if following else (None, None)
    swap_in = take() if swapping else None
    grad_out, vector, exit_out, triple_out, expand_total, shrink_total = take(6)
    next_exit_total, next_triple_total = take(2) if following else (None, None)
    swap_out = take() if swapping else None
    e, xs, wa, wb, wc, wd = take(6)
    em, ea, n2, qp, kp, vp, kt, o, g, du, lse = take(11)
    dk, dv, dqt, dt, part, gd = take(6)
    spread_one_sems, spread_two_sems = take(2)
    collect_one_scratch, collect_two_scratch = take(5), take(5)
    scatter_c_scratch, scatter_d_scratch = take(5), take(5)
    if following:
        ge_next, gt_next = take(2)
        scatter_e_scratch, scatter_t_scratch = take(5), take(5)
    swap_sems = take() if swapping else None
    local_sems = take()

    at = Place()
    local = Local(local_sems)
    load_e = local.start(grad_in, e)
    load_d = local.start(full_d, wd)
    load_slope = local.start(slope_in, du)
    load_c = local.start(full_c, wc)
    load_middle = local.start(middle, xs)
    load_g = local.start(g_in, g)
    load_n2 = local.start(n2_in, n2)
    load_b = local.start(full_b, wb)
    loads = [
        local.start(*pair)
        for pair in ((qp_in, qp), (kp_in, kp), (vp_in, vp), (o_in, o), (lse_in, lse))
    ]
    load_a = local.start(full_a, wa)
    if following:
        load_next = [local.start(next_exit, ge_next), local.start(next_triple, gt_next)]
    at.barrier()
    rows = Rows(at, e.shape[0])
    spread_one = Spread(at, rows, em, spread_one_sems)
    spread_two = Spread(at, rows, ea, spread_two_sems)
    collect_one = Collect(at, rows, part, *collect_one_scratch)
    collect_two = Collect(at, rows, part, *collect_two_scratch)
    scatter_c = Scatter(at, wd, expand_total, *scatter_c_scratch)
    scatter_d = Scatter(at, gd, shrink_total, *scatter_d_scratch)
    nexts = []
    if following:
        nexts = [
            Scatter(at, ge_next, next_exit_total, *scatter_e_scratch),
            Scatter(at, gt_next, next_triple_total, *scatter_t_scratch),
        ]
    swap = Swap(at, swap_in, swap_out, swap_sems) if swapping else None
    gains = (small[0:1, :], small[1:2, :])
    vector[...] = jnp.zeros_like(vector)

    def add(row, values):
        vector[row : row + 1, : values.shape[1]] += jnp.sum(
            values.astype(F32), axis=0, keepdims=True
        )

    def weight_grad(left, right, out, width):
        def block(j, carry):
            span = tile(j, 256)
            out[span, :width] = dot(left[:, span], right[...], TN).astype(BF16)
            return carry

        lax.fori_loop(0, left.shape[1] // 256, block, 0)

    load_e.wait()
    for k in range(CHUNKS):
        low = e[rows.own(k), :].astype(BF16)
        em[rows.at_(k, at.mine), :] = low
        spread_one.start(k)
        add(5, low)
    if following:
        for load in load_next:
            load.wait()
        for scatter in nexts:
            scatter.pstart()
    if swapping:
        swap.start()
    load_d.wait()
    load_slope.wait()
    load_c.wait()

    def shrink_back(k):
        spread_one.forward(k)
        spread_one.wait(k)
        whole = rows.whole(k)

        def columns(j, carry):
            span = tile(j, 256)
            active_grad = dot(em[whole, :], wd[:, span], NN)
            du[whole, span] = (active_grad * du[whole, span].astype(F32)).astype(BF16)
            return carry

        lax.fori_loop(0, wd.shape[1] // 256, columns, 0)
        add(6, du[whole, :])

        def outputs(j, carry):
            span = tile(j, 256)
            part[k, :, span] = dot(du[whole, :], wc[span, :], NT)
            return carry

        lax.fori_loop(0, part.shape[2] // 256, outputs, 0)
        collect_one.start(k)

    for k in range(CHUNKS):
        shrink_back(k)
        if k:
            collect_one.forward(k - 1)
    collect_one.forward(CHUNKS - 1)
    load_g.wait()
    weight_grad(em, g, gd, gd.shape[1])
    scatter_d.pstart()
    load_n1 = local.start(n1_in, g)
    load_middle.wait()

    def norm_step(k, which, collect):
        own = rows.own(k)
        scaled, inverse = stats(xs[own, :])
        upstream = collect.take(k)
        add(which, upstream * scaled)
        add(2 + which, upstream)
        e[own, :] = e[own, :] + norm_back(upstream, scaled, inverse, gains[which])

    for k in range(CHUNKS):
        norm_step(k, 1, collect_one)
        low = e[rows.own(k), :].astype(BF16)
        ea[rows.at_(k, at.mine), :] = low
        spread_two.start(k)
        add(4, low)
    load_hidden = local.start(hidden, xs)
    load_n2.wait()
    weight_grad(n2, du, wd, wd.shape[1])
    scatter_c.pstart()
    for scatter in nexts:
        scatter.psum()
        scatter.zstart()
    load_b.wait()
    for load in loads:
        load.wait()
    for pair in range(2):
        kt[pl.ds(pair * LANES, LANES), :] = kp[pair].astype(F32).T.astype(BF16)
    dk[...] = jnp.zeros_like(dk)
    dv[...] = jnp.zeros_like(dv)

    def attention_back(k):
        spread_two.forward(k)
        spread_two.wait(k)
        whole = rows.whole(k)
        out_grad = dot(ea[whole, :], wb[...], NN)
        low_grad = out_grad.astype(BF16)
        product = low_grad.astype(F32) * o[whole, :].astype(F32)
        high = product.astype(BF16)
        rest = (product - high.astype(F32)).astype(BF16)
        for pair in range(2):
            lanes = slice(pair * LANES, (pair + 1) * LANES)
            dop = low_grad[:, lanes]
            for half in range(2):
                h = 2 * pair + half
                pick = jnp.broadcast_to(
                    ((lane() // HEAD_DIM) == half).astype(BF16), (8, LANES)
                )
                center = dot(pick, high[:, lanes], NT) + dot(pick, rest[:, lanes], NT)
                qh = of_head(qp[pair, whole, :], half)
                doh = of_head(dop, half)
                scores = dot(kp[pair], qh, NT)
                chances = jnp.exp2(scores - lse[h : h + 1, whole])
                chance_grad = dot(vp[pair], doh, NT)
                score_grad = (chances * (chance_grad - center[0:1, :])).astype(BF16)
                dv[pair] += dot(chances.astype(BF16), doh, NN)
                dk[pair] += dot(score_grad, qh, NN)
                spans = slice(h * HEAD_DIM, (h + 1) * HEAD_DIM)
                dqt[spans, :] = dot(kt[spans, :], score_grad, NN)
        for pair in range(2):
            lanes = slice(pair * LANES, (pair + 1) * LANES)
            dq = dqt[lanes, :].T * SCALE
            dt[whole, lanes] = turned(dq, cosines[whole, :], -sines[whole, :]).astype(BF16)

    for k in range(CHUNKS):
        attention_back(k)
    width = 2 * LANES
    for pair in range(2):
        lanes = pl.ds(width + pair * LANES, LANES)
        dt[:, lanes] = turned(dk[pair] * LN2, cosines[...], -sines[...]).astype(BF16)
        dt[:, pl.ds(2 * width + pair * LANES, LANES)] = dv[pair].astype(BF16)
    load_a.wait()

    def projection_back(k):
        whole = rows.whole(k)

        def outputs(j, carry):
            span = tile(j, 256)
            part[k, :, span] = dot(dt[whole, :], wa[span, :], NT)
            return carry

        lax.fori_loop(0, part.shape[2] // 256, outputs, 0)
        collect_two.start(k)

    for k in range(CHUNKS):
        projection_back(k)
        if k:
            collect_two.forward(k - 1)
    collect_two.forward(CHUNKS - 1)
    spread_one.finish()
    load_n1.wait()
    weight_grad(g, dt, em, dt.shape[1])
    save_triple = local.start(em.at[:, pl.ds(0, dt.shape[1])], triple_out)
    weight_grad(ea, o, wb, wb.shape[1])
    save_exit = local.start(wb, exit_out)
    add(7, dt[...])
    load_hidden.wait()
    for scatter in nexts:
        scatter.zsum()
    scatter_d.psum()
    scatter_d.zstart()
    scatter_c.psum()
    scatter_c.zstart()
    for k in range(CHUNKS):
        norm_step(k, 0, collect_two)
    save_grad = local.start(e, grad_out)
    scatter_d.zsum()
    scatter_c.zsum()
    if swapping:
        swap.wait()
    save_grad.wait()
    save_exit.wait()
    save_triple.wait()
    spread_two.finish()
    collect_one.finish()
    collect_two.finish()


def end_kernel(n, refs):
    take = Take(refs)
    exit_in, triple_in, grad_in, vectors = take(4)
    exit_total, triple_total, grad_out, sums, own_sums = take(5)
    ge, gt = take(2)
    scatter_e_scratch, scatter_t_scratch = take(5), take(5)
    swap_sems = take()
    plane, column, plane_sems, column_sems = take(4)
    local_sems = take()
    at = Place()
    local = Local(local_sems)
    loads = [local.start(exit_in, ge), local.start(triple_in, gt)]
    sem = pltpu.get_barrier_semaphore()
    cubes = [(db, dth, dtl) for db in range(2) for dth in range(2) for dtl in range(2)][1:]

    def flipped(at, flips):
        return [jnp.abs(coordinate - flip) for coordinate, flip in zip(at.me[1:], flips)]

    greeted = [(at.dh, *flipped(at, flips)) for flips in cubes]
    greeted += [at.peer(step) for step in range(1, n)]
    for device in greeted:
        pl.semaphore_signal(sem, inc=1, device_id=device, device_id_type=MESH)
    pl.semaphore_wait(sem, len(greeted))
    scatters = [
        Scatter(at, ge, exit_total, *scatter_e_scratch),
        Scatter(at, gt, triple_total, *scatter_t_scratch),
    ]
    swap = Swap(at, grad_in, grad_out, swap_sems)
    plane[at.dh] = vectors[...]

    def plane_copy(step, slot):
        ref = plane.at[slot]
        return remote(ref, ref, plane_sems.at[0, step], plane_sems.at[1, step], at.peer(step))

    for step in range(1, n):
        plane_copy(step, at.dh).start()
    for load, scatter in zip(loads, scatters):
        load.wait()
        scatter.pstart()
    swap.start()
    for step in range(1, n):
        plane_copy(step, at.dh).wait_send()
        plane_copy(step, lax.rem(at.dh + n - step, n)).wait_recv()
    total = plane[0]
    for index in range(1, n):
        total = total + plane[index]

    def slot(b, th, tl):
        return 4 * b + 2 * th + tl

    mine = slot(*at.me[1:])
    column[mine] = total

    def column_copy(index, flips, where):
        ref = column.at[where]
        device = (at.dh, *flipped(at, flips))
        return remote(ref, ref, column_sems.at[0, index], column_sems.at[1, index], device)

    for index, flips in enumerate(cubes):
        column_copy(index, flips, mine).start()
    for scatter in scatters:
        scatter.psum()
        scatter.zstart()
    for index, flips in enumerate(cubes):
        column_copy(index, flips, mine).wait_send()
        column_copy(index, flips, slot(*flipped(at, flips))).wait_recv()
    whole = column[0]
    for index in range(1, 8):
        whole = whole + column[index]
    sums[...] = whole
    own_sums[...] = column[slot(at.th, 0, at.tl)] + column[slot(at.th, 1, at.tl)]
    for scatter in scatters:
        scatter.zsum()
    swap.wait()


def call(body, args, vmem_in, outs, vmem_out, scratch, collective_id, name, flops=0):
    def kernel(*refs):
        body(refs)

    in_specs = [VMEM if index in vmem_in else ANY for index in range(len(args))]
    out_specs = [VMEM if index in vmem_out else ANY for index in range(len(outs))]
    return pl.pallas_call(
        kernel,
        out_shape=outs,
        in_specs=in_specs,
        out_specs=out_specs,
        scratch_shapes=scratch,
        compiler_params=pltpu.CompilerParams(
            collective_id=collective_id, has_side_effects=True, vmem_limit_bytes=VMEM_LIMIT
        ),
        name=name,
    )(*args)


def shards(
    n,
    tokens,
    cotangent,
    clip_mask,
    positions,
    triple_weight,
    triple_bias,
    exit_weight,
    expand_weight,
    expand_bias,
    shrink_weight,
    norm_gain,
    norm_shift,
    branch_bias,
):
    count, _, depth = tokens.shape
    seq = 4 * count
    size = triple_weight.shape[1]
    local = triple_weight.shape[3]
    inner = expand_weight.shape[2]
    wide = 3 * local
    pairs = local // LANES
    DMA = pltpu.SemaphoreType.DMA
    shape = jax.ShapeDtypeStruct
    tokens, cotangent = tokens[:, 0, :], cotangent[:, 0, :]
    slices = []
    for layer in range(LAYERS):
        slices.append(
            (
                triple_weight[layer].reshape(size, wide),
                exit_weight[layer].T,
                expand_weight[layer],
                shrink_weight[layer].T,
            )
        )

    def padded(rows):
        return jnp.pad(rows.astype(F32), ((0, 0), (0, depth - rows.shape[1])))

    smalls = jnp.concatenate(
        [
            padded(positions[:, 0, :]),
            jnp.broadcast_to(clip_mask.astype(F32)[:, None], (1, depth)),
            padded(triple_bias.reshape(LAYERS, wide)),
            padded(expand_bias),
            jnp.zeros((8 - 2 * LAYERS + 4, depth), F32),
        ]
    )[:16]
    tokens, smalls, full_a = call(
        functools.partial(start_kernel, n),
        (tokens, smalls, slices[0][0]),
        (),
        [shape(tokens.shape, BF16), shape(smalls.shape, F32), shape((depth, wide), BF16)],
        (),
        [DMA((3,)), DMA((3,))] + Gather.scratch(n),
        1,
        "start",
    )
    live = smalls[3, 0]
    halfway = ROT // 2
    frequency = 10000.0 ** (-jnp.arange(halfway, dtype=F32) / halfway)
    places = smalls[:3].reshape(3, 4, CHUNKS, count // CHUNKS).transpose(0, 2, 1, 3).reshape(3, seq)
    angles = jnp.repeat(places.T, ROT, axis=1) * jnp.tile(frequency, 6)[None, :]
    angles = jnp.pad(angles, ((0, 0), (0, HEAD_DIM - 3 * ROT)))
    sign = jnp.where(jnp.arange(HEAD_DIM) % ROT < halfway, -1.0, 1.0).astype(F32)
    cosines = jnp.tile(jnp.cos(angles), (1, 2))
    sines = jnp.tile(jnp.sin(angles) * sign, (1, 2))
    parameters = [
        jnp.concatenate(
            [
                norm_gain[layer].astype(F32),
                norm_shift[layer].astype(F32),
                branch_bias[layer].astype(F32),
                smalls[6 + layer][None],
                smalls[4 + layer][None],
            ]
        )
        for layer in range(LAYERS)
    ]
    hidden = tokens.astype(F32)
    saved = []
    R = count // CHUNKS
    upstream = None
    for layer in range(LAYERS):
        following = layer + 1 < LAYERS
        swapping = layer == 0
        args = [hidden, full_a, *slices[layer][1:], parameters[layer], cosines, sines]
        if following:
            args.append(slices[layer + 1][0])
        if swapping:
            args.append(cotangent)
        outs = [
            shape((count, depth), F32),
            shape((count, depth), F32),
            shape((depth, local), BF16),
            shape((depth, inner), BF16),
            shape((depth, inner), BF16),
            shape((seq, depth), BF16),
            shape((seq, depth), BF16),
            shape((pairs, seq, LANES), BF16),
            shape((pairs, seq, LANES), BF16),
            shape((pairs, seq, LANES), BF16),
            shape((seq, local), BF16),
            shape((seq, inner), BF16),
            shape((seq, inner), BF16),
            shape((8, seq), F32),
        ]
        if following:
            outs.append(shape((depth, wide), BF16))
        if swapping:
            outs.append(shape(cotangent.shape, BF16))
        V = pltpu.VMEM
        scratch = [
            V((count, depth), F32),
            V((depth, wide), BF16),
            V((depth, local), BF16),
            V((depth, inner), BF16),
            V((depth, inner), BF16),
            V((seq, depth), BF16),
            V((seq, depth), BF16),
            V((pairs, seq, LANES), BF16),
            V((pairs, seq, LANES), BF16),
            V((pairs, seq, LANES), BF16),
            V((local, seq), BF16),
            V((seq, local), BF16),
            V((seq, inner), BF16),
            V((seq, inner), BF16),
            V((8, seq), F32),
            V((local, 4 * R), F32),
            V((CHUNKS, 4 * R, depth), F32),
        ]
        scratch += Spread.scratch(depth) + Spread.scratch(depth)
        scratch += Collect.scratch(count, depth) + Collect.scratch(count, depth)
        for _ in range(4 if following else 3):
            scratch += Gather.scratch(n)
        if swapping:
            scratch.append(DMA((3,)))
        scratch.append(DMA((20,)))
        results = call(
            functools.partial(forward_kernel, n, following, swapping),
            args,
            (5, 6, 7),
            outs,
            (),
            scratch,
            2 + layer,
            "forward",
        )
        after, middle, full_b, full_c, full_d = results[:5]
        saved.append((hidden, middle, full_a, full_b, full_c, full_d) + tuple(results[5:14]))
        hidden = after
        rest = list(results[14:])
        if following:
            full_a = rest.pop(0)
        if swapping:
            upstream = rest.pop(0).astype(F32) * live
    mixed = hidden * live
    vectors = [None] * LAYERS
    totals = [[None] * 4 for _ in range(LAYERS)]
    pending = None
    for layer in reversed(range(LAYERS)):
        following = pending is not None
        swapping = not following
        args = [upstream, *saved[layer], parameters[layer], cosines, sines]
        if following:
            args += list(pending)
        if swapping:
            args.append(mixed)
        outs = [
            shape((count, depth), F32),
            shape((8, depth), F32),
            shape((depth, local), BF16),
            shape((depth, wide), BF16),
            shape((size, inner), F32),
            shape((size, inner), F32),
        ]
        if following:
            outs += [shape((size, local), F32), shape((size, wide), F32)]
        if swapping:
            outs.append(shape((count, depth), F32))
        vmem_out = (1, 4, 5) + ((6, 7) if following else ())
        V = pltpu.VMEM
        scratch = [
            V((count, depth), F32),
            V((count, depth), F32),
            V((depth, wide), BF16),
            V((depth, local), BF16),
            V((depth, inner), BF16),
            V((depth, inner), BF16),
            V((seq, depth), BF16),
            V((seq, depth), BF16),
            V((seq, depth), BF16),
            V((pairs, seq, LANES), BF16),
            V((pairs, seq, LANES), BF16),
            V((pairs, seq, LANES), BF16),
            V((local, seq), BF16),
            V((seq, local), BF16),
            V((seq, inner), BF16),
            V((seq, inner), BF16),
            V((8, seq), F32),
            V((pairs, seq, LANES), F32),
            V((pairs, seq, LANES), F32),
            V((local, 4 * R), F32),
            V((seq, wide), BF16),
            V((CHUNKS, 4 * R, depth), F32),
            V((depth, inner), BF16),
        ]
        scratch += Spread.scratch(depth) + Spread.scratch(depth)
        scratch += Collect.scratch(count, depth) + Collect.scratch(count, depth)
        scratch += Scatter.scratch(n, depth, inner) + Scatter.scratch(n, depth, inner)
        if following:
            scratch += [V((depth, local), BF16), V((depth, wide), BF16)]
            scratch += Scatter.scratch(n, depth, local) + Scatter.scratch(n, depth, wide)
        if swapping:
            scratch.append(DMA((3,)))
        scratch.append(DMA((24,)))
        results = call(
            functools.partial(backward_kernel, n, following, swapping),
            args,
            (16, 17, 18),
            outs,
            vmem_out,
            scratch,
            2 + LAYERS + layer,
            "backward",
        )
        upstream, vectors[layer] = results[:2]
        if following:
            totals[layer + 1][1], totals[layer + 1][0] = results[6:8]
        if swapping:
            mixed = results[-1]
        pending = results[2:4]
        totals[layer][2], totals[layer][3] = results[4:6]
    stacked = jnp.concatenate(vectors)
    V = pltpu.VMEM
    exit_total, triple_total, grad, sums, own_sums = call(
        functools.partial(end_kernel, n),
        [*pending, upstream.astype(BF16), stacked],
        (3,),
        [
            shape((size, local), F32),
            shape((size, wide), F32),
            shape((count, depth), BF16),
            shape(stacked.shape, F32),
            shape(stacked.shape, F32),
        ],
        (0, 1, 3, 4),
        [V((depth, local), BF16), V((depth, wide), BF16)]
        + Scatter.scratch(n, depth, local)
        + Scatter.scratch(n, depth, wide)
        + [
            DMA((3,)),
            V((n, 8 * LAYERS, depth), F32),
            V((8, 8 * LAYERS, depth), F32),
            DMA((2, n)),
            DMA((2, 7)),
            DMA((2,)),
        ],
        2 + 2 * LAYERS,
        "end",
    )
    totals[0][1], totals[0][0] = exit_total, triple_total
    sums = sums.reshape(LAYERS, 8, depth)
    own_sums = own_sums.reshape(LAYERS, 8, depth)
    return (
        mixed[:, None, :],
        grad.astype(F32)[:, None, :],
        jnp.stack([total[0].reshape(size, 3, local) for total in totals]),
        own_sums[:, 7, :wide].reshape(LAYERS, 3, local),
        jnp.stack([total[1].T for total in totals]),
        jnp.stack([total[2] for total in totals]),
        own_sums[:, 6, :inner],
        jnp.stack([total[3].T for total in totals]),
        sums[:, 0:2],
        sums[:, 2:4],
        sums[:, 4:6],
    )


def solution(mesh):
    n = mesh.shape["dp"] // 2
    fine = jax.sharding.Mesh(
        mesh.devices.reshape(n, 2, mesh.shape["tensor"] // 2, 2), ("dh", "b", "th", "tl")
    )
    dp, tensor = ("dh", "b"), ("th", "tl")
    return jax.shard_map(
        functools.partial(shards, n),
        mesh=fine,
        in_specs=(
            P(tensor, dp, None),
            P(tensor, dp, None),
            P(dp),
            P(None, dp, None),
            P(None, dp, None, tensor),
            P(None, None, tensor),
            P(None, tensor, dp),
            P(None, dp, tensor),
            P(None, tensor),
            P(None, tensor, dp),
            P(),
            P(),
            P(),
        ),
        out_specs=(
            P(tensor, dp, None),
            P(tensor, dp, None),
            P(None, dp, None, tensor),
            P(None, None, tensor),
            P(None, tensor, dp),
            P(None, dp, tensor),
            P(None, tensor),
            P(None, tensor, dp),
            P(),
            P(),
            P(),
        ),
        check_vma=False,
    )
```

```python
import functools

import jax
import jax.numpy as jnp
from jax import lax
from jax.experimental import pallas as pl
from jax.experimental.pallas import tpu as pltpu
from jax.sharding import PartitionSpec as P

HEAD_DIM = 64
ROT = 20
LAYERS = 2
CHUNKS = 4
LANES = 128
EPSILON = 1e-06
LOG2E = 1.4426950408889634
LN2 = 0.6931471805599453
SCALE = HEAD_DIM ** (-0.5)
RSQRT_2PI = 0.3989422804014327
F32, BF16 = jnp.float32, jnp.bfloat16
NN = (((1,), (0,)), ((), ()))
NT = (((1,), (1,)), ((), ()))
TN = (((0,), (0,)), ((), ()))
MESH = pl.DeviceIdType.MESH
ANY = pl.BlockSpec(memory_space=pl.ANY)
VMEM = pl.BlockSpec(memory_space=pltpu.VMEM)
VMEM_LIMIT = 59 * 2**20


def dot(left, right, dims):
    return lax.dot_general(left, right, dims, preferred_element_type=F32)


def tile(index, size):
    return pl.ds(pl.multiple_of(index * size, size), size)


class Place:
    def __init__(self):
        self.dh, self.b, self.th, self.tl = [lax.axis_index(a) for a in ("dh", "b", "th", "tl")]
        self.n = lax.axis_size("dh")
        self.me = (self.dh, self.b, self.th, self.tl)
        self.sib = (self.dh, 1 - self.b, self.th, self.tl)
        self.link = (self.dh, self.b, self.th, 1 - self.tl)
        self.other = (self.dh, self.th, self.b, self.tl)
        self.mine = 2 * self.b + self.tl
        self.links = 2 * self.b + 1 - self.tl
        self.sibs = 2 * (1 - self.b) + self.tl
        self.diags = 2 * (1 - self.b) + 1 - self.tl

    def turn(self, which):
        y, x = self.dh // 2, lax.rem(self.dh, 2)
        across, along = 2 * y + 1 - x, 2 * (1 - y) + x
        first = self.b if which else 1 - self.b
        return first * across + (1 - first) * along

    def opposite(self):
        y, x = self.dh // 2, lax.rem(self.dh, 2)
        return 2 * (1 - y) + 1 - x

    def near(self, dh):
        return (dh, self.b, self.th, self.tl)

    def peer(self, step):
        return (lax.rem(self.dh + step, self.n), self.b, self.th, self.tl)

    def barrier(self):
        sem = pltpu.get_barrier_semaphore()
        greeted = [
            self.sib,
            self.link,
            (self.dh, self.b, 1 - self.th, self.tl),
            (self.dh, 1 - self.b, 1 - self.th, self.tl),
        ] + [self.peer(step) for step in range(1, self.n)]
        for device in greeted:
            pl.semaphore_signal(sem, inc=1, device_id=device, device_id_type=MESH)
        pl.semaphore_wait(sem, len(greeted))


def remote(src, dst, send, recv, device):
    return pltpu.make_async_remote_copy(
        src_ref=src, dst_ref=dst, send_sem=send, recv_sem=recv, device_id=device, device_id_type=MESH
    )


class Swap:
    def __init__(self, at, src, dst, sems):
        self.same = at.b == at.th
        self.far = remote(src, dst, sems.at[0], sems.at[1], at.other)
        self.near = pltpu.make_async_copy(src, dst, sems.at[2])

    def start(self):
        pl.when(self.same)(self.near.start)
        pl.when(jnp.logical_not(self.same))(self.far.start)

    def wait(self):
        pl.when(self.same)(self.near.wait)
        pl.when(jnp.logical_not(self.same))(self.far.wait)


class Gather:
    def __init__(self, at, src, full, zsems, psems):
        self.at, self.src, self.full = at, src, full
        self.zsems, self.psems = zsems, psems
        self.size = src.shape[0]
        self.same = at.b == at.th

    def slot(self, b):
        return self.full.at[tile(self.at.dh * 2 + b, self.size)]

    def block(self, dh):
        return self.full.at[tile(dh, 2 * self.size)]

    def zcopies(self):
        at = self.at
        dst = self.slot(at.b)
        far = remote(
            self.src,
            dst,
            self.zsems.at[0],
            self.zsems.at[4 + at.b],
            (at.dh, at.th, 1 - at.th, at.tl),
        )
        near = remote(self.src, dst, self.zsems.at[1], self.zsems.at[3], at.sib)
        own = pltpu.make_async_copy(self.src, dst, self.zsems.at[2])
        return far, near, own

    def zstart(self):
        far, near, own = self.zcopies()
        far.start()
        pl.when(self.same)(own.start)
        pl.when(jnp.logical_not(self.same))(near.start)

    def arrival(self, b, sem):
        return remote(self.src, self.slot(b), self.zsems.at[0], self.zsems.at[sem], self.at.sib)

    def zwait(self):
        at = self.at
        far, near, own = self.zcopies()
        far.wait_send()

        @pl.when(self.same)
        def _():
            own.wait()
            self.arrival(1 - at.b, 3).wait_recv()

        @pl.when(jnp.logical_not(self.same))
        def _():
            near.wait_send()
            self.arrival(at.b, 4 + at.b).wait_recv()
            self.arrival(1 - at.b, 5 - at.b).wait_recv()

    def pcopy(self, step, dh, device):
        block = self.block(dh)
        return remote(
            block, block, self.psems.at[0, step], self.psems.at[1, step], self.at.near(device)
        )

    def hop(self, which, dh):
        return self.pcopy(which, dh, self.at.turn(which % 2))

    def pstart(self):
        at = self.at
        if at.n == 4:
            self.hop(0, at.dh).start()
            self.hop(1, at.dh).start()
        else:
            for step in range(1, at.n):
                self.pcopy(step, at.dh, lax.rem(at.dh + step, at.n)).start()

    def pforward(self):
        if self.at.n == 4:
            first = self.at.turn(0)
            self.hop(0, first).wait_recv()
            self.pcopy(2, first, self.at.turn(1)).start()

    def pwait(self):
        at = self.at
        if at.n == 4:
            self.hop(0, at.dh).wait_send()
            self.hop(1, at.dh).wait_send()
            self.pcopy(2, at.turn(0), at.turn(1)).wait_send()
            self.hop(1, at.turn(1)).wait_recv()
            self.pcopy(2, at.opposite(), at.turn(1)).wait_recv()
        else:
            for step in range(1, at.n):
                source = lax.rem(at.dh + at.n - step, at.n)
                self.pcopy(step, at.dh, source).wait_send()
                self.pcopy(step, source, source).wait_recv()

    @staticmethod
    def scratch(n):
        return [pltpu.SemaphoreType.DMA((6,)), pltpu.SemaphoreType.DMA((2, n))]


class Scatter:
    def __init__(self, at, grad, out, flip, got, mid, zgot, psems, zsems):
        self.at, self.grad, self.out, self.flip = at, grad, out, flip
        self.got, self.mid, self.zgot = got, mid, zgot
        self.psems, self.zsems = psems, zsems
        self.size = mid.shape[0] // 2
        self.same = at.b == at.th

    @staticmethod
    def scratch(n, rows, columns):
        size = rows // n
        return [
            pltpu.VMEM((n - 1, size, columns), BF16),
            pltpu.VMEM((size, columns), BF16),
        ]

    @staticmethod
    def layer_scratch(n, rows, columns):
        return [
            pltpu.VMEM((2, rows // n // 2, columns), BF16),
            pltpu.SemaphoreType.DMA((2, n)),
            pltpu.SemaphoreType.DMA((6,)),
        ]

    def part(self, dh):
        return self.grad.at[tile(dh, 2 * self.size)]

    def pcopy(self, step, src, device):
        return remote(
            src,
            self.got.at[step],
            self.psems.at[0, step],
            self.psems.at[1, step],
            self.at.near(device),
        )

    def hop(self, index):
        at = self.at
        if index == 2:
            return self.pcopy(2, self.mid, at.turn(1))
        return self.pcopy(index, self.part(at.opposite() if index else at.turn(0)), at.turn(0))

    def pstart(self):
        at = self.at
        if at.n == 4:
            self.hop(1).start()
            self.hop(0).start()
        else:
            for step in range(1, at.n):
                target = lax.rem(at.dh + step, at.n)
                self.pcopy(step - 1, self.part(target), target).start()

    def pforward(self):
        at = self.at
        if at.n == 4:
            self.hop(1).wait()
            total = self.grad[tile(at.turn(1), 2 * self.size), :].astype(F32)
            self.mid[...] = (total + self.got[1].astype(F32)).astype(BF16)
            self.hop(2).start()

    def psum(self):
        at = self.at
        total = self.grad[tile(at.dh, 2 * self.size), :].astype(F32)
        if at.n == 4:
            self.hop(0).wait()
            self.hop(2).wait()
            total = total + self.got[0].astype(F32) + self.got[2].astype(F32)
        else:
            for step in range(1, at.n):
                target = lax.rem(at.dh + step, at.n)
                self.pcopy(step - 1, self.part(target), target).wait()
                total = total + self.got[step - 1].astype(F32)
        self.mid[...] = total.astype(BF16)

    def piece(self, b):
        return self.mid.at[tile(b, self.size)]

    def zcopies(self):
        at, sems = self.at, self.zsems
        dst = self.zgot.at[at.th]
        own = pltpu.make_async_copy(self.piece(at.b), dst, sems.at[0])
        near = remote(self.piece(1 - at.b), dst, sems.at[1], sems.at[4], at.sib)
        first = remote(
            self.piece(at.b), dst, sems.at[2], sems.at[5], (at.dh, at.b, 1 - at.th, at.tl)
        )
        second = remote(
            self.piece(1 - at.b), dst, sems.at[3], sems.at[5], (at.dh, 1 - at.b, 1 - at.th, at.tl)
        )
        return own, near, first, second

    def zstart(self):
        own, near, first, second = self.zcopies()

        @pl.when(self.same)
        def _():
            near.start()
            own.start()

        @pl.when(jnp.logical_not(self.same))
        def _():
            first.start()
            second.start()

    def arrival(self, th, sem):
        return remote(
            self.piece(0), self.zgot.at[th], self.zsems.at[0], self.zsems.at[sem], self.at.sib
        )

    def zsum(self):
        at = self.at
        own, near, first, second = self.zcopies()

        @pl.when(self.same)
        def _():
            near.wait_send()
            own.wait()

        @pl.when(jnp.logical_not(self.same))
        def _():
            first.wait_send()
            second.wait_send()
            self.arrival(at.th, 4).wait_recv()

        self.arrival(1 - at.th, 5).wait_recv()
        total = self.zgot[0].astype(F32) + self.zgot[1].astype(F32)
        self.out[...] = total.T if self.flip else total


class Rows:
    def __init__(self, at, count):
        self.at, self.R = at, count // CHUNKS

    def at_(self, chunk, owner):
        return tile(chunk * 4 + owner, self.R)

    def whole(self, chunk):
        return pl.ds(chunk * 4 * self.R, 4 * self.R)

    def own(self, chunk):
        return pl.ds(chunk * self.R, self.R)


class Spread:
    def __init__(self, at, rows, buf, sems):
        self.at, self.rows, self.buf, self.sems = at, rows, buf, sems

    @staticmethod
    def scratch(width):
        return [pltpu.SemaphoreType.DMA((6, CHUNKS))]

    def copy(self, chunk, kind, owner):
        ref = self.buf.at[self.rows.at_(chunk, owner)]
        device = self.at.link if kind == 0 else self.at.sib
        return remote(ref, ref, self.sems.at[kind, chunk], self.sems.at[3 + kind, chunk], device)

    def start(self, chunk):
        self.copy(chunk, 0, self.at.mine).start()
        self.copy(chunk, 1, self.at.mine).start()

    def forward(self, chunk):
        self.copy(chunk, 0, self.at.links).wait_recv()
        self.copy(chunk, 2, self.at.links).start()

    def wait(self, chunk):
        self.copy(chunk, 1, self.at.sibs).wait_recv()
        self.copy(chunk, 2, self.at.diags).wait_recv()

    def finish(self):
        for chunk in range(CHUNKS):
            self.copy(chunk, 0, self.at.mine).wait_send()
            self.copy(chunk, 1, self.at.mine).wait_send()
            self.copy(chunk, 2, self.at.links).wait_send()


class Collect:
    def __init__(self, at, rows, part, sent, got, sent_far, got_far, sems):
        self.at, self.R, self.part = at, rows.R, part
        self.sent, self.got, self.sent_far, self.got_far, self.sems = sent, got, sent_far, got_far, sems

    @staticmethod
    def scratch(count, width):
        R = count // CHUNKS
        return [
            pltpu.VMEM((CHUNKS, 2 * R, width), BF16),
            pltpu.VMEM((CHUNKS, 2 * R, width), BF16),
            pltpu.VMEM((CHUNKS, R, width), BF16),
            pltpu.VMEM((CHUNKS, R, width), BF16),
        ]

    SEMS = pltpu.SemaphoreType.DMA((4, CHUNKS))

    def near(self, chunk):
        return remote(
            self.sent.at[chunk],
            self.got.at[chunk],
            self.sems.at[0, chunk],
            self.sems.at[1, chunk],
            self.at.sib,
        )

    def far(self, chunk):
        return remote(
            self.sent_far.at[chunk],
            self.got_far.at[chunk],
            self.sems.at[2, chunk],
            self.sems.at[3, chunk],
            self.at.link,
        )

    def left(self, ref, chunk):
        halves = [ref[tile(2 * chunk + b, 2 * self.R), :] for b in (self.at.b, 1 - self.at.b)]
        return jnp.concatenate(halves, axis=0)

    def put(self, chunk, span, values):
        self.part[chunk, :, span] = values[: 2 * self.R]
        self.sent[chunk, :, span] = values[2 * self.R :].astype(BF16)

    def start(self, chunk):
        self.near(chunk).start()

    def half(self, chunk, tl):
        mine = self.part[chunk, tile(tl, self.R), :]
        return mine + self.got[chunk, tile(tl, self.R), :].astype(F32)

    def forward(self, chunk):
        self.near(chunk).wait_recv()
        self.sent_far[chunk] = self.half(chunk, 1 - self.at.tl).astype(BF16)
        self.far(chunk).start()

    def take(self, chunk):
        self.far(chunk).wait_recv()
        return self.half(chunk, self.at.tl) + self.got_far[chunk].astype(F32)

    def finish(self):
        for chunk in range(CHUNKS):
            self.near(chunk).wait_send()
            self.far(chunk).wait_send()


class Take:
    def __init__(self, refs):
        self.refs = list(refs)

    def __call__(self, count=None):
        if count is None:
            return self.refs.pop(0)
        return [self.refs.pop(0) for _ in range(count)]


class Local:
    def __init__(self, sems):
        self.sems, self.used = sems, 0

    def start(self, src, dst):
        copy = pltpu.make_async_copy(src, dst, self.sems.at[self.used])
        self.used += 1
        copy.start()
        return copy


def stats(values):
    center = values - jnp.mean(values, axis=-1, keepdims=True)
    inverse = lax.rsqrt(jnp.mean(center * center, axis=-1, keepdims=True) + EPSILON)
    return center * inverse, inverse


def norm(values, gain, shift):
    return stats(values)[0] * gain + shift


def norm_back(upstream, scaled, inverse, gain):
    weighted = upstream * gain
    first_mean = jnp.mean(weighted, axis=-1, keepdims=True)
    second_mean = jnp.mean(weighted * scaled, axis=-1, keepdims=True)
    return inverse * (weighted - first_mean - scaled * second_mean)


def lane():
    return lax.broadcasted_iota(jnp.int32, (1, LANES), 1)


def turned(values, cosines, sines):
    within = lax.rem(lane(), HEAD_DIM)
    former = lax.rem(within, ROT) < ROT // 2
    half = ROT // 2
    moved = jnp.where(former, pltpu.roll(values, LANES - half, 1), pltpu.roll(values, half, 1))
    return values * cosines + moved * sines


def of_head(values, head):
    keep = (lane() // HEAD_DIM) == head % 2
    return jnp.where(keep, values, jnp.zeros_like(values))


def gelu_and_slope(u):
    size = jnp.abs(u) * 0.7071067811865476
    t = 1.0 / (1.0 + 0.3275911 * size)
    bell = jnp.exp(-0.5 * u * u)
    poly = t * (
        0.127414796
        + t * (-0.142248368 + t * (0.7107068705 + t * (-0.7265760135 + t * 0.5307027145)))
    )
    tail = poly * bell
    phi = jnp.where(u < 0, tail, 1.0 - tail)
    return u * phi, phi + u * bell * RSQRT_2PI


def tables(places, cosines, sines, rows):
    row = lax.broadcasted_iota(jnp.int32, (HEAD_DIM, places.shape[1]), 0)
    which = row // ROT
    place = jnp.where(
        which == 0, places[0:1, :], jnp.where(which == 1, places[1:2, :], places[2:3, :])
    )
    step = lax.rem(row, ROT // 2).astype(F32) / (ROT // 2)
    frequency = jnp.where(which < 3, jnp.exp(step * -9.210340371976184), 0.0)
    angle = place * frequency
    sign = jnp.where(lax.rem(row, ROT) < ROT // 2, -1.0, 1.0)
    for table, values in ((cosines, jnp.cos(angle)), (sines, jnp.sin(angle) * sign)):
        turned_values = jnp.concatenate([values, values], axis=0).T
        for k in range(CHUNKS):
            for owner in range(4):
                start = (owner * CHUNKS + k) * rows.R
                table[pl.ds((k * 4 + owner) * rows.R, rows.R), :] = turned_values[
                    start : start + rows.R, :
                ]


def forward_kernel(n, refs):
    take = Take(refs)
    tokens, cotangent, clip_mask, positions = take(4)
    triple_in, triple_bias, exit_in, expand_in, expand_bias, shrink_in = take(6)
    norm_gain, norm_shift, branch_bias = take(3)
    mixed, upstream, cosines_out, sines_out = take(4)
    outs = [take(15) for _ in range(LAYERS)]
    x, smalls, small, parameters, turned_tokens, turned_cotangent, cosines, sines = take(8)
    exit_turned, shrink_turned = take(2)
    weights = [take(4) for _ in range(LAYERS)]
    n1, n2, qp, kp, vp, vt, o, g, slope, lse, ot, part = take(12)
    spread_sems = take(2 * LAYERS)
    one_buffers, two_buffers = take(4), take(4)
    collect_sems = take(2 * LAYERS)
    gather_sems = [[take(2) for _ in range(4)] for _ in range(LAYERS)]
    token_sems, small_sems, cotangent_sems, local_sems = take(4)

    at = Place()
    local = Local(local_sems)
    rows = Rows(at, x.shape[0])
    slices = [
        [source.at[l] for source in (triple_in, exit_turned, expand_in, shrink_turned)]
        for l in range(LAYERS)
    ]
    gathers = [
        [Gather(at, *triple) for triple in zip(slices[l], weights[l], *zip(*gather_sems[l]))]
        for l in range(LAYERS)
    ]
    smalls[...] = jnp.zeros_like(smalls)
    smalls[0:3, :] = positions[...].astype(F32)
    smalls[3:4, :] = jnp.broadcast_to(clip_mask[...].astype(F32), (1, smalls.shape[1]))
    for l in range(LAYERS):
        for kind in range(3):
            width = triple_bias.shape[2]
            smalls[4 + l : 5 + l, kind * width : (kind + 1) * width] = triple_bias[
                l, kind : kind + 1, :
            ].astype(F32)
        smalls[6 + l : 7 + l, :] = expand_bias[l : l + 1, :].astype(F32)
    swap_small = Swap(at, smalls, small, small_sems)
    swap_tokens = [
        Swap(
            at,
            tokens.at[rows.own(k)],
            turned_tokens.at[rows.own(k)],
            token_sems.at[k],
        )
        for k in range(CHUNKS)
    ]
    swap_cotangent = Swap(at, cotangent, turned_cotangent, cotangent_sems)

    at.barrier()
    gathers[0][0].zstart()
    swap_small.start()
    for swap in swap_tokens:
        swap.start()
    for l in range(LAYERS):
        exit_turned[l] = exit_in[l].T
        shrink_turned[l] = shrink_in[l].T
        for index, source in enumerate((norm_gain, norm_shift, branch_bias)):
            parameters[8 * l + 2 * index : 8 * l + 2 * index + 2, :] = source[l].astype(F32)
    swap_small.wait()
    tables(small, cosines, sines, rows)
    saves = [local.start(cosines, cosines_out), local.start(sines, sines_out)]

    def begin(l):
        spread = [Spread(at, rows, buf, spread_sems[2 * l + i]) for i, buf in enumerate((n1, n2))]
        collect = [
            Collect(at, rows, part, *buffers, collect_sems[2 * l + i])
            for i, buffers in enumerate((one_buffers, two_buffers))
        ]
        return spread + collect

    stages = [begin(l) for l in range(LAYERS)]

    def row(l, index):
        return parameters[8 * l + index : 8 * l + index + 1, :]

    def first_norm(l, k):
        n1[rows.at_(k, at.mine), :] = norm(x[rows.own(k), :], row(l, 0), row(l, 2)).astype(BF16)
        stages[l][0].start(k)

    def project(l, k):
        stages[l][0].wait(k)
        whole = rows.whole(k)
        wa = weights[l][0]
        for kind in range(3):
            columns = slice(2 * kind * LANES, 2 * (kind + 1) * LANES)
            bias = small[4 + l : 5 + l, columns]
            both = dot(n1[whole, :], wa[:, columns], NN) + bias
            for pair in range(2):
                t = both[:, pair * LANES : (pair + 1) * LANES]
                if kind < 2:
                    t = turned(t, cosines[whole, :], sines[whole, :])
                if kind == 0:
                    qp[pair, whole, :] = (t * (SCALE * LOG2E)).astype(BF16)
                elif kind == 1:
                    kp[pair, whole, :] = t.astype(BF16)
                else:
                    vp[pair, whole, :] = t.astype(BF16)
                    vt[pl.ds(pair * LANES, LANES), whole] = t.T.astype(BF16)

    def attention(k):
        whole = rows.whole(k)

        def head(h, carry):
            scores = dot(kp[h // 2], of_head(qp[h // 2, whole, :], h), NT)
            highest = jnp.max(scores, axis=0, keepdims=True)
            weights = jnp.exp2(scores - highest)
            total = jnp.sum(weights, axis=0, keepdims=True)
            spans = tile(h, HEAD_DIM)
            ot[spans, :] = dot(vt[spans, :], weights.astype(BF16), NN) / total
            lse[pl.ds(h, 1), whole] = highest + jnp.log2(total)
            return carry

        lax.fori_loop(0, 4, head, 0)
        o[whole, :] = ot[...].T.astype(BF16)

    def leave(l, k):
        wb, collect = weights[l][1], stages[l][2]
        left = collect.left(o, k)

        def columns(j, carry):
            span = tile(j, 256)
            collect.put(k, span, dot(left, wb[span, :], NT))
            return carry

        lax.fori_loop(0, part.shape[2] // 256, columns, 0)
        collect.start(k)

    def second_norm(l, k):
        own = rows.own(k)
        x[own, :] = x[own, :] + (stages[l][2].take(k) + row(l, 4))
        n2[rows.at_(k, at.mine), :] = norm(x[own, :], row(l, 1), row(l, 3)).astype(BF16)
        stages[l][1].start(k)

    def up(l, k):
        whole = rows.whole(k)
        wc = weights[l][2]
        stages[l][1].wait(k)

        def columns(j, carry):
            span = tile(j, 256)
            u = dot(n2[whole, :], wc[:, span], NN) + small[pl.ds(6 + l, 1), span]
            active, grade = gelu_and_slope(u)
            g[whole, span] = active.astype(BF16)
            slope[whole, span] = grade.astype(BF16)
            return carry

        lax.fori_loop(0, wc.shape[1] // 256, columns, 0)

    def down(l, k):
        wd, collect = weights[l][3], stages[l][3]
        left = collect.left(g, k)

        def outputs(j, carry):
            span = tile(j, 256)
            collect.put(k, span, dot(left, wd[span, :], NT))
            return carry

        lax.fori_loop(0, part.shape[2] // 256, outputs, 0)
        collect.start(k)

    def end(l, k):
        own = rows.own(k)
        x[own, :] = x[own, :] + (stages[l][3].take(k) + row(l, 5))
        if l + 1 < LAYERS:
            first_norm(l + 1, k)

    A, B, C, D = range(4)

    def begin_plane(gather):
        gather.zwait()
        gather.pstart()

    begin_plane(gathers[0][A])
    for k in range(CHUNKS):
        swap_tokens[k].wait()
        x[rows.own(k), :] = turned_tokens[rows.own(k), :].astype(F32)
        first_norm(0, k)
    for gather in gathers[0][B:]:
        gather.zstart()
    gathers[0][A].pforward()
    pending = []
    for l in range(LAYERS):
        hidden_out, middle_out, *full_outs = outs[l][:6]
        n1_out, n2_out, qp_out, kp_out, vp_out, o_out, g_out, slope_out, lse_out = outs[l][6:]
        spread_one, spread_two, collect_one, collect_two = stages[l]
        now = gathers[l]
        following = gathers[l + 1] if l + 1 < LAYERS else None
        save_x = local.start(x, hidden_out)
        for k in range(CHUNKS):
            spread_one.forward(k)
        now[A].pwait()
        if l == 0:
            begin_plane(now[B])
        else:
            now[B].pforward()
            begin_plane(now[C])
        for save in pending:
            save.wait()
        for k in range(CHUNKS):
            project(l, k)
        spread_one.finish()
        save_n1 = local.start(n1, n1_out)
        pending = [
            local.start(*pair) for pair in ((qp, qp_out), (kp, kp_out), (vp, vp_out))
        ]
        if l == 0:
            now[B].pforward()
        attention(0)
        now[B].pwait()
        leave(l, 0)
        if l == 0:
            begin_plane(now[C])
        attention(1)
        collect_one.forward(0)
        leave(l, 1)
        if l:
            begin_plane(now[D])
            now[C].pforward()
        save_x.wait()
        attention(2)
        collect_one.forward(1)
        leave(l, 2)
        second_norm(l, 0)
        attention(3)
        collect_one.forward(2)
        leave(l, 3)
        if l == 0:
            now[C].pforward()
            begin_plane(now[D])
        second_norm(l, 1)
        collect_one.forward(3)
        second_norm(l, 2)
        second_norm(l, 3)
        if following:
            following[A].zstart()
            following[B].zstart()
        save_x = local.start(x, middle_out)
        pending += [local.start(o, o_out), local.start(lse, lse_out)]
        save_n1.wait()
        spread_two.forward(0)
        now[C].pwait()
        for k in range(CHUNKS):
            up(l, k)
            if k == 1:
                now[D].pforward()
            if k + 1 < CHUNKS:
                spread_two.forward(k + 1)
        save_x.wait()
        spread_two.finish()
        now[D].pwait()
        for k in range(CHUNKS):
            down(l, k)
            if k:
                collect_two.forward(k - 1)
            if following:
                if k == 0:
                    begin_plane(following[A])
                    following[C].zstart()
                if k == 2:
                    begin_plane(following[B])
            if k > 1:
                end(l, k - 2)
        collect_two.forward(CHUNKS - 1)
        pending += [local.start(*pair) for pair in ((n2, n2_out), (g, g_out), (slope, slope_out))]
        pending += [local.start(*pair) for pair in zip(weights[l], full_outs)]
        end(l, CHUNKS - 2)
        if following:
            following[A].pforward()
        end(l, CHUNKS - 1)
        if following:
            following[D].zstart()
        else:
            swap_cotangent.start()
        collect_one.finish()
        collect_two.finish()
    live = small[3:4, :]
    mixed[...] = (x[...] * live).astype(BF16)
    swap_cotangent.wait()
    upstream[...] = turned_cotangent[...].astype(F32) * live
    for save in saves + pending:
        save.wait()


def backward_kernel(n, refs):
    take = Take(refs)
    upstream, mixed, gain_in = take(3)
    ins = [take(15) for _ in range(LAYERS)]
    cosines_in, sines_in = take(2)
    mixed_out, grad_out, triple_out, triple_bias_out, exit_out, expand_out = take(6)
    expand_bias_out, shrink_out, gain_out, shift_out, bias_out = take(5)
    e, xs, wa, wb, wc, wd = take(6)
    em, ea, n2, qp, kp, vp, kt, o, g, du, lse = take(11)
    dk, dv, dqt, dt, part, gd, ge, gt, vectors, cosines, sines = take(11)
    turned_mixed, low_grad_own, turned_grad = take(3)
    spread_sems = take(2 * LAYERS)
    one_buffers, two_buffers = take(4), take(4)
    collect_sems = take(2 * LAYERS)
    scatter_buffers = [take(2) for _ in range(4)]
    scatter_layers = [[take(3) for _ in range(4)] for _ in range(LAYERS)]
    mixed_sems, grad_sems = take(2)
    plane, column, plane_sems, column_sems = take(4)
    local_sems = take()

    at = Place()
    local = Local(local_sems)
    rows = Rows(at, e.shape[0])

    def load(l, name):
        where = {
            "hidden": (0, xs),
            "middle": (1, xs),
            "a": (2, wa),
            "b": (3, wb),
            "c": (4, wc),
            "d": (5, wd),
            "n1": (6, g),
            "n2": (7, n2),
            "q": (8, qp),
            "k": (9, kp),
            "v": (10, vp),
            "o": (11, o),
            "g": (12, g),
            "slope": (13, du),
            "lse": (14, lse),
        }
        index, target = where[name]
        loads[(l, name)] = local.start(ins[l][index], target)

    def ready(l, *names):
        for name in names:
            loads.pop((l, name)).wait()

    loads = {}
    top = LAYERS - 1
    load_e = local.start(upstream, e)
    for name in ("d", "slope", "c", "middle", "g", "n2", "b", "q", "k", "v", "o", "lse", "a"):
        load(top, name)
    load_tables = [local.start(cosines_in, cosines), local.start(sines_in, sines)]

    cubes = [(db, dth, dtl) for db in range(2) for dth in range(2) for dtl in range(2)][1:]

    def flipped(flips):
        return [jnp.abs(coordinate - flip) for coordinate, flip in zip(at.me[1:], flips)]

    barrier = pltpu.get_barrier_semaphore()
    greeted = [(at.dh, *flipped(flips)) for flips in cubes]
    greeted += [at.peer(step) for step in range(1, n)]
    for device in greeted:
        pl.semaphore_signal(barrier, inc=1, device_id=device, device_id_type=MESH)
    pl.semaphore_wait(barrier, len(greeted))

    spreads = [
        [Spread(at, rows, buf, spread_sems[2 * l + i]) for i, buf in enumerate((em, ea))]
        for l in range(LAYERS)
    ]
    collects = [
        [
            Collect(at, rows, part, *buffers, collect_sems[2 * l + i])
            for i, buffers in enumerate((one_buffers, two_buffers))
        ]
        for l in range(LAYERS)
    ]
    pieces = ((gt, triple_out, False), (ge, exit_out, True), (wd, expand_out, False), (gd, shrink_out, True))
    scatters = [
        [
            Scatter(at, grad, out.at[l], flip, *buffers, *own)
            for (grad, out, flip), buffers, own in zip(pieces, scatter_buffers, scatter_layers[l])
        ]
        for l in range(LAYERS)
    ]
    swap_mixed = Swap(at, mixed, turned_mixed, mixed_sems)
    swap_grads = [
        Swap(
            at, low_grad_own.at[rows.own(k)], turned_grad.at[rows.own(k)], grad_sems.at[k]
        )
        for k in range(CHUNKS)
    ]
    vectors[...] = jnp.zeros_like(vectors)

    def add(l, row, values):
        vectors[8 * l + row : 8 * l + row + 1, : values.shape[1]] += jnp.sum(
            values.astype(F32), axis=0, keepdims=True
        )

    def weight_grad(left, right, out):
        def block(j, carry):
            span = tile(j, 256)
            out[span, :] = dot(left[:, span], right[...], TN).astype(BF16)
            return carry

        lax.fori_loop(0, left.shape[1] // 256, block, 0)

    def send_branch(l, k):
        low = e[rows.own(k), :].astype(BF16)
        em[rows.at_(k, at.mine), :] = low
        spreads[l][0].start(k)
        add(l, 5, low)

    def shrink_back(l, k):
        spreads[l][0].wait(k)
        whole = rows.whole(k)
        collect = collects[l][0]

        def columns(j, carry):
            span = tile(j, 256)
            active_grad = dot(em[whole, :], wd[:, span], NN)
            du[whole, span] = (active_grad * du[whole, span].astype(F32)).astype(BF16)
            return carry

        lax.fori_loop(0, wd.shape[1] // 256, columns, 0)
        add(l, 6, du[whole, :])
        left = collect.left(du, k)

        def outputs(j, carry):
            span = tile(j, 256)
            collect.put(k, span, dot(left, wc[span, :], NT))
            return carry

        lax.fori_loop(0, part.shape[2] // 256, outputs, 0)
        collect.start(k)

    def norm_step(l, k, which):
        own = rows.own(k)
        scaled, inverse = stats(xs[own, :])
        grads = collects[l][1 - which].take(k)
        add(l, which, grads * scaled)
        add(l, 2 + which, grads)
        gain = gain_in[l, which : which + 1, :].astype(F32)
        e[own, :] = e[own, :] + norm_back(grads, scaled, inverse, gain)

    def middle_step(l, k):
        norm_step(l, k, 1)
        low = e[rows.own(k), :].astype(BF16)
        ea[rows.at_(k, at.mine), :] = low
        spreads[l][1].start(k)
        add(l, 4, low)

    def first_step(l, k):
        norm_step(l, k, 0)
        if l:
            send_branch(l - 1, k)
        else:
            low_grad_own[rows.own(k), :] = e[rows.own(k), :].astype(BF16)
            swap_grads[k].start()

    def attention_back(l, k):
        spreads[l][1].wait(k)
        whole = rows.whole(k)
        out_grad = dot(ea[whole, :], wb[...], NN)
        low_grad = out_grad.astype(BF16)
        product = low_grad.astype(F32) * o[whole, :].astype(F32)
        high = product.astype(BF16)
        rest = (product - high.astype(F32)).astype(BF16)
        for pair in range(2):
            lanes = slice(pair * LANES, (pair + 1) * LANES)
            dop = low_grad[:, lanes]
            for half in range(2):
                h = 2 * pair + half
                pick = jnp.broadcast_to(((lane() // HEAD_DIM) == half).astype(BF16), (8, LANES))
                center = dot(pick, high[:, lanes], NT) + dot(pick, rest[:, lanes], NT)
                qh = of_head(qp[pair, whole, :], half)
                doh = of_head(dop, half)
                scores = dot(kp[pair], qh, NT)
                chances = jnp.exp2(scores - lse[h : h + 1, whole])
                chance_grad = dot(vp[pair], doh, NT)
                score_grad = (chances * (chance_grad - center[0:1, :])).astype(BF16)
                dv[pair] += dot(chances.astype(BF16), doh, NN)
                dk[pair] += dot(score_grad, qh, NN)
                spans = slice(h * HEAD_DIM, (h + 1) * HEAD_DIM)
                dqt[spans, :] = dot(kt[spans, :], score_grad, NN)
        for pair in range(2):
            lanes = slice(pair * LANES, (pair + 1) * LANES)
            dq = dqt[lanes, :].T * SCALE
            dt[whole, lanes] = turned(dq, cosines[whole, :], -sines[whole, :]).astype(BF16)

    def projection_back(l, k):
        collect = collects[l][1]
        left = collect.left(dt, k)

        def outputs(j, carry):
            span = tile(j, 256)
            collect.put(k, span, dot(left, wa[span, :], NT))
            return carry

        lax.fori_loop(0, part.shape[2] // 256, outputs, 0)
        collect.start(k)

    load_e.wait()
    for k in range(CHUNKS):
        send_branch(top, k)
    swap_mixed.start()
    for l in reversed(range(LAYERS)):
        spread_one, spread_two = spreads[l]
        collect_one, collect_two = collects[l]
        st, se, sc, sd = scatters[l]
        previous = scatters[l + 1] if l < top else None
        ready(l, "d", "slope", "c", "middle")
        for k in range(CHUNKS):
            spread_one.forward(k)
            shrink_back(l, k)
            if k:
                collect_one.forward(k - 1)
            if k > 1:
                middle_step(l, k - 2)
        collect_one.forward(CHUNKS - 1)
        spread_one.finish()
        if previous:
            for scatter in previous[:2]:
                scatter.psum()
                scatter.zstart()
        ready(l, "g")
        weight_grad(em, g, gd)
        sd.pstart()
        load(l, "n1")
        middle_step(l, CHUNKS - 2)
        middle_step(l, CHUNKS - 1)
        load(l, "hidden")
        ready(l, "n2")
        weight_grad(n2, du, wd)
        sc.pstart()
        if l:
            load(l - 1, "slope")
            load(l - 1, "c")
            load(l - 1, "n2")
        ready(l, "b", "q", "k", "v", "o", "lse")
        for pair in range(2):
            kt[pl.ds(pair * LANES, LANES), :] = kp[pair].astype(F32).T.astype(BF16)
        dk[...] = jnp.zeros_like(dk)
        dv[...] = jnp.zeros_like(dv)
        if l == top:
            for copy in load_tables:
                copy.wait()
        spread_two.forward(0)
        spread_two.forward(1)
        attention_back(l, 0)
        spread_two.forward(2)
        spread_two.forward(3)
        sd.pforward()
        attention_back(l, 1)
        sc.pforward()
        attention_back(l, 2)
        if previous:
            for scatter in previous[:2]:
                scatter.zsum()
        sd.psum()
        sd.zstart()
        attention_back(l, 3)
        spread_two.finish()
        sc.psum()
        sc.zstart()
        width = 2 * LANES
        for pair in range(2):
            lanes = pl.ds(width + pair * LANES, LANES)
            dt[:, lanes] = turned(dk[pair] * LN2, cosines[...], -sines[...]).astype(BF16)
            dt[:, pl.ds(2 * width + pair * LANES, LANES)] = dv[pair].astype(BF16)
        ready(l, "a", "n1")
        weight_grad(g, dt, gt)
        st.pstart()
        for k in range(CHUNKS):
            projection_back(l, k)
            if k:
                collect_two.forward(k - 1)
        collect_two.forward(CHUNKS - 1)
        weight_grad(ea, o, ge)
        se.pstart()
        add(l, 7, dt[...])
        ready(l, "hidden")
        if l:
            for name in ("d", "g", "b", "q", "k", "v", "o", "lse", "a"):
                load(l - 1, name)
        sd.zsum()
        collect_one.finish()
        first_step(l, 0)
        first_step(l, 1)
        st.pforward()
        se.pforward()
        first_step(l, 2)
        first_step(l, 3)
        if l:
            load(l - 1, "middle")
        collect_two.finish()
        sc.zsum()

    st, se = scatters[0][:2]
    plane[at.dh] = vectors[...]

    def plane_copy(step, slot):
        ref = plane.at[slot]
        return remote(ref, ref, plane_sems.at[0, step], plane_sems.at[1, step], at.peer(step))

    for step in range(1, n):
        plane_copy(step, at.dh).start()
    for scatter in (st, se):
        scatter.psum()
        scatter.zstart()
    for step in range(1, n):
        plane_copy(step, at.dh).wait_send()
        plane_copy(step, lax.rem(at.dh + n - step, n)).wait_recv()
    total = plane[0]
    for index in range(1, n):
        total = total + plane[index]

    def slot(b, th, tl):
        return 4 * b + 2 * th + tl

    mine = slot(*at.me[1:])
    column[mine] = total

    def column_copy(index, flips, where):
        ref = column.at[where]
        device = (at.dh, *flipped(flips))
        return remote(ref, ref, column_sems.at[0, index], column_sems.at[1, index], device)

    for index, flips in enumerate(cubes):
        column_copy(index, flips, mine).start()
    swap_mixed.wait()
    mixed_out[...] = turned_mixed[...].astype(F32)
    for index, flips in enumerate(cubes):
        column_copy(index, flips, mine).wait_send()
        column_copy(index, flips, slot(*flipped(flips))).wait_recv()
    total = column[0]
    for index in range(1, 8):
        total = total + column[index]
    own = column[slot(at.th, 0, at.tl)] + column[slot(at.th, 1, at.tl)]
    width = triple_bias_out.shape[2]
    for l in range(LAYERS):
        gain_out[l] = total[8 * l : 8 * l + 2, :]
        shift_out[l] = total[8 * l + 2 : 8 * l + 4, :]
        bias_out[l] = total[8 * l + 4 : 8 * l + 6, :]
        expand_bias_out[l : l + 1, :] = own[8 * l + 6 : 8 * l + 7, :]
        for kind in range(3):
            triple_bias_out[l, kind : kind + 1, :] = own[
                8 * l + 7 : 8 * l + 8, kind * width : (kind + 1) * width
            ]
    for k in range(CHUNKS):
        swap_grads[k].wait()
    grad_out[...] = turned_grad[...].astype(F32)
    for scatter in (st, se):
        scatter.zsum()


def call(body, args, vmem_in, outs, vmem_out, scratch, collective_id, name, flops=0):
    def kernel(*refs):
        body(refs)

    in_specs = [VMEM if index in vmem_in else ANY for index in range(len(args))]
    out_specs = [VMEM if index in vmem_out else ANY for index in range(len(outs))]
    return pl.pallas_call(
        kernel,
        out_shape=outs,
        in_specs=in_specs,
        out_specs=out_specs,
        scratch_shapes=scratch,
        compiler_params=pltpu.CompilerParams(
            collective_id=collective_id, has_side_effects=True, vmem_limit_bytes=VMEM_LIMIT
        ),
        name=name,
    )(*args)


def shards(
    n,
    tokens,
    cotangent,
    clip_mask,
    positions,
    triple_weight,
    triple_bias,
    exit_weight,
    expand_weight,
    expand_bias,
    shrink_weight,
    norm_gain,
    norm_shift,
    branch_bias,
):
    count, _, depth = tokens.shape
    seq = 4 * count
    size = triple_weight.shape[1]
    local = triple_weight.shape[3]
    inner = expand_weight.shape[2]
    wide = 3 * local
    pairs = local // LANES
    R = count // CHUNKS
    V, DMA, shape = pltpu.VMEM, pltpu.SemaphoreType.DMA, jax.ShapeDtypeStruct
    wides = (wide, local, inner, inner)
    pair_shape = (pairs, seq, LANES)
    args = [
        tokens[:, 0, :],
        cotangent[:, 0, :],
        clip_mask[:, None],
        positions[:, 0, :],
        triple_weight.reshape(LAYERS, size, wide),
        triple_bias,
        exit_weight,
        expand_weight,
        expand_bias,
        shrink_weight,
        norm_gain,
        norm_shift,
        branch_bias,
    ]
    outs = [
        shape((count, depth), BF16),
        shape((count, depth), F32),
        shape((seq, LANES), F32),
        shape((seq, LANES), F32),
    ]
    for _ in range(LAYERS):
        outs += [shape((count, depth), F32)] * 2
        outs += [shape((depth, width), BF16) for width in wides]
        outs += [shape((seq, depth), BF16)] * 2
        outs += [shape(pair_shape, BF16)] * 3
        outs += [shape((seq, local), BF16)]
        outs += [shape((seq, inner), BF16)] * 2
        outs += [shape((8, seq), F32)]
    scratch = [
        V((count, depth), F32),
        V((8, depth), F32),
        V((8, depth), F32),
        V((8 * LAYERS, depth), F32),
        V((count, depth), BF16),
        V((count, depth), BF16),
        V((seq, LANES), F32),
        V((seq, LANES), F32),
        V((LAYERS, size, local), BF16),
        V((LAYERS, size, inner), BF16),
    ]
    for _ in range(LAYERS):
        scratch += [V((depth, width), BF16) for width in wides]
    scratch += [V((seq, depth), BF16)] * 2
    scratch += [V(pair_shape, BF16)] * 3
    scratch += [V((local, seq), BF16), V((seq, local), BF16)]
    scratch += [V((seq, inner), BF16)] * 2
    scratch += [V((8, seq), F32), V((local, 4 * R), F32), V((CHUNKS, 2 * R, depth), F32)]
    scratch += Spread.scratch(depth) * (2 * LAYERS)
    scratch += Collect.scratch(count, depth) * 2
    scratch += [Collect.SEMS] * (2 * LAYERS)
    scratch += Gather.scratch(n) * (4 * LAYERS)
    scratch += [DMA((CHUNKS, 3)), DMA((3,)), DMA((3,)), DMA((48,))]
    results = call(
        functools.partial(forward_kernel, n),
        args,
        tuple(range(len(args))),
        outs,
        (0, 1),
        scratch,
        1,
        "forward",
    )
    mixed, upstream, cosines, sines = results[:4]
    args = [upstream, mixed, norm_gain, *results[4:], cosines, sines]
    outs = [
        shape((count, depth), F32),
        shape((count, depth), F32),
        shape((LAYERS, size, wide), F32),
        shape(triple_bias.shape, F32),
        shape(exit_weight.shape, F32),
        shape(expand_weight.shape, F32),
        shape(expand_bias.shape, F32),
        shape(shrink_weight.shape, F32),
        shape(norm_gain.shape, F32),
        shape(norm_shift.shape, F32),
        shape(branch_bias.shape, F32),
    ]
    scratch = [V((count, depth), F32)] * 2
    scratch += [V((depth, width), BF16) for width in wides]
    scratch += [V((seq, depth), BF16)] * 3
    scratch += [V(pair_shape, BF16)] * 3
    scratch += [V((local, seq), BF16), V((seq, local), BF16)]
    scratch += [V((seq, inner), BF16)] * 2
    scratch += [V((8, seq), F32)]
    scratch += [V(pair_shape, F32)] * 2
    scratch += [V((local, 4 * R), F32), V((seq, wide), BF16), V((CHUNKS, 2 * R, depth), F32)]
    scratch += [V((depth, inner), BF16), V((depth, local), BF16), V((depth, wide), BF16)]
    scratch += [V((8 * LAYERS, depth), F32), V((seq, LANES), F32), V((seq, LANES), F32)]
    scratch += [V((count, depth), BF16)] * 3
    scratch += Spread.scratch(depth) * (2 * LAYERS)
    scratch += Collect.scratch(count, depth) * 2
    scratch += [Collect.SEMS] * (2 * LAYERS)
    for width in wides:
        scratch += Scatter.scratch(n, depth, width)
    for _ in range(LAYERS):
        for width in wides:
            scratch += Scatter.layer_scratch(n, depth, width)
    scratch += [DMA((3,)), DMA((CHUNKS, 3))]
    scratch += [V((n, 8 * LAYERS, depth), F32), V((8, 8 * LAYERS, depth), F32)]
    scratch += [DMA((2, n)), DMA((2, 7)), DMA((48,))]
    results = call(
        functools.partial(backward_kernel, n),
        args,
        (1, 2),
        outs,
        tuple(range(len(outs))),
        scratch,
        2,
        "backward",
    )
    mixed, grad, triple_total, *others = results
    return (
        mixed[:, None, :],
        grad[:, None, :],
        triple_total.reshape(triple_weight.shape),
        *others,
    )


def solution(mesh):
    n = mesh.shape["dp"] // 2
    fine = jax.sharding.Mesh(
        mesh.devices.reshape(n, 2, mesh.shape["tensor"] // 2, 2), ("dh", "b", "th", "tl")
    )
    dp, tensor = ("dh", "b"), ("th", "tl")
    return jax.shard_map(
        functools.partial(shards, n),
        mesh=fine,
        in_specs=(
            P(tensor, dp, None),
            P(tensor, dp, None),
            P(dp),
            P(None, dp, None),
            P(None, dp, None, tensor),
            P(None, None, tensor),
            P(None, tensor, dp),
            P(None, dp, tensor),
            P(None, tensor),
            P(None, tensor, dp),
            P(),
            P(),
            P(),
        ),
        out_specs=(
            P(tensor, dp, None),
            P(tensor, dp, None),
            P(None, dp, None, tensor),
            P(None, None, tensor),
            P(None, tensor, dp),
            P(None, dp, tensor),
            P(None, tensor),
            P(None, tensor, dp),
            P(),
            P(),
            P(),
        ),
        check_vma=False,
    )
```

```python
import functools

import jax
import jax.numpy as jnp
from jax import lax
from jax.experimental import pallas as pl
from jax.experimental.pallas import tpu as pltpu
from jax.sharding import PartitionSpec as P

HEAD_DIM = 64
ROT = 20
LAYERS = 2
CHUNKS = 4
LANES = 128
EPSILON = 1e-06
LOG2E = 1.4426950408889634
LN2 = 0.6931471805599453
SCALE = HEAD_DIM ** (-0.5)
RSQRT_2PI = 0.3989422804014327
F32, BF16 = jnp.float32, jnp.bfloat16
NN = (((1,), (0,)), ((), ()))
NT = (((1,), (1,)), ((), ()))
TN = (((0,), (0,)), ((), ()))
MESH = pl.DeviceIdType.MESH
ANY = pl.BlockSpec(memory_space=pl.ANY)
VMEM = pl.BlockSpec(memory_space=pltpu.VMEM)
VMEM_LIMIT = 59 * 2**20


def dot(left, right, dims):
    return lax.dot_general(left, right, dims, preferred_element_type=F32)


def tile(index, size):
    return pl.ds(pl.multiple_of(index * size, size), size)


class Place:
    def __init__(self):
        self.dh, self.b, self.th, self.tl = [lax.axis_index(a) for a in ("dh", "b", "th", "tl")]
        self.n = lax.axis_size("dh")
        self.me = (self.dh, self.b, self.th, self.tl)
        self.sib = (self.dh, 1 - self.b, self.th, self.tl)
        self.link = (self.dh, self.b, self.th, 1 - self.tl)
        self.other = (self.dh, self.th, self.b, self.tl)
        self.mine = 2 * self.b + self.tl
        self.links = 2 * self.b + 1 - self.tl
        self.sibs = 2 * (1 - self.b) + self.tl
        self.diags = 2 * (1 - self.b) + 1 - self.tl

    def turn(self, which):
        y, x = self.dh // 2, lax.rem(self.dh, 2)
        across, along = 2 * y + 1 - x, 2 * (1 - y) + x
        first = self.b if which else 1 - self.b
        return first * across + (1 - first) * along

    def opposite(self):
        y, x = self.dh // 2, lax.rem(self.dh, 2)
        return 2 * (1 - y) + 1 - x

    def near(self, dh):
        return (dh, self.b, self.th, self.tl)

    def peer(self, step):
        return (lax.rem(self.dh + step, self.n), self.b, self.th, self.tl)

    def barrier(self):
        sem = pltpu.get_barrier_semaphore()
        greeted = [
            self.sib,
            self.link,
            (self.dh, self.b, 1 - self.th, self.tl),
            (self.dh, 1 - self.b, 1 - self.th, self.tl),
        ] + [self.peer(step) for step in range(1, self.n)]
        for device in greeted:
            pl.semaphore_signal(sem, inc=1, device_id=device, device_id_type=MESH)
        pl.semaphore_wait(sem, len(greeted))


def remote(src, dst, send, recv, device):
    return pltpu.make_async_remote_copy(
        src_ref=src, dst_ref=dst, send_sem=send, recv_sem=recv, device_id=device, device_id_type=MESH
    )


class Swap:
    def __init__(self, at, src, dst, sems):
        self.same = at.b == at.th
        self.far = remote(src, dst, sems.at[0], sems.at[1], at.other)
        self.near = pltpu.make_async_copy(src, dst, sems.at[2])

    def start(self):
        pl.when(self.same)(self.near.start)
        pl.when(jnp.logical_not(self.same))(self.far.start)

    def wait(self):
        pl.when(self.same)(self.near.wait)
        pl.when(jnp.logical_not(self.same))(self.far.wait)


class Gather:
    def __init__(self, at, src, full, zsems, psems):
        self.at, self.src, self.full = at, src, full
        self.zsems, self.psems = zsems, psems
        self.size = src.shape[0]
        self.same = at.b == at.th

    def slot(self, b):
        return self.full.at[tile(self.at.dh * 2 + b, self.size)]

    def block(self, dh):
        return self.full.at[tile(dh, 2 * self.size)]

    def zcopies(self):
        at = self.at
        dst = self.slot(at.b)
        far = remote(
            self.src,
            dst,
            self.zsems.at[0],
            self.zsems.at[4 + at.b],
            (at.dh, at.th, 1 - at.th, at.tl),
        )
        near = remote(self.src, dst, self.zsems.at[1], self.zsems.at[3], at.sib)
        own = pltpu.make_async_copy(self.src, dst, self.zsems.at[2])
        return far, near, own

    def zstart(self):
        far, near, own = self.zcopies()
        far.start()
        pl.when(self.same)(own.start)
        pl.when(jnp.logical_not(self.same))(near.start)

    def arrival(self, b, sem):
        return remote(self.src, self.slot(b), self.zsems.at[0], self.zsems.at[sem], self.at.sib)

    def zwait(self):
        at = self.at
        far, near, own = self.zcopies()
        far.wait_send()

        @pl.when(self.same)
        def _():
            own.wait()
            self.arrival(1 - at.b, 3).wait_recv()

        @pl.when(jnp.logical_not(self.same))
        def _():
            near.wait_send()
            self.arrival(at.b, 4 + at.b).wait_recv()
            self.arrival(1 - at.b, 5 - at.b).wait_recv()

    def pcopy(self, step, dh, device):
        block = self.block(dh)
        return remote(
            block, block, self.psems.at[0, step], self.psems.at[1, step], self.at.near(device)
        )

    def hop(self, which, dh):
        return self.pcopy(which, dh, self.at.turn(which % 2))

    def pstart(self):
        at = self.at
        if at.n == 4:
            self.hop(0, at.dh).start()
            self.hop(1, at.dh).start()
        else:
            for step in range(1, at.n):
                self.pcopy(step, at.dh, lax.rem(at.dh + step, at.n)).start()

    def pforward(self):
        if self.at.n == 4:
            first = self.at.turn(0)
            self.hop(0, first).wait_recv()
            self.pcopy(2, first, self.at.turn(1)).start()

    def pwait(self):
        at = self.at
        if at.n == 4:
            self.hop(0, at.dh).wait_send()
            self.hop(1, at.dh).wait_send()
            self.pcopy(2, at.turn(0), at.turn(1)).wait_send()
            self.hop(1, at.turn(1)).wait_recv()
            self.pcopy(2, at.opposite(), at.turn(1)).wait_recv()
        else:
            for step in range(1, at.n):
                source = lax.rem(at.dh + at.n - step, at.n)
                self.pcopy(step, at.dh, source).wait_send()
                self.pcopy(step, source, source).wait_recv()

    @staticmethod
    def scratch(n):
        return [pltpu.SemaphoreType.DMA((6,)), pltpu.SemaphoreType.DMA((2, n))]


class Scatter:
    def __init__(self, at, grad, out, flip, got, mid, zgot, psems, zsems):
        self.at, self.grad, self.out, self.flip = at, grad, out, flip
        self.got, self.mid, self.zgot = got, mid, zgot
        self.psems, self.zsems = psems, zsems
        self.size = mid.shape[0] // 2
        self.same = at.b == at.th

    @staticmethod
    def scratch(n, rows, columns):
        size = rows // n
        return [
            pltpu.VMEM((n - 1, size, columns), BF16),
            pltpu.VMEM((size, columns), BF16),
        ]

    @staticmethod
    def layer_scratch(n, rows, columns):
        return [
            pltpu.VMEM((2, rows // n // 2, columns), BF16),
            pltpu.SemaphoreType.DMA((2, n)),
            pltpu.SemaphoreType.DMA((6,)),
        ]

    def part(self, dh):
        return self.grad.at[tile(dh, 2 * self.size)]

    def pcopy(self, step, src, device):
        return remote(
            src,
            self.got.at[step],
            self.psems.at[0, step],
            self.psems.at[1, step],
            self.at.near(device),
        )

    def hop(self, index):
        at = self.at
        if index == 2:
            return self.pcopy(2, self.mid, at.turn(1))
        return self.pcopy(index, self.part(at.opposite() if index else at.turn(0)), at.turn(0))

    def pstart(self):
        at = self.at
        if at.n == 4:
            self.hop(1).start()
            self.hop(0).start()
        else:
            for step in range(1, at.n):
                target = lax.rem(at.dh + step, at.n)
                self.pcopy(step - 1, self.part(target), target).start()

    def pforward(self):
        at = self.at
        if at.n == 4:
            self.hop(1).wait()
            total = self.grad[tile(at.turn(1), 2 * self.size), :].astype(F32)
            self.mid[...] = (total + self.got[1].astype(F32)).astype(BF16)
            self.hop(2).start()

    def psum(self):
        at = self.at
        total = self.grad[tile(at.dh, 2 * self.size), :].astype(F32)
        if at.n == 4:
            self.hop(0).wait()
            self.hop(2).wait()
            total = total + self.got[0].astype(F32) + self.got[2].astype(F32)
        else:
            for step in range(1, at.n):
                target = lax.rem(at.dh + step, at.n)
                self.pcopy(step - 1, self.part(target), target).wait()
                total = total + self.got[step - 1].astype(F32)
        self.mid[...] = total.astype(BF16)

    def piece(self, b):
        return self.mid.at[tile(b, self.size)]

    def zcopies(self):
        at, sems = self.at, self.zsems
        dst = self.zgot.at[at.th]
        own = pltpu.make_async_copy(self.piece(at.b), dst, sems.at[0])
        near = remote(self.piece(1 - at.b), dst, sems.at[1], sems.at[4], at.sib)
        first = remote(
            self.piece(at.b), dst, sems.at[2], sems.at[5], (at.dh, at.b, 1 - at.th, at.tl)
        )
        second = remote(
            self.piece(1 - at.b), dst, sems.at[3], sems.at[5], (at.dh, 1 - at.b, 1 - at.th, at.tl)
        )
        return own, near, first, second

    def zstart(self):
        own, near, first, second = self.zcopies()

        @pl.when(self.same)
        def _():
            near.start()
            own.start()

        @pl.when(jnp.logical_not(self.same))
        def _():
            first.start()
            second.start()

    def arrival(self, th, sem):
        return remote(
            self.piece(0), self.zgot.at[th], self.zsems.at[0], self.zsems.at[sem], self.at.sib
        )

    def zsum(self):
        at = self.at
        own, near, first, second = self.zcopies()

        @pl.when(self.same)
        def _():
            near.wait_send()
            own.wait()

        @pl.when(jnp.logical_not(self.same))
        def _():
            first.wait_send()
            second.wait_send()
            self.arrival(at.th, 4).wait_recv()

        self.arrival(1 - at.th, 5).wait_recv()
        total = self.zgot[0].astype(F32) + self.zgot[1].astype(F32)
        if self.flip is None:
            for kind in range(3):
                self.out[kind][...] = total[:, kind * LANES : (kind + 1) * LANES]
        else:
            self.out[...] = total.T if self.flip else total


class Rows:
    def __init__(self, at, count):
        self.at, self.R = at, count // CHUNKS

    def at_(self, chunk, owner):
        return tile(chunk * 4 + owner, self.R)

    def whole(self, chunk):
        return pl.ds(chunk * 4 * self.R, 4 * self.R)

    def own(self, chunk):
        return pl.ds(chunk * self.R, self.R)


class Spread:
    def __init__(self, at, rows, buf, sems):
        self.at, self.rows, self.buf, self.sems = at, rows, buf, sems

    @staticmethod
    def scratch(width):
        return [pltpu.SemaphoreType.DMA((6, CHUNKS))]

    def copy(self, chunk, kind, owner):
        ref = self.buf.at[self.rows.at_(chunk, owner)]
        device = self.at.link if kind == 0 else self.at.sib
        return remote(ref, ref, self.sems.at[kind, chunk], self.sems.at[3 + kind, chunk], device)

    def start(self, chunk):
        self.copy(chunk, 0, self.at.mine).start()
        self.copy(chunk, 1, self.at.mine).start()

    def forward(self, chunk):
        self.copy(chunk, 0, self.at.links).wait_recv()
        self.copy(chunk, 2, self.at.links).start()

    def wait(self, chunk):
        self.copy(chunk, 1, self.at.sibs).wait_recv()
        self.copy(chunk, 2, self.at.diags).wait_recv()

    def finish(self):
        for chunk in range(CHUNKS):
            self.copy(chunk, 0, self.at.mine).wait_send()
            self.copy(chunk, 1, self.at.mine).wait_send()
            self.copy(chunk, 2, self.at.links).wait_send()


class Collect:
    def __init__(self, at, rows, part, sent, got, sent_far, got_far, sems):
        self.at, self.R, self.part = at, rows.R, part
        self.sent, self.got, self.sent_far, self.got_far, self.sems = sent, got, sent_far, got_far, sems

    @staticmethod
    def scratch(count, width):
        R = count // CHUNKS
        return [
            pltpu.VMEM((CHUNKS, 2 * R, width), BF16),
            pltpu.VMEM((CHUNKS, 2 * R, width), BF16),
            pltpu.VMEM((CHUNKS, R, width), BF16),
            pltpu.VMEM((CHUNKS, R, width), BF16),
        ]

    SEMS = pltpu.SemaphoreType.DMA((4, CHUNKS))

    def near(self, chunk):
        return remote(
            self.sent.at[chunk],
            self.got.at[chunk],
            self.sems.at[0, chunk],
            self.sems.at[1, chunk],
            self.at.sib,
        )

    def far(self, chunk):
        return remote(
            self.sent_far.at[chunk],
            self.got_far.at[chunk],
            self.sems.at[2, chunk],
            self.sems.at[3, chunk],
            self.at.link,
        )

    def left(self, ref, chunk):
        halves = [ref[tile(2 * chunk + b, 2 * self.R), :] for b in (self.at.b, 1 - self.at.b)]
        return jnp.concatenate(halves, axis=0)

    def put(self, chunk, span, values):
        self.part[chunk, :, span] = values[: 2 * self.R]
        self.sent[chunk, :, span] = values[2 * self.R :].astype(BF16)

    def start(self, chunk):
        self.near(chunk).start()

    def half(self, chunk, tl):
        mine = self.part[chunk, tile(tl, self.R), :]
        return mine + self.got[chunk, tile(tl, self.R), :].astype(F32)

    def forward(self, chunk):
        self.near(chunk).wait_recv()
        self.sent_far[chunk] = self.half(chunk, 1 - self.at.tl).astype(BF16)
        self.far(chunk).start()

    def take(self, chunk):
        self.far(chunk).wait_recv()
        return self.half(chunk, self.at.tl) + self.got_far[chunk].astype(F32)

    def finish(self):
        for chunk in range(CHUNKS):
            self.near(chunk).wait_send()
            self.far(chunk).wait_send()


class Take:
    def __init__(self, refs):
        self.refs = list(refs)

    def __call__(self, count=None):
        if count is None:
            return self.refs.pop(0)
        return [self.refs.pop(0) for _ in range(count)]


class Local:
    def __init__(self, sems):
        self.sems, self.used = sems, 0

    def start(self, src, dst):
        copy = pltpu.make_async_copy(src, dst, self.sems.at[self.used])
        self.used += 1
        copy.start()
        return copy


def stats(values):
    center = values - jnp.mean(values, axis=-1, keepdims=True)
    inverse = lax.rsqrt(jnp.mean(center * center, axis=-1, keepdims=True) + EPSILON)
    return center * inverse, inverse


def norm(values, gain, shift):
    return stats(values)[0] * gain + shift


def norm_back(upstream, scaled, inverse, gain):
    weighted = upstream * gain
    first_mean = jnp.mean(weighted, axis=-1, keepdims=True)
    second_mean = jnp.mean(weighted * scaled, axis=-1, keepdims=True)
    return inverse * (weighted - first_mean - scaled * second_mean)


def lane():
    return lax.broadcasted_iota(jnp.int32, (1, LANES), 1)


def turned(values, cosines, sines):
    within = lax.rem(lane(), HEAD_DIM)
    former = lax.rem(within, ROT) < ROT // 2
    half = ROT // 2
    moved = jnp.where(former, pltpu.roll(values, LANES - half, 1), pltpu.roll(values, half, 1))
    return values * cosines + moved * sines


def of_head(values, head):
    keep = (lane() // HEAD_DIM) == head % 2
    return jnp.where(keep, values, jnp.zeros_like(values))


def gelu_and_slope(u):
    size = jnp.abs(u) * 0.7071067811865476
    t = 1.0 / (1.0 + 0.3275911 * size)
    bell = jnp.exp(-0.5 * u * u)
    poly = t * (
        0.127414796
        + t * (-0.142248368 + t * (0.7107068705 + t * (-0.7265760135 + t * 0.5307027145)))
    )
    tail = poly * bell
    phi = jnp.where(u < 0, tail, 1.0 - tail)
    return u * phi, phi + u * bell * RSQRT_2PI


def tables(places, cosines, sines, rows):
    row = lax.broadcasted_iota(jnp.int32, (HEAD_DIM, places.shape[1]), 0)
    which = row // ROT
    place = jnp.where(
        which == 0, places[0:1, :], jnp.where(which == 1, places[1:2, :], places[2:3, :])
    )
    step = lax.rem(row, ROT // 2).astype(F32) / (ROT // 2)
    frequency = jnp.where(which < 3, jnp.exp(step * -9.210340371976184), 0.0)
    angle = place * frequency
    sign = jnp.where(lax.rem(row, ROT) < ROT // 2, -1.0, 1.0)
    for table, values in ((cosines, jnp.cos(angle)), (sines, jnp.sin(angle) * sign)):
        turned_values = jnp.concatenate([values, values], axis=0).T
        for k in range(CHUNKS):
            for owner in range(4):
                start = (owner * CHUNKS + k) * rows.R
                table[pl.ds((k * 4 + owner) * rows.R, rows.R), :] = turned_values[
                    start : start + rows.R, :
                ]


def forward_kernel(n, refs):
    take = Take(refs)
    tokens, cotangent, clip_mask, positions = take(4)
    triple_in, triple_bias, exit_in, expand_in, expand_bias, shrink_in = take(6)
    norm_gain, norm_shift, branch_bias = take(3)
    upstream, cosines_out, sines_out, small_out, em_out = take(5)
    outs = [take(15) for _ in range(LAYERS)]
    x, smalls, small, parameters, turned_tokens, turned_cotangent, cosines, sines = take(8)
    exit_turned, shrink_turned, triple_turned, em = take(4)
    weights = [take(4) for _ in range(LAYERS)]
    n1, n2, qp, kp, vp, vt, o, g, slope, lse, ot, part = take(12)
    spread_sems = take(2 * LAYERS)
    one_buffers, two_buffers = take(4), take(4)
    collect_sems = take(2 * LAYERS)
    gather_sems = [[take(2) for _ in range(4)] for _ in range(LAYERS)]
    em_sems, token_sems, small_sems, cotangent_sems, local_sems = take(5)

    at = Place()
    local = Local(local_sems)
    rows = Rows(at, x.shape[0])
    slices = [
        [source.at[l] for source in (triple_turned, exit_turned, expand_in, shrink_turned)]
        for l in range(LAYERS)
    ]
    gathers = [
        [Gather(at, *triple) for triple in zip(slices[l], weights[l], *zip(*gather_sems[l]))]
        for l in range(LAYERS)
    ]
    smalls[...] = jnp.zeros_like(smalls)
    smalls[0:3, :] = positions[...].astype(F32)
    smalls[3:4, :] = jnp.broadcast_to(clip_mask[...].astype(F32), (1, smalls.shape[1]))
    for l in range(LAYERS):
        for kind in range(3):
            width = triple_bias.shape[2]
            columns = slice(kind * width, (kind + 1) * width)
            smalls[4 + l : 5 + l, columns] = triple_bias[kind, l : l + 1, :].astype(F32)
            triple_turned[l, :, columns] = triple_in[l, kind]
        smalls[6 + l : 7 + l, :] = expand_bias[l : l + 1, :].astype(F32)
    swap_small = Swap(at, smalls, small, small_sems)
    swap_tokens = [
        Swap(
            at,
            tokens.at[rows.own(k)],
            turned_tokens.at[rows.own(k)],
            token_sems.at[k],
        )
        for k in range(CHUNKS)
    ]
    swap_cotangent = Swap(at, cotangent, turned_cotangent, cotangent_sems)

    at.barrier()
    gathers[0][0].zstart()
    swap_small.start()
    for swap in swap_tokens:
        swap.start()
    for l in range(LAYERS):
        exit_turned[l] = exit_in[l].T
        shrink_turned[l] = shrink_in[l].T
        for index, source in enumerate((norm_gain, norm_shift, branch_bias)):
            parameters[8 * l + 2 * index : 8 * l + 2 * index + 2, :] = source[l].astype(F32)
    swap_small.wait()
    tables(small, cosines, sines, rows)
    saves = [
        local.start(*pair)
        for pair in ((cosines, cosines_out), (sines, sines_out), (small, small_out))
    ]
    spread_em = Spread(at, rows, em, em_sems)

    def begin(l):
        spread = [Spread(at, rows, buf, spread_sems[2 * l + i]) for i, buf in enumerate((n1, n2))]
        collect = [
            Collect(at, rows, part, *buffers, collect_sems[2 * l + i])
            for i, buffers in enumerate((one_buffers, two_buffers))
        ]
        return spread + collect

    stages = [begin(l) for l in range(LAYERS)]

    def row(l, index):
        return parameters[8 * l + index : 8 * l + index + 1, :]

    def first_norm(l, k):
        n1[rows.at_(k, at.mine), :] = norm(x[rows.own(k), :], row(l, 0), row(l, 2)).astype(BF16)
        stages[l][0].start(k)

    def project(l, k):
        stages[l][0].wait(k)
        whole = rows.whole(k)
        wa = weights[l][0]
        for kind in range(3):
            columns = slice(2 * kind * LANES, 2 * (kind + 1) * LANES)
            bias = small[4 + l : 5 + l, columns]
            both = dot(n1[whole, :], wa[:, columns], NN) + bias
            for pair in range(2):
                t = both[:, pair * LANES : (pair + 1) * LANES]
                if kind < 2:
                    t = turned(t, cosines[whole, :], sines[whole, :])
                if kind == 0:
                    qp[pair, whole, :] = (t * (SCALE * LOG2E)).astype(BF16)
                elif kind == 1:
                    kp[pair, whole, :] = t.astype(BF16)
                else:
                    vp[pair, whole, :] = t.astype(BF16)
                    vt[pl.ds(pair * LANES, LANES), whole] = t.T.astype(BF16)

    def attention(k):
        whole = rows.whole(k)

        def head(h, carry):
            scores = dot(kp[h // 2], of_head(qp[h // 2, whole, :], h), NT)
            highest = jnp.max(scores, axis=0, keepdims=True)
            weights = jnp.exp2(scores - highest)
            total = jnp.sum(weights, axis=0, keepdims=True)
            spans = tile(h, HEAD_DIM)
            ot[spans, :] = dot(vt[spans, :], weights.astype(BF16), NN) / total
            lse[pl.ds(h, 1), whole] = highest + jnp.log2(total)
            return carry

        lax.fori_loop(0, 4, head, 0)
        o[whole, :] = ot[...].T.astype(BF16)

    def leave(l, k):
        wb, collect = weights[l][1], stages[l][2]
        left = collect.left(o, k)

        def columns(j, carry):
            span = tile(j, 256)
            collect.put(k, span, dot(left, wb[span, :], NT))
            return carry

        lax.fori_loop(0, part.shape[2] // 256, columns, 0)
        collect.start(k)

    def second_norm(l, k):
        own = rows.own(k)
        x[own, :] = x[own, :] + (stages[l][2].take(k) + row(l, 4))
        n2[rows.at_(k, at.mine), :] = norm(x[own, :], row(l, 1), row(l, 3)).astype(BF16)
        stages[l][1].start(k)

    def up(l, k):
        whole = rows.whole(k)
        wc = weights[l][2]
        stages[l][1].wait(k)

        def columns(j, carry):
            span = tile(j, 256)
            u = dot(n2[whole, :], wc[:, span], NN) + small[pl.ds(6 + l, 1), span]
            active, grade = gelu_and_slope(u)
            g[whole, span] = active.astype(BF16)
            slope[whole, span] = grade.astype(BF16)
            return carry

        lax.fori_loop(0, wc.shape[1] // 256, columns, 0)

    def down(l, k):
        wd, collect = weights[l][3], stages[l][3]
        left = collect.left(g, k)

        def outputs(j, carry):
            span = tile(j, 256)
            collect.put(k, span, dot(left, wd[span, :], NT))
            return carry

        lax.fori_loop(0, part.shape[2] // 256, outputs, 0)
        collect.start(k)

    def end(l, k):
        own = rows.own(k)
        x[own, :] = x[own, :] + (stages[l][3].take(k) + row(l, 5))
        if l + 1 < LAYERS:
            first_norm(l + 1, k)

    A, B, C, D = range(4)

    def begin_plane(gather):
        gather.zwait()
        gather.pstart()

    begin_plane(gathers[0][A])
    for k in range(CHUNKS):
        swap_tokens[k].wait()
        x[rows.own(k), :] = turned_tokens[rows.own(k), :].astype(F32)
        first_norm(0, k)
    for gather in gathers[0][B:]:
        gather.zstart()
    gathers[0][A].pforward()
    pending = []
    for l in range(LAYERS):
        hidden_out, middle_out, *full_outs = outs[l][:6]
        n1_out, n2_out, qp_out, kp_out, vp_out, o_out, g_out, slope_out, lse_out = outs[l][6:]
        spread_one, spread_two, collect_one, collect_two = stages[l]
        now = gathers[l]
        following = gathers[l + 1] if l + 1 < LAYERS else None
        save_x = local.start(x, hidden_out)
        for k in range(CHUNKS):
            spread_one.forward(k)
        now[A].pwait()
        if l == 0:
            begin_plane(now[B])
        else:
            now[B].pforward()
            begin_plane(now[C])
        for save in pending:
            save.wait()
        for k in range(CHUNKS):
            project(l, k)
        spread_one.finish()
        save_n1 = local.start(n1, n1_out)
        pending = [
            local.start(*pair) for pair in ((qp, qp_out), (kp, kp_out), (vp, vp_out))
        ]
        if l == 0:
            now[B].pforward()
        attention(0)
        now[B].pwait()
        leave(l, 0)
        if l == 0:
            begin_plane(now[C])
            following[A].zstart()
            following[B].zstart()
        attention(1)
        collect_one.forward(0)
        leave(l, 1)
        if l:
            begin_plane(now[D])
            now[C].pforward()
        save_x.wait()
        attention(2)
        collect_one.forward(1)
        leave(l, 2)
        second_norm(l, 0)
        attention(3)
        collect_one.forward(2)
        leave(l, 3)
        if l == 0:
            now[C].pforward()
            begin_plane(now[D])
            following[C].zstart()
        if not following:
            swap_cotangent.wait()
            upstream[...] = turned_cotangent[...].astype(F32) * small[3:4, :]
            for k in range(CHUNKS):
                em[rows.at_(k, at.mine), :] = upstream[rows.own(k), :].astype(BF16)
        second_norm(l, 1)
        collect_one.forward(3)
        second_norm(l, 2)
        second_norm(l, 3)
        if not following:
            for k in range(CHUNKS):
                spread_em.start(k)
        save_x = local.start(x, middle_out)
        pending += [local.start(o, o_out), local.start(lse, lse_out)]
        save_n1.wait()
        spread_two.forward(0)
        now[C].pwait()
        for k in range(CHUNKS):
            up(l, k)
            if k == 1 and following:
                begin_plane(following[A])
            if k == 1 and not following:
                now[D].pforward()
            if k + 1 < CHUNKS:
                spread_two.forward(k + 1)
        if following:
            now[D].pforward()
        else:
            for k in range(CHUNKS):
                spread_em.forward(k)
        pending += [local.start(*pair) for pair in ((n2, n2_out), (g, g_out), (slope, slope_out))]
        save_x.wait()
        spread_two.finish()
        now[D].pwait()
        pending += [local.start(*pair) for pair in zip(weights[l], full_outs)]
        if not following:
            collect_one.finish()
            for k in range(CHUNKS):
                spread_em.wait(k)
            spread_em.finish()
            pending.append(local.start(em, em_out))
            continue
        for k in range(CHUNKS):
            down(l, k)
            if k:
                collect_two.forward(k - 1)
            if k == 0:
                following[D].zstart()
                swap_cotangent.start()
            if k == 1:
                begin_plane(following[B])
            if k > 1:
                end(l, k - 2)
        collect_two.forward(CHUNKS - 1)
        end(l, CHUNKS - 2)
        following[A].pforward()
        end(l, CHUNKS - 1)
        collect_one.finish()
        collect_two.finish()
    for save in saves + pending:
        save.wait()


def backward_kernel(n, refs):
    take = Take(refs)
    upstream, gain_in, bias_in, small, em_in = take(5)
    ins = [take(15) for _ in range(LAYERS)]
    cosines_in, sines_in = take(2)
    mixed_out, grad_out, triple_out, triple_bias_out, exit_out, expand_out = take(6)
    expand_bias_out, shrink_out, gain_out, shift_out, bias_out = take(5)
    e, xs, wa, wb, wc, wd = take(6)
    em, ea, n2, qp, kp, vp, kt, o, g, du, lse = take(11)
    dk, dv, dqt, do, part, gd, ge, vectors, cosines, sines = take(10)
    dt, gt = take(2), take(2)
    mixed, turned_mixed, low_grad_own, turned_grad = take(4)
    part_last, last_got, last_sems = take(), take(2), take()
    spread_sems = take(2 * LAYERS)
    one_buffers, two_buffers = take(4), take(4)
    collect_sems = take(2 * LAYERS)
    scatter_buffers = [take(2) for _ in range(5)]
    scatter_layers = [[take(3) for _ in range(5)] for _ in range(LAYERS)]
    mixed_sems, grad_sems = take(2)
    plane, column, plane_sems, column_sems = take(4)
    local_sems = take()

    at = Place()
    local = Local(local_sems)
    rows = Rows(at, e.shape[0])

    def load(l, name):
        where = {
            "hidden": (0, xs),
            "middle": (1, xs),
            "a": (2, wa),
            "b": (3, wb),
            "c": (4, wc),
            "d": (5, wd),
            "n1": (6, g),
            "n2": (7, n2),
            "q": (8, qp),
            "k": (9, kp),
            "v": (10, vp),
            "o": (11, o),
            "g": (12, g),
            "slope": (13, du),
            "lse": (14, lse),
        }
        index, target = where[name]
        loads[(l, name)] = local.start(ins[l][index], target)

    def ready(l, *names):
        for name in names:
            loads.pop((l, name)).wait()

    loads = {}
    top = LAYERS - 1
    load_em = local.start(em_in, em)
    load_e = local.start(upstream, e)
    for name in ("d", "slope", "c", "middle", "g", "n2", "b", "q", "k", "v", "o", "lse", "a"):
        load(top, name)
    load_tables = [local.start(cosines_in, cosines), local.start(sines_in, sines)]

    cubes = [(db, dth, dtl) for db in range(2) for dth in range(2) for dtl in range(2)][1:]

    def flipped(flips):
        return [jnp.abs(coordinate - flip) for coordinate, flip in zip(at.me[1:], flips)]

    barrier = pltpu.get_barrier_semaphore()
    greeted = [(at.dh, *flipped(flips)) for flips in cubes]
    greeted += [at.peer(step) for step in range(1, n)]
    for device in greeted:
        pl.semaphore_signal(barrier, inc=1, device_id=device, device_id_type=MESH)
    pl.semaphore_wait(barrier, len(greeted))

    spreads = [
        [Spread(at, rows, buf, spread_sems[2 * l + i]) for i, buf in enumerate((em, ea))]
        for l in range(LAYERS)
    ]
    collects = [
        [
            Collect(at, rows, part, *buffers, collect_sems[2 * l + i])
            for i, buffers in enumerate((one_buffers, two_buffers))
        ]
        for l in range(LAYERS)
    ]
    def triple_columns(l, pair):
        return [triple_out.at[l, kind, :, pl.ds(pair * LANES, LANES)] for kind in range(3)]

    def pieces(l):
        return (
            (gt[0], triple_columns(l, 0), None),
            (gt[1], triple_columns(l, 1), None),
            (ge, exit_out.at[l], True),
            (wd, expand_out.at[l], False),
            (gd, shrink_out.at[l], True),
        )

    scatters = [
        [
            Scatter(at, *piece, *buffers, *own)
            for piece, buffers, own in zip(pieces(l), scatter_buffers, scatter_layers[l])
        ]
        for l in range(LAYERS)
    ]
    collect_last = Collect(
        at, rows, part_last, two_buffers[0], last_got[0], two_buffers[2], last_got[1], last_sems
    )
    swap_mixed = Swap(at, mixed, turned_mixed, mixed_sems)
    swap_grads = [
        Swap(
            at, low_grad_own.at[rows.own(k)], turned_grad.at[rows.own(k)], grad_sems.at[k]
        )
        for k in range(CHUNKS)
    ]
    vectors[...] = jnp.zeros_like(vectors)

    def add(l, row, values):
        vectors[8 * l + row : 8 * l + row + 1, : values.shape[1]] += jnp.sum(
            values.astype(F32), axis=0, keepdims=True
        )

    def weight_grad(left, right, out):
        def block(j, carry):
            span = tile(j, 256)
            out[span, :] = dot(left[:, span], right[...], TN).astype(BF16)
            return carry

        lax.fori_loop(0, left.shape[1] // 256, block, 0)

    def send_branch(l, k):
        low = e[rows.own(k), :].astype(BF16)
        em[rows.at_(k, at.mine), :] = low
        spreads[l][0].start(k)
        add(l, 5, low)

    def shrink_back(l, k):
        if l < top:
            spreads[l][0].forward(k)
            spreads[l][0].wait(k)
        whole = rows.whole(k)
        collect = collects[l][0]

        def columns(j, carry):
            span = tile(j, 256)
            active_grad = dot(em[whole, :], wd[:, span], NN)
            du[whole, span] = (active_grad * du[whole, span].astype(F32)).astype(BF16)
            return carry

        lax.fori_loop(0, wd.shape[1] // 256, columns, 0)
        add(l, 6, du[whole, :])
        left = collect.left(du, k)

        def outputs(j, carry):
            span = tile(j, 256)
            collect.put(k, span, dot(left, wc[span, :], NT))
            return carry

        lax.fori_loop(0, part.shape[2] // 256, outputs, 0)
        collect.start(k)

    def norm_step(l, k, which):
        own = rows.own(k)
        scaled, inverse = stats(xs[own, :])
        grads = collects[l][1 - which].take(k)
        add(l, which, grads * scaled)
        add(l, 2 + which, grads)
        gain = gain_in[l, which : which + 1, :].astype(F32)
        e[own, :] = e[own, :] + norm_back(grads, scaled, inverse, gain)

    def middle_step(l, k):
        norm_step(l, k, 1)
        low = e[rows.own(k), :].astype(BF16)
        ea[rows.at_(k, at.mine), :] = low
        spreads[l][1].start(k)
        add(l, 4, low)

    def first_step(l, k):
        norm_step(l, k, 0)
        if l:
            send_branch(l - 1, k)
        else:
            low_grad_own[rows.own(k), :] = e[rows.own(k), :].astype(BF16)
            swap_grads[k].start()

    def branch_last(k):
        left = collect_last.left(g, k)

        def outputs(j, carry):
            span = tile(j, 256)
            collect_last.put(k, span, dot(left, wd[span, :], NT))
            return carry

        lax.fori_loop(0, part.shape[2] // 256, outputs, 0)
        collect_last.start(k)

    def end_last(k):
        own = rows.own(k)
        bias = bias_in[top, 1:2, :].astype(F32)
        hidden = xs[own, :] + (collect_last.take(k) + bias)
        mixed[own, :] = (hidden * small[3:4, :]).astype(BF16)

    def attention_back(l, pair, k):
        whole = rows.whole(k)
        if pair == 0:
            spreads[l][1].wait(k)
            do[whole, :] = dot(ea[whole, :], wb[...], NN).astype(BF16)
        lanes = slice(pair * LANES, (pair + 1) * LANES)
        dop = do[whole, lanes]
        product = dop.astype(F32) * o[whole, lanes].astype(F32)
        high = product.astype(BF16)
        rest = (product - high.astype(F32)).astype(BF16)
        for half in range(2):
            h = 2 * pair + half
            pick = jnp.broadcast_to(((lane() // HEAD_DIM) == half).astype(BF16), (8, LANES))
            center = dot(pick, high, NT) + dot(pick, rest, NT)
            qh = of_head(qp[pair, whole, :], half)
            doh = of_head(dop, half)
            scores = dot(kp[pair], qh, NT)
            chances = jnp.exp2(scores - lse[h : h + 1, whole])
            chance_grad = dot(vp[pair], doh, NT)
            score_grad = (chances * (chance_grad - center[0:1, :])).astype(BF16)
            dv[pair] += dot(chances.astype(BF16), doh, NN)
            dk[pair] += dot(score_grad, qh, NN)
            spans = slice(h * HEAD_DIM, (h + 1) * HEAD_DIM)
            dqt[half * HEAD_DIM : (half + 1) * HEAD_DIM, :] = dot(kt[spans, :], score_grad, NN)
        dq = dqt[...].T * SCALE
        dt[pair][whole, :LANES] = turned(dq, cosines[whole, :], -sines[whole, :]).astype(BF16)

    def pair_done(l, pair):
        dt[pair][:, LANES : 2 * LANES] = turned(
            dk[pair] * LN2, cosines[...], -sines[...]
        ).astype(BF16)
        dt[pair][:, 2 * LANES :] = dv[pair].astype(BF16)
        weight_grad(g, dt[pair], gt[pair])
        scatters[l][pair].pstart()

    def triple_sum(l):
        width = 2 * LANES
        for pair in range(2):
            sums = jnp.sum(dt[pair][...].astype(F32), axis=0, keepdims=True)
            for kind in range(3):
                start = kind * width + pair * LANES
                vectors[8 * l + 7 : 8 * l + 8, start : start + LANES] = sums[
                    :, kind * LANES : (kind + 1) * LANES
                ]

    def projection_back(l, k):
        collect = collects[l][1]
        left = jnp.concatenate(
            [
                collect.left(dt[pair], k)[:, kind * LANES : (kind + 1) * LANES]
                for kind in range(3)
                for pair in range(2)
            ],
            axis=1,
        )

        def outputs(j, carry):
            span = tile(j, 256)
            collect.put(k, span, dot(left, wa[span, :], NT))
            return carry

        lax.fori_loop(0, part.shape[2] // 256, outputs, 0)
        collect.start(k)

    load_e.wait()
    load_em.wait()
    for k in range(CHUNKS):
        add(top, 5, em[rows.at_(k, at.mine), :])
    for l in reversed(range(LAYERS)):
        spread_one, spread_two = spreads[l]
        collect_one, collect_two = collects[l]
        st0, st1, se, sc, sd = scatters[l]
        previous = scatters[l + 1] if l < top else None
        ready(l, "d", "slope", "c", "middle")
        for k in range(CHUNKS):
            shrink_back(l, k)
            if k:
                collect_one.forward(k - 1)
            if k > 1:
                middle_step(l, k - 2)
        collect_one.forward(CHUNKS - 1)
        if previous:
            spread_one.finish()
            previous[1].psum()
        ready(l, "g")
        if l == top:
            branch_last(0)
            branch_last(1)
        weight_grad(em, g, gd)
        sd.pstart()
        middle_step(l, CHUNKS - 2)
        middle_step(l, CHUNKS - 1)
        if l == top:
            branch_last(2)
            branch_last(3)
        else:
            load(l, "hidden")
        load(l, "n1")
        ready(l, "n2")
        weight_grad(n2, du, wd)
        sc.pstart()
        if l:
            load(l - 1, "slope")
            load(l - 1, "c")
            load(l - 1, "n2")
        ready(l, "b", "q", "k", "v", "o", "lse")
        for pair in range(2):
            kt[pl.ds(pair * LANES, LANES), :] = kp[pair].astype(F32).T.astype(BF16)
        dk[...] = jnp.zeros_like(dk)
        dv[...] = jnp.zeros_like(dv)
        if l == top:
            for copy in load_tables:
                copy.wait()
        spread_two.forward(0)
        spread_two.forward(1)
        attention_back(l, 0, 0)
        spread_two.forward(2)
        spread_two.forward(3)
        sd.pforward()
        if l == top:
            collect_last.forward(0)
            collect_last.forward(1)
        else:
            previous[1].zstart()
        attention_back(l, 0, 1)
        if l == top:
            collect_last.forward(2)
            collect_last.forward(3)
        sc.pforward()
        attention_back(l, 0, 2)
        sd.psum()
        sd.zstart()
        attention_back(l, 0, 3)
        spread_two.finish()
        weight_grad(ea, o, ge)
        se.pstart()
        ready(l, "n1")
        pair_done(l, 0)
        sc.psum()
        sc.zstart()
        attention_back(l, 1, 0)
        if l == top:
            for k in range(CHUNKS):
                end_last(k)
            load(l, "hidden")
            swap_mixed.start()
        else:
            previous[1].zsum()
        attention_back(l, 1, 1)
        se.pforward()
        st0.pforward()
        attention_back(l, 1, 2)
        se.psum()
        se.zstart()
        attention_back(l, 1, 3)
        st0.psum()
        st0.zstart()
        ready(l, "a")
        if l == top:
            collect_last.finish()
        pair_done(l, 1)
        for k in range(CHUNKS):
            projection_back(l, k)
            if k:
                collect_two.forward(k - 1)
        collect_two.forward(CHUNKS - 1)
        triple_sum(l)
        ready(l, "hidden")
        if l:
            for name in ("d", "g", "b", "q", "k", "v", "o", "lse", "a"):
                load(l - 1, name)
        collect_one.finish()
        sd.zsum()
        first_step(l, 0)
        first_step(l, 1)
        st1.pforward()
        first_step(l, 2)
        first_step(l, 3)
        if l:
            load(l - 1, "middle")
        collect_two.finish()
        for scatter in (sc, se, st0):
            scatter.zsum()

    last = scatters[0][1]
    plane[at.dh] = vectors[...]

    def plane_copy(step, slot):
        ref = plane.at[slot]
        return remote(ref, ref, plane_sems.at[0, step], plane_sems.at[1, step], at.peer(step))

    for step in range(1, n):
        plane_copy(step, at.dh).start()
    last.psum()
    last.zstart()
    for step in range(1, n):
        plane_copy(step, at.dh).wait_send()
        plane_copy(step, lax.rem(at.dh + n - step, n)).wait_recv()
    total = plane[0]
    for index in range(1, n):
        total = total + plane[index]

    def slot(b, th, tl):
        return 4 * b + 2 * th + tl

    mine = slot(*at.me[1:])
    column[mine] = total

    def column_copy(index, flips, where):
        ref = column.at[where]
        device = (at.dh, *flipped(flips))
        return remote(ref, ref, column_sems.at[0, index], column_sems.at[1, index], device)

    for index, flips in enumerate(cubes):
        column_copy(index, flips, mine).start()
    swap_mixed.wait()
    save_mixed = local.start(turned_mixed, mixed_out)
    for index, flips in enumerate(cubes):
        column_copy(index, flips, mine).wait_send()
        column_copy(index, flips, slot(*flipped(flips))).wait_recv()
    total = column[0]
    for index in range(1, 8):
        total = total + column[index]
    own = column[slot(at.th, 0, at.tl)] + column[slot(at.th, 1, at.tl)]
    width = triple_bias_out.shape[2]
    for l in range(LAYERS):
        gain_out[l] = total[8 * l : 8 * l + 2, :]
        shift_out[l] = total[8 * l + 2 : 8 * l + 4, :]
        bias_out[l] = total[8 * l + 4 : 8 * l + 6, :]
        expand_bias_out[l : l + 1, :] = own[8 * l + 6 : 8 * l + 7, :]
        for kind in range(3):
            triple_bias_out[kind, l : l + 1, :] = own[
                8 * l + 7 : 8 * l + 8, kind * width : (kind + 1) * width
            ]
    for k in range(CHUNKS):
        swap_grads[k].wait()
    save_grad = local.start(turned_grad, grad_out)
    last.zsum()
    save_mixed.wait()
    save_grad.wait()


def finish_kernel(*refs):
    half = len(refs) // 2
    for source, target in zip(refs[:half], refs[half:]):
        if len(source.shape) < len(target.shape):
            target[:, 0, :] = source[...].astype(F32)
        else:
            target[...] = source[...]


def call(body, args, vmem_in, outs, vmem_out, scratch, collective_id, name, flops=0):
    def kernel(*refs):
        body(refs)

    in_specs = [VMEM if index in vmem_in else ANY for index in range(len(args))]
    out_specs = [VMEM if index in vmem_out else ANY for index in range(len(outs))]
    return pl.pallas_call(
        kernel,
        out_shape=outs,
        in_specs=in_specs,
        out_specs=out_specs,
        scratch_shapes=scratch,
        compiler_params=pltpu.CompilerParams(
            collective_id=collective_id, has_side_effects=True, vmem_limit_bytes=VMEM_LIMIT
        ),
        name=name,
    )(*args)


def shards(
    n,
    tokens,
    cotangent,
    clip_mask,
    positions,
    triple_weight,
    triple_bias,
    exit_weight,
    expand_weight,
    expand_bias,
    shrink_weight,
    norm_gain,
    norm_shift,
    branch_bias,
):
    count, _, depth = tokens.shape
    seq = 4 * count
    size = triple_weight.shape[1]
    local = triple_weight.shape[3]
    inner = expand_weight.shape[2]
    wide = 3 * local
    pairs = local // LANES
    R = count // CHUNKS
    V, DMA, shape = pltpu.VMEM, pltpu.SemaphoreType.DMA, jax.ShapeDtypeStruct
    wides = (wide, local, inner, inner)
    pair_shape = (pairs, seq, LANES)
    args = [
        tokens[:, 0, :],
        cotangent[:, 0, :],
        clip_mask[:, None],
        positions[:, 0, :],
        triple_weight.transpose(0, 2, 1, 3),
        triple_bias.transpose(1, 0, 2),
        exit_weight,
        expand_weight,
        expand_bias,
        shrink_weight,
        norm_gain,
        norm_shift,
        branch_bias,
    ]
    outs = [
        shape((count, depth), F32),
        shape((seq, LANES), F32),
        shape((seq, LANES), F32),
        shape((8, depth), F32),
        shape((seq, depth), BF16),
    ]
    for _ in range(LAYERS):
        outs += [shape((count, depth), F32)] * 2
        outs += [shape((depth, width), BF16) for width in wides]
        outs += [shape((seq, depth), BF16)] * 2
        outs += [shape(pair_shape, BF16)] * 3
        outs += [shape((seq, local), BF16)]
        outs += [shape((seq, inner), BF16)] * 2
        outs += [shape((8, seq), F32)]
    scratch = [
        V((count, depth), F32),
        V((8, depth), F32),
        V((8, depth), F32),
        V((8 * LAYERS, depth), F32),
        V((count, depth), BF16),
        V((count, depth), BF16),
        V((seq, LANES), F32),
        V((seq, LANES), F32),
        V((LAYERS, size, local), BF16),
        V((LAYERS, size, inner), BF16),
        V((LAYERS, size, wide), BF16),
        V((seq, depth), BF16),
    ]
    for _ in range(LAYERS):
        scratch += [V((depth, width), BF16) for width in wides]
    scratch += [V((seq, depth), BF16)] * 2
    scratch += [V(pair_shape, BF16)] * 3
    scratch += [V((local, seq), BF16), V((seq, local), BF16)]
    scratch += [V((seq, inner), BF16)] * 2
    scratch += [V((8, seq), F32), V((local, 4 * R), F32), V((CHUNKS, 2 * R, depth), F32)]
    scratch += Spread.scratch(depth) * (2 * LAYERS)
    scratch += Collect.scratch(count, depth) * 2
    scratch += [Collect.SEMS] * (2 * LAYERS)
    scratch += Gather.scratch(n) * (4 * LAYERS)
    scratch += Spread.scratch(depth)
    scratch += [DMA((CHUNKS, 3)), DMA((3,)), DMA((3,)), DMA((48,))]
    results = call(
        functools.partial(forward_kernel, n),
        args,
        tuple(range(len(args))),
        outs,
        (0,),
        scratch,
        1,
        "forward",
    )
    upstream, cosines, sines, small, em = results[:5]
    args = [upstream, norm_gain, branch_bias, small, em, *results[5:], cosines, sines]
    outs = [
        shape((count, depth), BF16),
        shape((count, depth), BF16),
        shape((LAYERS, 3, size, local), F32),
        shape((3, LAYERS, local), F32),
        shape(exit_weight.shape, F32),
        shape(expand_weight.shape, F32),
        shape(expand_bias.shape, F32),
        shape(shrink_weight.shape, F32),
        shape(norm_gain.shape, F32),
        shape(norm_shift.shape, F32),
        shape(branch_bias.shape, F32),
    ]
    scratch = [V((count, depth), F32)] * 2
    scratch += [V((depth, width), BF16) for width in wides]
    scratch += [V((seq, depth), BF16)] * 3
    scratch += [V(pair_shape, BF16)] * 3
    scratch += [V((local, seq), BF16), V((seq, local), BF16)]
    scratch += [V((seq, inner), BF16)] * 2
    scratch += [V((8, seq), F32)]
    scratch += [V(pair_shape, F32)] * 2
    scratch += [V((LANES, 4 * R), F32), V((seq, local), BF16), V((CHUNKS, 2 * R, depth), F32)]
    scratch += [V((depth, inner), BF16), V((depth, local), BF16)]
    scratch += [V((8 * LAYERS, depth), F32), V((seq, LANES), F32), V((seq, LANES), F32)]
    scratch += [V((seq, 3 * LANES), BF16)] * 2 + [V((depth, 3 * LANES), BF16)] * 2
    scratch += [V((count, depth), BF16)] * 4
    scratch += [V((CHUNKS, 2 * R, depth), F32)] + Collect.scratch(count, depth)[1::2] + [Collect.SEMS]
    scratch += Spread.scratch(depth) * (2 * LAYERS)
    scratch += Collect.scratch(count, depth) * 2
    scratch += [Collect.SEMS] * (2 * LAYERS)
    widths = (3 * LANES, 3 * LANES, local, inner, inner)
    for width in widths:
        scratch += Scatter.scratch(n, depth, width)
    for _ in range(LAYERS):
        for width in widths:
            scratch += Scatter.layer_scratch(n, depth, width)
    scratch += [DMA((3,)), DMA((CHUNKS, 3))]
    scratch += [V((n, 8 * LAYERS, depth), F32), V((8, 8 * LAYERS, depth), F32)]
    scratch += [DMA((2, n)), DMA((2, 7)), DMA((48,))]
    results = call(
        functools.partial(backward_kernel, n),
        args,
        (1, 2, 3),
        outs,
        tuple(range(2, len(outs))),
        scratch,
        2,
        "backward",
    )
    outs = [shape((count, 1, depth), F32)] * 2 + [shape(r.shape, F32) for r in results[2:]]
    mixed, grad, triple_total, bias_total, *others = pl.pallas_call(
        finish_kernel, out_shape=outs, name="finish"
    )(*results)
    return (
        mixed,
        grad,
        triple_total.transpose(0, 2, 1, 3),
        bias_total.transpose(1, 0, 2),
        *others,
    )


def solution(mesh):
    n = mesh.shape["dp"] // 2
    fine = jax.sharding.Mesh(
        mesh.devices.reshape(n, 2, mesh.shape["tensor"] // 2, 2), ("dh", "b", "th", "tl")
    )
    dp, tensor = ("dh", "b"), ("th", "tl")
    return jax.shard_map(
        functools.partial(shards, n),
        mesh=fine,
        in_specs=(
            P(tensor, dp, None),
            P(tensor, dp, None),
            P(dp),
            P(None, dp, None),
            P(None, dp, None, tensor),
            P(None, None, tensor),
            P(None, tensor, dp),
            P(None, dp, tensor),
            P(None, tensor),
            P(None, tensor, dp),
            P(),
            P(),
            P(),
        ),
        out_specs=(
            P(tensor, dp, None),
            P(tensor, dp, None),
            P(None, dp, None, tensor),
            P(None, None, tensor),
            P(None, tensor, dp),
            P(None, dp, tensor),
            P(None, tensor),
            P(None, tensor, dp),
            P(),
            P(),
            P(),
        ),
        check_vma=False,
    )
```

```python
import functools

import jax
import jax.numpy as jnp
from jax import lax
from jax.experimental import pallas as pl
from jax.experimental.pallas import tpu as pltpu
from jax.sharding import PartitionSpec as P

HEAD_DIM = 64
ROT = 20
LAYERS = 2
CHUNKS = 4
LANES = 128
EPSILON = 1e-06
LOG2E = 1.4426950408889634
LN2 = 0.6931471805599453
SCALE = HEAD_DIM ** (-0.5)
RSQRT_2PI = 0.3989422804014327
F32, BF16 = jnp.float32, jnp.bfloat16
NN = (((1,), (0,)), ((), ()))
NT = (((1,), (1,)), ((), ()))
TN = (((0,), (0,)), ((), ()))
MESH = pl.DeviceIdType.MESH
ANY = pl.BlockSpec(memory_space=pl.ANY)
VMEM = pl.BlockSpec(memory_space=pltpu.VMEM)
VMEM_LIMIT = 59 * 2**20


def dot(left, right, dims):
    return lax.dot_general(left, right, dims, preferred_element_type=F32)


def tile(index, size):
    return pl.ds(pl.multiple_of(index * size, size), size)


class Place:
    def __init__(self):
        self.dh, self.b, self.th, self.tl = [lax.axis_index(a) for a in ("dh", "b", "th", "tl")]
        self.n = lax.axis_size("dh")
        self.me = (self.dh, self.b, self.th, self.tl)
        self.sib = (self.dh, 1 - self.b, self.th, self.tl)
        self.link = (self.dh, self.b, self.th, 1 - self.tl)
        self.other = (self.dh, self.th, self.b, self.tl)
        self.mine = 2 * self.b + self.tl
        self.links = 2 * self.b + 1 - self.tl
        self.sibs = 2 * (1 - self.b) + self.tl
        self.diags = 2 * (1 - self.b) + 1 - self.tl

    def turn(self, which):
        y, x = self.dh // 2, lax.rem(self.dh, 2)
        across, along = 2 * y + 1 - x, 2 * (1 - y) + x
        first = self.b if which else 1 - self.b
        return first * across + (1 - first) * along

    def opposite(self):
        y, x = self.dh // 2, lax.rem(self.dh, 2)
        return 2 * (1 - y) + 1 - x

    def near(self, dh):
        return (dh, self.b, self.th, self.tl)

    def peer(self, step):
        return (lax.rem(self.dh + step, self.n), self.b, self.th, self.tl)

    def barrier(self):
        sem = pltpu.get_barrier_semaphore()
        greeted = [
            self.sib,
            self.link,
            (self.dh, self.b, 1 - self.th, self.tl),
            (self.dh, 1 - self.b, 1 - self.th, self.tl),
        ] + [self.peer(step) for step in range(1, self.n)]
        for device in greeted:
            pl.semaphore_signal(sem, inc=1, device_id=device, device_id_type=MESH)
        pl.semaphore_wait(sem, len(greeted))


def remote(src, dst, send, recv, device):
    return pltpu.make_async_remote_copy(
        src_ref=src, dst_ref=dst, send_sem=send, recv_sem=recv, device_id=device, device_id_type=MESH
    )


class Swap:
    def __init__(self, at, src, dst, sems):
        self.same = at.b == at.th
        self.far = remote(src, dst, sems.at[0], sems.at[1], at.other)
        self.near = pltpu.make_async_copy(src, dst, sems.at[2])

    def start(self):
        pl.when(self.same)(self.near.start)
        pl.when(jnp.logical_not(self.same))(self.far.start)

    def wait(self):
        pl.when(self.same)(self.near.wait)
        pl.when(jnp.logical_not(self.same))(self.far.wait)


class Gather:
    def __init__(self, at, src, full, zsems, psems):
        self.at, self.src, self.full = at, src, full
        self.zsems, self.psems = zsems, psems
        self.size = src.shape[0]
        self.same = at.b == at.th

    def slot(self, b):
        return self.full.at[tile(self.at.dh * 2 + b, self.size)]

    def block(self, dh):
        return self.full.at[tile(dh, 2 * self.size)]

    def zcopies(self):
        at = self.at
        dst = self.slot(at.b)
        far = remote(
            self.src,
            dst,
            self.zsems.at[0],
            self.zsems.at[4 + at.b],
            (at.dh, at.th, 1 - at.th, at.tl),
        )
        near = remote(self.src, dst, self.zsems.at[1], self.zsems.at[3], at.sib)
        own = pltpu.make_async_copy(self.src, dst, self.zsems.at[2])
        return far, near, own

    def zstart(self):
        far, near, own = self.zcopies()
        far.start()
        pl.when(self.same)(own.start)
        pl.when(jnp.logical_not(self.same))(near.start)

    def arrival(self, b, sem):
        return remote(self.src, self.slot(b), self.zsems.at[0], self.zsems.at[sem], self.at.sib)

    def zwait(self):
        at = self.at
        far, near, own = self.zcopies()
        far.wait_send()

        @pl.when(self.same)
        def _():
            own.wait()
            self.arrival(1 - at.b, 3).wait_recv()

        @pl.when(jnp.logical_not(self.same))
        def _():
            near.wait_send()
            self.arrival(at.b, 4 + at.b).wait_recv()
            self.arrival(1 - at.b, 5 - at.b).wait_recv()

    def pcopy(self, step, dh, device):
        block = self.block(dh)
        return remote(
            block, block, self.psems.at[0, step], self.psems.at[1, step], self.at.near(device)
        )

    def hop(self, which, dh):
        return self.pcopy(which, dh, self.at.turn(which % 2))

    def pstart(self):
        at = self.at
        if at.n == 4:
            self.hop(0, at.dh).start()
            self.hop(1, at.dh).start()
        else:
            for step in range(1, at.n):
                self.pcopy(step, at.dh, lax.rem(at.dh + step, at.n)).start()

    def pforward(self):
        if self.at.n == 4:
            first = self.at.turn(0)
            self.hop(0, first).wait_recv()
            self.pcopy(2, first, self.at.turn(1)).start()

    def pwait(self):
        at = self.at
        if at.n == 4:
            self.hop(0, at.dh).wait_send()
            self.hop(1, at.dh).wait_send()
            self.pcopy(2, at.turn(0), at.turn(1)).wait_send()
            self.hop(1, at.turn(1)).wait_recv()
            self.pcopy(2, at.opposite(), at.turn(1)).wait_recv()
        else:
            for step in range(1, at.n):
                source = lax.rem(at.dh + at.n - step, at.n)
                self.pcopy(step, at.dh, source).wait_send()
                self.pcopy(step, source, source).wait_recv()

    @staticmethod
    def scratch(n):
        return [pltpu.SemaphoreType.DMA((6,)), pltpu.SemaphoreType.DMA((2, n))]


class Scatter:
    def __init__(self, at, grad, out, flip, got, mid, zgot, psems, zsems):
        self.at, self.grad, self.out, self.flip = at, grad, out, flip
        self.got, self.mid, self.zgot = got, mid, zgot
        self.psems, self.zsems = psems, zsems
        self.size = mid.shape[0] // 2
        self.same = at.b == at.th

    @staticmethod
    def scratch(n, rows, columns):
        size = rows // n
        return [
            pltpu.VMEM((n - 1, size, columns), BF16),
            pltpu.VMEM((size, columns), BF16),
        ]

    @staticmethod
    def layer_scratch(n, rows, columns):
        return [
            pltpu.VMEM((2, rows // n // 2, columns), BF16),
            pltpu.SemaphoreType.DMA((2, n)),
            pltpu.SemaphoreType.DMA((6,)),
        ]

    def part(self, dh):
        return self.grad.at[tile(dh, 2 * self.size)]

    def pcopy(self, step, src, device):
        return remote(
            src,
            self.got.at[step],
            self.psems.at[0, step],
            self.psems.at[1, step],
            self.at.near(device),
        )

    def hop(self, index):
        at = self.at
        if index == 2:
            return self.pcopy(2, self.mid, at.turn(1))
        return self.pcopy(index, self.part(at.opposite() if index else at.turn(0)), at.turn(0))

    def pstart(self):
        at = self.at
        if at.n == 4:
            self.hop(1).start()
            self.hop(0).start()
        else:
            for step in range(1, at.n):
                target = lax.rem(at.dh + step, at.n)
                self.pcopy(step - 1, self.part(target), target).start()

    def pforward(self):
        at = self.at
        if at.n == 4:
            self.hop(1).wait()
            total = self.grad[tile(at.turn(1), 2 * self.size), :].astype(F32)
            self.mid[...] = (total + self.got[1].astype(F32)).astype(BF16)
            self.hop(2).start()

    def psum(self):
        at = self.at
        total = self.grad[tile(at.dh, 2 * self.size), :].astype(F32)
        if at.n == 4:
            self.hop(0).wait()
            self.hop(2).wait()
            total = total + self.got[0].astype(F32) + self.got[2].astype(F32)
        else:
            for step in range(1, at.n):
                target = lax.rem(at.dh + step, at.n)
                self.pcopy(step - 1, self.part(target), target).wait()
                total = total + self.got[step - 1].astype(F32)
        self.mid[...] = total.astype(BF16)

    def piece(self, b):
        return self.mid.at[tile(b, self.size)]

    def zcopies(self):
        at, sems = self.at, self.zsems
        dst = self.zgot.at[at.th]
        own = pltpu.make_async_copy(self.piece(at.b), dst, sems.at[0])
        near = remote(self.piece(1 - at.b), dst, sems.at[1], sems.at[4], at.sib)
        first = remote(
            self.piece(at.b), dst, sems.at[2], sems.at[5], (at.dh, at.b, 1 - at.th, at.tl)
        )
        second = remote(
            self.piece(1 - at.b), dst, sems.at[3], sems.at[5], (at.dh, 1 - at.b, 1 - at.th, at.tl)
        )
        return own, near, first, second

    def zstart(self):
        own, near, first, second = self.zcopies()

        @pl.when(self.same)
        def _():
            near.start()
            own.start()

        @pl.when(jnp.logical_not(self.same))
        def _():
            first.start()
            second.start()

    def arrival(self, th, sem):
        return remote(
            self.piece(0), self.zgot.at[th], self.zsems.at[0], self.zsems.at[sem], self.at.sib
        )

    def zsum(self):
        at = self.at
        own, near, first, second = self.zcopies()

        @pl.when(self.same)
        def _():
            near.wait_send()
            own.wait()

        @pl.when(jnp.logical_not(self.same))
        def _():
            first.wait_send()
            second.wait_send()
            self.arrival(at.th, 4).wait_recv()

        self.arrival(1 - at.th, 5).wait_recv()
        total = self.zgot[0].astype(F32) + self.zgot[1].astype(F32)
        if self.flip is None:
            for kind in range(3):
                self.out[kind][...] = total[:, kind * LANES : (kind + 1) * LANES]
        else:
            self.out[...] = total.T if self.flip else total


class Rows:
    def __init__(self, at, count):
        self.at, self.R = at, count // CHUNKS

    def at_(self, chunk, owner):
        return tile(chunk * 4 + owner, self.R)

    def whole(self, chunk):
        return pl.ds(chunk * 4 * self.R, 4 * self.R)

    def own(self, chunk):
        return pl.ds(chunk * self.R, self.R)


class Spread:
    def __init__(self, at, rows, buf, sems):
        self.at, self.rows, self.buf, self.sems = at, rows, buf, sems

    @staticmethod
    def scratch(width):
        return [pltpu.SemaphoreType.DMA((6, CHUNKS))]

    def copy(self, chunk, kind, owner):
        ref = self.buf.at[self.rows.at_(chunk, owner)]
        device = self.at.link if kind == 0 else self.at.sib
        return remote(ref, ref, self.sems.at[kind, chunk], self.sems.at[3 + kind, chunk], device)

    def start(self, chunk):
        self.copy(chunk, 0, self.at.mine).start()
        self.copy(chunk, 1, self.at.mine).start()

    def forward(self, chunk):
        self.copy(chunk, 0, self.at.links).wait_recv()
        self.copy(chunk, 2, self.at.links).start()

    def wait(self, chunk):
        self.copy(chunk, 1, self.at.sibs).wait_recv()
        self.copy(chunk, 2, self.at.diags).wait_recv()

    def finish(self):
        for chunk in range(CHUNKS):
            self.copy(chunk, 0, self.at.mine).wait_send()
            self.copy(chunk, 1, self.at.mine).wait_send()
            self.copy(chunk, 2, self.at.links).wait_send()


class Collect:
    def __init__(self, at, rows, part, sent, got, sent_far, got_far, sems):
        self.at, self.R, self.part = at, rows.R, part
        self.sent, self.got, self.sent_far, self.got_far, self.sems = sent, got, sent_far, got_far, sems

    @staticmethod
    def scratch(count, width):
        R = count // CHUNKS
        return [
            pltpu.VMEM((CHUNKS, 2 * R, width), BF16),
            pltpu.VMEM((CHUNKS, 2 * R, width), BF16),
            pltpu.VMEM((CHUNKS, R, width), BF16),
            pltpu.VMEM((CHUNKS, R, width), BF16),
        ]

    SEMS = pltpu.SemaphoreType.DMA((4, CHUNKS))

    def near(self, chunk):
        return remote(
            self.sent.at[chunk],
            self.got.at[chunk],
            self.sems.at[0, chunk],
            self.sems.at[1, chunk],
            self.at.sib,
        )

    def far(self, chunk):
        return remote(
            self.sent_far.at[chunk],
            self.got_far.at[chunk],
            self.sems.at[2, chunk],
            self.sems.at[3, chunk],
            self.at.link,
        )

    def left(self, ref, chunk):
        halves = [ref[tile(2 * chunk + b, 2 * self.R), :] for b in (self.at.b, 1 - self.at.b)]
        return jnp.concatenate(halves, axis=0)

    def put(self, chunk, span, values):
        self.part[chunk, :, span] = values[: 2 * self.R]
        self.sent[chunk, :, span] = values[2 * self.R :].astype(BF16)

    def start(self, chunk):
        self.near(chunk).start()

    def half(self, chunk, tl):
        mine = self.part[chunk, tile(tl, self.R), :]
        return mine + self.got[chunk, tile(tl, self.R), :].astype(F32)

    def forward(self, chunk):
        self.near(chunk).wait_recv()
        self.sent_far[chunk] = self.half(chunk, 1 - self.at.tl).astype(BF16)
        self.far(chunk).start()

    def take(self, chunk):
        self.far(chunk).wait_recv()
        return self.half(chunk, self.at.tl) + self.got_far[chunk].astype(F32)

    def finish(self):
        for chunk in range(CHUNKS):
            self.near(chunk).wait_send()
            self.far(chunk).wait_send()


class Take:
    def __init__(self, refs):
        self.refs = list(refs)

    def __call__(self, count=None):
        if count is None:
            return self.refs.pop(0)
        return [self.refs.pop(0) for _ in range(count)]


class Local:
    def __init__(self, sems):
        self.sems, self.used = sems, 0

    def start(self, src, dst):
        copy = pltpu.make_async_copy(src, dst, self.sems.at[self.used])
        self.used += 1
        copy.start()
        return copy


def stats(values):
    center = values - jnp.mean(values, axis=-1, keepdims=True)
    inverse = lax.rsqrt(jnp.mean(center * center, axis=-1, keepdims=True) + EPSILON)
    return center * inverse, inverse


def norm(values, gain, shift):
    return stats(values)[0] * gain + shift


def norm_back(upstream, scaled, inverse, gain):
    weighted = upstream * gain
    first_mean = jnp.mean(weighted, axis=-1, keepdims=True)
    second_mean = jnp.mean(weighted * scaled, axis=-1, keepdims=True)
    return inverse * (weighted - first_mean - scaled * second_mean)


def lane():
    return lax.broadcasted_iota(jnp.int32, (1, LANES), 1)


def turned(values, cosines, sines):
    within = lax.rem(lane(), HEAD_DIM)
    former = lax.rem(within, ROT) < ROT // 2
    half = ROT // 2
    moved = jnp.where(former, pltpu.roll(values, LANES - half, 1), pltpu.roll(values, half, 1))
    return values * cosines + moved * sines


def of_head(values, head):
    keep = (lane() // HEAD_DIM) == head % 2
    return jnp.where(keep, values, jnp.zeros_like(values))


def gelu_and_slope(u):
    size = jnp.abs(u) * 0.7071067811865476
    t = 1.0 / (1.0 + 0.3275911 * size)
    bell = jnp.exp(-0.5 * u * u)
    poly = t * (
        0.127414796
        + t * (-0.142248368 + t * (0.7107068705 + t * (-0.7265760135 + t * 0.5307027145)))
    )
    tail = poly * bell
    phi = jnp.where(u < 0, tail, 1.0 - tail)
    return u * phi, phi + u * bell * RSQRT_2PI


def tables(places, cosines, sines, rows):
    row = lax.broadcasted_iota(jnp.int32, (HEAD_DIM, places.shape[1]), 0)
    which = row // ROT
    place = jnp.where(
        which == 0, places[0:1, :], jnp.where(which == 1, places[1:2, :], places[2:3, :])
    )
    step = lax.rem(row, ROT // 2).astype(F32) / (ROT // 2)
    frequency = jnp.where(which < 3, jnp.exp(step * -9.210340371976184), 0.0)
    angle = place * frequency
    sign = jnp.where(lax.rem(row, ROT) < ROT // 2, -1.0, 1.0)
    for table, values in ((cosines, jnp.cos(angle)), (sines, jnp.sin(angle) * sign)):
        turned_values = jnp.concatenate([values, values], axis=0).T
        for k in range(CHUNKS):
            for owner in range(4):
                start = (owner * CHUNKS + k) * rows.R
                table[pl.ds((k * 4 + owner) * rows.R, rows.R), :] = turned_values[
                    start : start + rows.R, :
                ]


def forward_kernel(n, refs):
    take = Take(refs)
    tokens, cotangent, clip_mask, positions = take(4)
    triple_in, triple_bias, exit_in, expand_in, expand_bias, shrink_in = take(6)
    norm_gain, norm_shift, branch_bias = take(3)
    upstream, cosines_out, sines_out, small_out, em_out = take(5)
    outs = [take(15) for _ in range(LAYERS)]
    x, smalls, small, parameters, turned_tokens, turned_cotangent, cosines, sines = take(8)
    exit_turned, shrink_turned, triple_turned, em = take(4)
    weights = [take(4) for _ in range(LAYERS)]
    n1, n2, qp, kp, vp, vt, o, g, slope, lse, ot, part = take(12)
    spread_sems = take(2 * LAYERS)
    one_buffers, two_buffers = take(4), take(4)
    collect_sems = take(2 * LAYERS)
    gather_sems = [[take(2) for _ in range(4)] for _ in range(LAYERS)]
    em_sems, token_sems, small_sems, cotangent_sems, local_sems = take(5)

    at = Place()
    local = Local(local_sems)
    rows = Rows(at, x.shape[0])
    slices = [
        [source.at[l] for source in (triple_turned, exit_turned, expand_in, shrink_turned)]
        for l in range(LAYERS)
    ]
    gathers = [
        [Gather(at, *triple) for triple in zip(slices[l], weights[l], *zip(*gather_sems[l]))]
        for l in range(LAYERS)
    ]
    smalls[...] = jnp.zeros_like(smalls)
    smalls[0:3, :] = positions[...].astype(F32)
    smalls[3:4, :] = jnp.broadcast_to(clip_mask[...].astype(F32), (1, smalls.shape[1]))
    for l in range(LAYERS):
        for kind in range(3):
            width = triple_bias.shape[2]
            columns = slice(kind * width, (kind + 1) * width)
            smalls[4 + l : 5 + l, columns] = triple_bias[kind, l : l + 1, :].astype(F32)
            triple_turned[l, :, columns] = triple_in[l, kind]
        smalls[6 + l : 7 + l, :] = expand_bias[l : l + 1, :].astype(F32)
    swap_small = Swap(at, smalls, small, small_sems)
    swap_tokens = [
        Swap(
            at,
            tokens.at[rows.own(k)],
            turned_tokens.at[rows.own(k)],
            token_sems.at[k],
        )
        for k in range(CHUNKS)
    ]
    swap_cotangent = Swap(at, cotangent, turned_cotangent, cotangent_sems)

    at.barrier()
    gathers[0][0].zstart()
    swap_small.start()
    for swap in swap_tokens:
        swap.start()
    for l in range(LAYERS):
        exit_turned[l] = exit_in[l].T
        shrink_turned[l] = shrink_in[l].T
        for index, source in enumerate((norm_gain, norm_shift, branch_bias)):
            parameters[8 * l + 2 * index : 8 * l + 2 * index + 2, :] = source[l].astype(F32)
    swap_small.wait()
    tables(small, cosines, sines, rows)
    saves = [
        local.start(*pair)
        for pair in ((cosines, cosines_out), (sines, sines_out), (small, small_out))
    ]
    spread_em = Spread(at, rows, em, em_sems)

    def begin(l):
        spread = [Spread(at, rows, buf, spread_sems[2 * l + i]) for i, buf in enumerate((n1, n2))]
        collect = [
            Collect(at, rows, part, *buffers, collect_sems[2 * l + i])
            for i, buffers in enumerate((one_buffers, two_buffers))
        ]
        return spread + collect

    stages = [begin(l) for l in range(LAYERS)]

    def row(l, index):
        return parameters[8 * l + index : 8 * l + index + 1, :]

    def first_norm(l, k):
        n1[rows.at_(k, at.mine), :] = norm(x[rows.own(k), :], row(l, 0), row(l, 2)).astype(BF16)
        stages[l][0].start(k)

    def project(l, k):
        stages[l][0].wait(k)
        whole = rows.whole(k)
        wa = weights[l][0]
        for kind in range(3):
            columns = slice(2 * kind * LANES, 2 * (kind + 1) * LANES)
            bias = small[4 + l : 5 + l, columns]
            both = dot(n1[whole, :], wa[:, columns], NN) + bias
            for pair in range(2):
                t = both[:, pair * LANES : (pair + 1) * LANES]
                if kind < 2:
                    t = turned(t, cosines[whole, :], sines[whole, :])
                if kind == 0:
                    qp[pair, whole, :] = (t * (SCALE * LOG2E)).astype(BF16)
                elif kind == 1:
                    kp[pair, whole, :] = t.astype(BF16)
                else:
                    vp[pair, whole, :] = t.astype(BF16)
                    vt[pl.ds(pair * LANES, LANES), whole] = t.T.astype(BF16)

    def attention(k):
        whole = rows.whole(k)

        def head(h, carry):
            scores = dot(kp[h // 2], of_head(qp[h // 2, whole, :], h), NT)
            highest = jnp.max(scores, axis=0, keepdims=True)
            weights = jnp.exp2(scores - highest)
            total = jnp.sum(weights, axis=0, keepdims=True)
            spans = tile(h, HEAD_DIM)
            ot[spans, :] = dot(vt[spans, :], weights.astype(BF16), NN) / total
            lse[pl.ds(h, 1), whole] = highest + jnp.log2(total)
            return carry

        lax.fori_loop(0, 4, head, 0)
        o[whole, :] = ot[...].T.astype(BF16)

    def leave(l, k):
        wb, collect = weights[l][1], stages[l][2]
        left = collect.left(o, k)

        def columns(j, carry):
            span = tile(j, 256)
            collect.put(k, span, dot(left, wb[span, :], NT))
            return carry

        lax.fori_loop(0, part.shape[2] // 256, columns, 0, unroll=True)
        collect.start(k)

    def second_norm(l, k):
        own = rows.own(k)
        x[own, :] = x[own, :] + (stages[l][2].take(k) + row(l, 4))
        n2[rows.at_(k, at.mine), :] = norm(x[own, :], row(l, 1), row(l, 3)).astype(BF16)
        stages[l][1].start(k)

    def up(l, k):
        whole = rows.whole(k)
        wc = weights[l][2]
        stages[l][1].wait(k)

        def columns(j, carry):
            span = tile(j, 256)
            u = dot(n2[whole, :], wc[:, span], NN) + small[pl.ds(6 + l, 1), span]
            active, grade = gelu_and_slope(u)
            g[whole, span] = active.astype(BF16)
            slope[whole, span] = grade.astype(BF16)
            return carry

        lax.fori_loop(0, wc.shape[1] // 256, columns, 0, unroll=True)

    def down(l, k):
        wd, collect = weights[l][3], stages[l][3]
        left = collect.left(g, k)

        def outputs(j, carry):
            span = tile(j, 256)
            collect.put(k, span, dot(left, wd[span, :], NT))
            return carry

        lax.fori_loop(0, part.shape[2] // 256, outputs, 0, unroll=True)
        collect.start(k)

    def end(l, k):
        own = rows.own(k)
        x[own, :] = x[own, :] + (stages[l][3].take(k) + row(l, 5))
        if l + 1 < LAYERS:
            first_norm(l + 1, k)

    A, B, C, D = range(4)

    def begin_plane(gather):
        gather.zwait()
        gather.pstart()

    begin_plane(gathers[0][A])
    for k in range(CHUNKS):
        swap_tokens[k].wait()
        x[rows.own(k), :] = turned_tokens[rows.own(k), :].astype(F32)
        first_norm(0, k)
    for gather in gathers[0][B:]:
        gather.zstart()
    gathers[0][A].pforward()
    pending = []
    for l in range(LAYERS):
        hidden_out, middle_out, *full_outs = outs[l][:6]
        n1_out, n2_out, qp_out, kp_out, vp_out, o_out, g_out, slope_out, lse_out = outs[l][6:]
        spread_one, spread_two, collect_one, collect_two = stages[l]
        now = gathers[l]
        following = gathers[l + 1] if l + 1 < LAYERS else None
        save_x = local.start(x, hidden_out)
        for k in range(CHUNKS):
            spread_one.forward(k)
        now[A].pwait()
        if l == 0:
            begin_plane(now[B])
        else:
            now[B].pforward()
            begin_plane(now[C])
        for save in pending:
            save.wait()
        for k in range(CHUNKS):
            project(l, k)
        spread_one.finish()
        save_n1 = local.start(n1, n1_out)
        pending = [
            local.start(*pair) for pair in ((qp, qp_out), (kp, kp_out), (vp, vp_out))
        ]
        if l == 0:
            now[B].pforward()
        attention(0)
        now[B].pwait()
        leave(l, 0)
        if l == 0:
            begin_plane(now[C])
            following[A].zstart()
            following[B].zstart()
        attention(1)
        collect_one.forward(0)
        leave(l, 1)
        if l:
            begin_plane(now[D])
            now[C].pforward()
        save_x.wait()
        attention(2)
        collect_one.forward(1)
        leave(l, 2)
        second_norm(l, 0)
        attention(3)
        collect_one.forward(2)
        leave(l, 3)
        if l == 0:
            now[C].pforward()
            begin_plane(now[D])
            following[C].zstart()
        if not following:
            swap_cotangent.wait()
            upstream[...] = turned_cotangent[...].astype(F32) * small[3:4, :]
            for k in range(CHUNKS):
                em[rows.at_(k, at.mine), :] = upstream[rows.own(k), :].astype(BF16)
        second_norm(l, 1)
        collect_one.forward(3)
        second_norm(l, 2)
        second_norm(l, 3)
        if not following:
            for k in range(CHUNKS):
                spread_em.start(k)
        save_x = local.start(x, middle_out)
        pending += [local.start(o, o_out), local.start(lse, lse_out)]
        save_n1.wait()
        spread_two.forward(0)
        now[C].pwait()
        for k in range(CHUNKS):
            up(l, k)
            if k == 1 and following:
                begin_plane(following[A])
            if k == 1 and not following:
                now[D].pforward()
            if k + 1 < CHUNKS:
                spread_two.forward(k + 1)
        if following:
            now[D].pforward()
        else:
            for k in range(CHUNKS):
                spread_em.forward(k)
        pending += [local.start(*pair) for pair in ((n2, n2_out), (g, g_out), (slope, slope_out))]
        save_x.wait()
        spread_two.finish()
        now[D].pwait()
        pending += [local.start(*pair) for pair in zip(weights[l], full_outs)]
        if not following:
            collect_one.finish()
            for k in range(CHUNKS):
                spread_em.wait(k)
            spread_em.finish()
            pending.append(local.start(em, em_out))
            continue
        for k in range(CHUNKS):
            down(l, k)
            if k:
                collect_two.forward(k - 1)
            if k == 0:
                following[D].zstart()
                swap_cotangent.start()
            if k == 1:
                begin_plane(following[B])
            if k > 1:
                end(l, k - 2)
        collect_two.forward(CHUNKS - 1)
        end(l, CHUNKS - 2)
        following[A].pforward()
        end(l, CHUNKS - 1)
        collect_one.finish()
        collect_two.finish()
    for save in saves + pending:
        save.wait()


def backward_kernel(n, refs):
    take = Take(refs)
    upstream, gain_in, bias_in, small, em_in = take(5)
    ins = [take(15) for _ in range(LAYERS)]
    cosines_in, sines_in = take(2)
    mixed_out, grad_out, triple_out, triple_bias_out, exit_out, expand_out = take(6)
    expand_bias_out, shrink_out, gain_out, shift_out, bias_out = take(5)
    e, xs, wa, wb, wc, wd = take(6)
    em, ea, n2, qp, kp, vp, kt, o, g, du, lse = take(11)
    dk, dv, dqt, do, part, gd, ge, vectors, cosines, sines = take(10)
    dt, gt = take(2), take(2)
    mixed, turned_mixed, low_grad_own, turned_grad = take(4)
    part_last, last_got, last_sems = take(), take(2), take()
    spread_sems = take(2 * LAYERS)
    one_buffers, two_buffers = take(4), take(4)
    collect_sems = take(2 * LAYERS)
    scatter_buffers = [take(2) for _ in range(5)]
    scatter_layers = [[take(3) for _ in range(5)] for _ in range(LAYERS)]
    mixed_sems, grad_sems = take(2)
    plane, column, plane_sems, column_sems = take(4)
    local_sems = take()

    at = Place()
    local = Local(local_sems)
    rows = Rows(at, e.shape[0])

    def load(l, name):
        where = {
            "hidden": (0, xs),
            "middle": (1, xs),
            "a": (2, wa),
            "b": (3, wb),
            "c": (4, wc),
            "d": (5, wd),
            "n1": (6, g),
            "n2": (7, n2),
            "q": (8, qp),
            "k": (9, kp),
            "v": (10, vp),
            "o": (11, o),
            "g": (12, g),
            "slope": (13, du),
            "lse": (14, lse),
        }
        index, target = where[name]
        loads[(l, name)] = local.start(ins[l][index], target)

    def ready(l, *names):
        for name in names:
            loads.pop((l, name)).wait()

    loads = {}
    top = LAYERS - 1
    load_em = local.start(em_in, em)
    load_e = local.start(upstream, e)
    for name in ("d", "slope", "c", "middle", "g", "n2", "b", "q", "k", "v", "o", "lse", "a"):
        load(top, name)
    load_tables = [local.start(cosines_in, cosines), local.start(sines_in, sines)]

    cubes = [(db, dth, dtl) for db in range(2) for dth in range(2) for dtl in range(2)][1:]

    def flipped(flips):
        return [jnp.abs(coordinate - flip) for coordinate, flip in zip(at.me[1:], flips)]

    barrier = pltpu.get_barrier_semaphore()
    greeted = [(at.dh, *flipped(flips)) for flips in cubes]
    greeted += [at.peer(step) for step in range(1, n)]
    for device in greeted:
        pl.semaphore_signal(barrier, inc=1, device_id=device, device_id_type=MESH)
    pl.semaphore_wait(barrier, len(greeted))

    spreads = [
        [Spread(at, rows, buf, spread_sems[2 * l + i]) for i, buf in enumerate((em, ea))]
        for l in range(LAYERS)
    ]
    collects = [
        [
            Collect(at, rows, part, *buffers, collect_sems[2 * l + i])
            for i, buffers in enumerate((one_buffers, two_buffers))
        ]
        for l in range(LAYERS)
    ]
    def triple_columns(l, pair):
        return [triple_out.at[l, kind, :, pl.ds(pair * LANES, LANES)] for kind in range(3)]

    def pieces(l):
        return (
            (gt[0], triple_columns(l, 0), None),
            (gt[1], triple_columns(l, 1), None),
            (ge, exit_out.at[l], True),
            (wd, expand_out.at[l], False),
            (gd, shrink_out.at[l], True),
        )

    scatters = [
        [
            Scatter(at, *piece, *buffers, *own)
            for piece, buffers, own in zip(pieces(l), scatter_buffers, scatter_layers[l])
        ]
        for l in range(LAYERS)
    ]
    collect_last = Collect(
        at, rows, part_last, two_buffers[0], last_got[0], two_buffers[2], last_got[1], last_sems
    )
    swap_mixed = Swap(at, mixed, turned_mixed, mixed_sems)
    swap_grads = [
        Swap(
            at, low_grad_own.at[rows.own(k)], turned_grad.at[rows.own(k)], grad_sems.at[k]
        )
        for k in range(CHUNKS)
    ]
    vectors[...] = jnp.zeros_like(vectors)

    def add(l, row, values):
        vectors[8 * l + row : 8 * l + row + 1, : values.shape[1]] += jnp.sum(
            values.astype(F32), axis=0, keepdims=True
        )

    def weight_grad(left, right, out):
        def block(j, carry):
            span = tile(j, 256)
            out[span, :] = dot(left[:, span], right[...], TN).astype(BF16)
            return carry

        lax.fori_loop(0, left.shape[1] // 256, block, 0, unroll=True)

    def send_branch(l, k):
        low = e[rows.own(k), :].astype(BF16)
        em[rows.at_(k, at.mine), :] = low
        spreads[l][0].start(k)
        add(l, 5, low)

    def shrink_back(l, k):
        if l < top:
            spreads[l][0].forward(k)
            spreads[l][0].wait(k)
        whole = rows.whole(k)
        collect = collects[l][0]

        def columns(j, carry):
            span = tile(j, 256)
            active_grad = dot(em[whole, :], wd[:, span], NN)
            du[whole, span] = (active_grad * du[whole, span].astype(F32)).astype(BF16)
            return carry

        lax.fori_loop(0, wd.shape[1] // 256, columns, 0, unroll=True)
        add(l, 6, du[whole, :])
        left = collect.left(du, k)

        def outputs(j, carry):
            span = tile(j, 256)
            collect.put(k, span, dot(left, wc[span, :], NT))
            return carry

        lax.fori_loop(0, part.shape[2] // 256, outputs, 0, unroll=True)
        collect.start(k)

    def norm_step(l, k, which):
        own = rows.own(k)
        scaled, inverse = stats(xs[own, :])
        grads = collects[l][1 - which].take(k)
        add(l, which, grads * scaled)
        add(l, 2 + which, grads)
        gain = gain_in[l, which : which + 1, :].astype(F32)
        e[own, :] = e[own, :] + norm_back(grads, scaled, inverse, gain)

    def middle_step(l, k):
        norm_step(l, k, 1)
        low = e[rows.own(k), :].astype(BF16)
        ea[rows.at_(k, at.mine), :] = low
        spreads[l][1].start(k)
        add(l, 4, low)

    def first_step(l, k):
        norm_step(l, k, 0)
        if l:
            send_branch(l - 1, k)
        else:
            low_grad_own[rows.own(k), :] = e[rows.own(k), :].astype(BF16)
            swap_grads[k].start()

    def branch_last(k):
        left = collect_last.left(g, k)

        def outputs(j, carry):
            span = tile(j, 256)
            collect_last.put(k, span, dot(left, wd[span, :], NT))
            return carry

        lax.fori_loop(0, part.shape[2] // 256, outputs, 0, unroll=True)
        collect_last.start(k)

    def end_last(k):
        own = rows.own(k)
        bias = bias_in[top, 1:2, :].astype(F32)
        hidden = xs[own, :] + (collect_last.take(k) + bias)
        mixed[own, :] = (hidden * small[3:4, :]).astype(BF16)

    def attention_back(l, pair, k):
        whole = rows.whole(k)
        if pair == 0:
            spreads[l][1].wait(k)
            do[whole, :] = dot(ea[whole, :], wb[...], NN).astype(BF16)
        lanes = slice(pair * LANES, (pair + 1) * LANES)
        dop = do[whole, lanes]
        product = dop.astype(F32) * o[whole, lanes].astype(F32)
        high = product.astype(BF16)
        rest = (product - high.astype(F32)).astype(BF16)
        for half in range(2):
            h = 2 * pair + half
            pick = jnp.broadcast_to(((lane() // HEAD_DIM) == half).astype(BF16), (8, LANES))
            center = dot(pick, high, NT) + dot(pick, rest, NT)
            qh = of_head(qp[pair, whole, :], half)
            doh = of_head(dop, half)
            scores = dot(kp[pair], qh, NT)
            chances = jnp.exp2(scores - lse[h : h + 1, whole])
            chance_grad = dot(vp[pair], doh, NT)
            score_grad = (chances * (chance_grad - center[0:1, :])).astype(BF16)
            dv[pair] += dot(chances.astype(BF16), doh, NN)
            dk[pair] += dot(score_grad, qh, NN)
            spans = slice(h * HEAD_DIM, (h + 1) * HEAD_DIM)
            dqt[half * HEAD_DIM : (half + 1) * HEAD_DIM, :] = dot(kt[spans, :], score_grad, NN)
        dq = dqt[...].T * SCALE
        dt[pair][whole, :LANES] = turned(dq, cosines[whole, :], -sines[whole, :]).astype(BF16)

    def pair_done(l, pair):
        dt[pair][:, LANES : 2 * LANES] = turned(
            dk[pair] * LN2, cosines[...], -sines[...]
        ).astype(BF16)
        dt[pair][:, 2 * LANES :] = dv[pair].astype(BF16)
        weight_grad(g, dt[pair], gt[pair])
        scatters[l][pair].pstart()

    def triple_sum(l):
        width = 2 * LANES
        for pair in range(2):
            sums = jnp.sum(dt[pair][...].astype(F32), axis=0, keepdims=True)
            for kind in range(3):
                start = kind * width + pair * LANES
                vectors[8 * l + 7 : 8 * l + 8, start : start + LANES] = sums[
                    :, kind * LANES : (kind + 1) * LANES
                ]

    def projection_back(l, k):
        collect = collects[l][1]
        left = jnp.concatenate(
            [
                collect.left(dt[pair], k)[:, kind * LANES : (kind + 1) * LANES]
                for kind in range(3)
                for pair in range(2)
            ],
            axis=1,
        )

        def outputs(j, carry):
            span = tile(j, 256)
            collect.put(k, span, dot(left, wa[span, :], NT))
            return carry

        lax.fori_loop(0, part.shape[2] // 256, outputs, 0, unroll=True)
        collect.start(k)

    load_e.wait()
    load_em.wait()
    for k in range(CHUNKS):
        add(top, 5, em[rows.at_(k, at.mine), :])
    for l in reversed(range(LAYERS)):
        spread_one, spread_two = spreads[l]
        collect_one, collect_two = collects[l]
        st0, st1, se, sc, sd = scatters[l]
        previous = scatters[l + 1] if l < top else None
        ready(l, "d", "slope", "c", "middle")
        for k in range(CHUNKS):
            shrink_back(l, k)
            if k:
                collect_one.forward(k - 1)
            if k > 1:
                middle_step(l, k - 2)
        collect_one.forward(CHUNKS - 1)
        if previous:
            spread_one.finish()
            previous[1].psum()
        ready(l, "g")
        if l == top:
            branch_last(0)
            branch_last(1)
        weight_grad(em, g, gd)
        sd.pstart()
        middle_step(l, CHUNKS - 2)
        middle_step(l, CHUNKS - 1)
        if l == top:
            branch_last(2)
            branch_last(3)
        else:
            load(l, "hidden")
        load(l, "n1")
        ready(l, "n2")
        weight_grad(n2, du, wd)
        sc.pstart()
        if l:
            load(l - 1, "slope")
            load(l - 1, "c")
            load(l - 1, "n2")
        ready(l, "b", "q", "k", "v", "o", "lse")
        for pair in range(2):
            kt[pl.ds(pair * LANES, LANES), :] = kp[pair].astype(F32).T.astype(BF16)
        dk[...] = jnp.zeros_like(dk)
        dv[...] = jnp.zeros_like(dv)
        if l == top:
            for copy in load_tables:
                copy.wait()
        spread_two.forward(0)
        spread_two.forward(1)
        attention_back(l, 0, 0)
        spread_two.forward(2)
        spread_two.forward(3)
        sd.pforward()
        if l == top:
            collect_last.forward(0)
            collect_last.forward(1)
        else:
            previous[1].zstart()
        attention_back(l, 0, 1)
        if l == top:
            collect_last.forward(2)
            collect_last.forward(3)
        sc.pforward()
        attention_back(l, 0, 2)
        sd.psum()
        sd.zstart()
        attention_back(l, 0, 3)
        spread_two.finish()
        weight_grad(ea, o, ge)
        se.pstart()
        ready(l, "n1")
        pair_done(l, 0)
        sc.psum()
        sc.zstart()
        attention_back(l, 1, 0)
        if l == top:
            for k in range(CHUNKS):
                end_last(k)
            load(l, "hidden")
            swap_mixed.start()
        else:
            previous[1].zsum()
        attention_back(l, 1, 1)
        se.pforward()
        st0.pforward()
        attention_back(l, 1, 2)
        se.psum()
        se.zstart()
        attention_back(l, 1, 3)
        st0.psum()
        st0.zstart()
        ready(l, "a")
        if l == top:
            collect_last.finish()
        pair_done(l, 1)
        for k in range(CHUNKS):
            projection_back(l, k)
            if k:
                collect_two.forward(k - 1)
        collect_two.forward(CHUNKS - 1)
        triple_sum(l)
        ready(l, "hidden")
        if l:
            for name in ("d", "g", "b", "q", "k", "v", "o", "lse", "a"):
                load(l - 1, name)
        collect_one.finish()
        sd.zsum()
        first_step(l, 0)
        first_step(l, 1)
        st1.pforward()
        first_step(l, 2)
        first_step(l, 3)
        if l:
            load(l - 1, "middle")
        collect_two.finish()
        for scatter in (sc, se, st0):
            scatter.zsum()

    last = scatters[0][1]
    plane[at.dh] = vectors[...]

    def plane_copy(step, slot):
        ref = plane.at[slot]
        return remote(ref, ref, plane_sems.at[0, step], plane_sems.at[1, step], at.peer(step))

    for step in range(1, n):
        plane_copy(step, at.dh).start()
    last.psum()
    last.zstart()
    for step in range(1, n):
        plane_copy(step, at.dh).wait_send()
        plane_copy(step, lax.rem(at.dh + n - step, n)).wait_recv()
    total = plane[0]
    for index in range(1, n):
        total = total + plane[index]

    def slot(b, th, tl):
        return 4 * b + 2 * th + tl

    mine = slot(*at.me[1:])
    column[mine] = total

    def column_copy(index, flips, where):
        ref = column.at[where]
        device = (at.dh, *flipped(flips))
        return remote(ref, ref, column_sems.at[0, index], column_sems.at[1, index], device)

    for index, flips in enumerate(cubes):
        column_copy(index, flips, mine).start()
    swap_mixed.wait()
    save_mixed = local.start(turned_mixed, mixed_out)
    for index, flips in enumerate(cubes):
        column_copy(index, flips, mine).wait_send()
        column_copy(index, flips, slot(*flipped(flips))).wait_recv()
    total = column[0]
    for index in range(1, 8):
        total = total + column[index]
    own = column[slot(at.th, 0, at.tl)] + column[slot(at.th, 1, at.tl)]
    width = triple_bias_out.shape[2]
    for l in range(LAYERS):
        gain_out[l] = total[8 * l : 8 * l + 2, :]
        shift_out[l] = total[8 * l + 2 : 8 * l + 4, :]
        bias_out[l] = total[8 * l + 4 : 8 * l + 6, :]
        expand_bias_out[l : l + 1, :] = own[8 * l + 6 : 8 * l + 7, :]
        for kind in range(3):
            triple_bias_out[kind, l : l + 1, :] = own[
                8 * l + 7 : 8 * l + 8, kind * width : (kind + 1) * width
            ]
    for k in range(CHUNKS):
        swap_grads[k].wait()
    save_grad = local.start(turned_grad, grad_out)
    last.zsum()
    save_mixed.wait()
    save_grad.wait()


def finish_kernel(*refs):
    half = len(refs) // 2
    for source, target in zip(refs[:half], refs[half:]):
        if len(source.shape) < len(target.shape):
            target[:, 0, :] = source[...].astype(F32)
        else:
            target[...] = source[...]


def call(body, args, vmem_in, outs, vmem_out, scratch, collective_id, name, flops=0):
    def kernel(*refs):
        body(refs)

    in_specs = [VMEM if index in vmem_in else ANY for index in range(len(args))]
    out_specs = [VMEM if index in vmem_out else ANY for index in range(len(outs))]
    return pl.pallas_call(
        kernel,
        out_shape=outs,
        in_specs=in_specs,
        out_specs=out_specs,
        scratch_shapes=scratch,
        compiler_params=pltpu.CompilerParams(
            collective_id=collective_id, has_side_effects=True, vmem_limit_bytes=VMEM_LIMIT
        ),
        name=name,
    )(*args)


def shards(
    n,
    tokens,
    cotangent,
    clip_mask,
    positions,
    triple_weight,
    triple_bias,
    exit_weight,
    expand_weight,
    expand_bias,
    shrink_weight,
    norm_gain,
    norm_shift,
    branch_bias,
):
    count, _, depth = tokens.shape
    seq = 4 * count
    size = triple_weight.shape[1]
    local = triple_weight.shape[3]
    inner = expand_weight.shape[2]
    wide = 3 * local
    pairs = local // LANES
    R = count // CHUNKS
    V, DMA, shape = pltpu.VMEM, pltpu.SemaphoreType.DMA, jax.ShapeDtypeStruct
    wides = (wide, local, inner, inner)
    pair_shape = (pairs, seq, LANES)
    args = [
        tokens[:, 0, :],
        cotangent[:, 0, :],
        clip_mask[:, None],
        positions[:, 0, :],
        triple_weight.transpose(0, 2, 1, 3),
        triple_bias.transpose(1, 0, 2),
        exit_weight,
        expand_weight,
        expand_bias,
        shrink_weight,
        norm_gain,
        norm_shift,
        branch_bias,
    ]
    outs = [
        shape((count, depth), F32),
        shape((seq, LANES), F32),
        shape((seq, LANES), F32),
        shape((8, depth), F32),
        shape((seq, depth), BF16),
    ]
    for _ in range(LAYERS):
        outs += [shape((count, depth), F32)] * 2
        outs += [shape((depth, width), BF16) for width in wides]
        outs += [shape((seq, depth), BF16)] * 2
        outs += [shape(pair_shape, BF16)] * 3
        outs += [shape((seq, local), BF16)]
        outs += [shape((seq, inner), BF16)] * 2
        outs += [shape((8, seq), F32)]
    scratch = [
        V((count, depth), F32),
        V((8, depth), F32),
        V((8, depth), F32),
        V((8 * LAYERS, depth), F32),
        V((count, depth), BF16),
        V((count, depth), BF16),
        V((seq, LANES), F32),
        V((seq, LANES), F32),
        V((LAYERS, size, local), BF16),
        V((LAYERS, size, inner), BF16),
        V((LAYERS, size, wide), BF16),
        V((seq, depth), BF16),
    ]
    for _ in range(LAYERS):
        scratch += [V((depth, width), BF16) for width in wides]
    scratch += [V((seq, depth), BF16)] * 2
    scratch += [V(pair_shape, BF16)] * 3
    scratch += [V((local, seq), BF16), V((seq, local), BF16)]
    scratch += [V((seq, inner), BF16)] * 2
    scratch += [V((8, seq), F32), V((local, 4 * R), F32), V((CHUNKS, 2 * R, depth), F32)]
    scratch += Spread.scratch(depth) * (2 * LAYERS)
    scratch += Collect.scratch(count, depth) * 2
    scratch += [Collect.SEMS] * (2 * LAYERS)
    scratch += Gather.scratch(n) * (4 * LAYERS)
    scratch += Spread.scratch(depth)
    scratch += [DMA((CHUNKS, 3)), DMA((3,)), DMA((3,)), DMA((48,))]
    results = call(
        functools.partial(forward_kernel, n),
        args,
        tuple(range(len(args))),
        outs,
        (0,),
        scratch,
        1,
        "forward",
    )
    upstream, cosines, sines, small, em = results[:5]
    args = [upstream, norm_gain, branch_bias, small, em, *results[5:], cosines, sines]
    outs = [
        shape((count, depth), BF16),
        shape((count, depth), BF16),
        shape((LAYERS, 3, size, local), F32),
        shape((3, LAYERS, local), F32),
        shape(exit_weight.shape, F32),
        shape(expand_weight.shape, F32),
        shape(expand_bias.shape, F32),
        shape(shrink_weight.shape, F32),
        shape(norm_gain.shape, F32),
        shape(norm_shift.shape, F32),
        shape(branch_bias.shape, F32),
    ]
    scratch = [V((count, depth), F32)] * 2
    scratch += [V((depth, width), BF16) for width in wides]
    scratch += [V((seq, depth), BF16)] * 3
    scratch += [V(pair_shape, BF16)] * 3
    scratch += [V((local, seq), BF16), V((seq, local), BF16)]
    scratch += [V((seq, inner), BF16)] * 2
    scratch += [V((8, seq), F32)]
    scratch += [V(pair_shape, F32)] * 2
    scratch += [V((LANES, 4 * R), F32), V((seq, local), BF16), V((CHUNKS, 2 * R, depth), F32)]
    scratch += [V((depth, inner), BF16), V((depth, local), BF16)]
    scratch += [V((8 * LAYERS, depth), F32), V((seq, LANES), F32), V((seq, LANES), F32)]
    scratch += [V((seq, 3 * LANES), BF16)] * 2 + [V((depth, 3 * LANES), BF16)] * 2
    scratch += [V((count, depth), BF16)] * 4
    scratch += [V((CHUNKS, 2 * R, depth), F32)] + Collect.scratch(count, depth)[1::2] + [Collect.SEMS]
    scratch += Spread.scratch(depth) * (2 * LAYERS)
    scratch += Collect.scratch(count, depth) * 2
    scratch += [Collect.SEMS] * (2 * LAYERS)
    widths = (3 * LANES, 3 * LANES, local, inner, inner)
    for width in widths:
        scratch += Scatter.scratch(n, depth, width)
    for _ in range(LAYERS):
        for width in widths:
            scratch += Scatter.layer_scratch(n, depth, width)
    scratch += [DMA((3,)), DMA((CHUNKS, 3))]
    scratch += [V((n, 8 * LAYERS, depth), F32), V((8, 8 * LAYERS, depth), F32)]
    scratch += [DMA((2, n)), DMA((2, 7)), DMA((48,))]
    results = call(
        functools.partial(backward_kernel, n),
        args,
        (1, 2, 3),
        outs,
        tuple(range(2, len(outs))),
        scratch,
        2,
        "backward",
    )
    outs = [shape((count, 1, depth), F32)] * 2 + [shape(r.shape, F32) for r in results[2:]]
    mixed, grad, triple_total, bias_total, *others = pl.pallas_call(
        finish_kernel, out_shape=outs, name="finish"
    )(*results)
    return (
        mixed,
        grad,
        triple_total.transpose(0, 2, 1, 3),
        bias_total.transpose(1, 0, 2),
        *others,
    )


def solution(mesh):
    n = mesh.shape["dp"] // 2
    fine = jax.sharding.Mesh(
        mesh.devices.reshape(n, 2, mesh.shape["tensor"] // 2, 2), ("dh", "b", "th", "tl")
    )
    dp, tensor = ("dh", "b"), ("th", "tl")
    return jax.shard_map(
        functools.partial(shards, n),
        mesh=fine,
        in_specs=(
            P(tensor, dp, None),
            P(tensor, dp, None),
            P(dp),
            P(None, dp, None),
            P(None, dp, None, tensor),
            P(None, None, tensor),
            P(None, tensor, dp),
            P(None, dp, tensor),
            P(None, tensor),
            P(None, tensor, dp),
            P(),
            P(),
            P(),
        ),
        out_specs=(
            P(tensor, dp, None),
            P(tensor, dp, None),
            P(None, dp, None, tensor),
            P(None, None, tensor),
            P(None, tensor, dp),
            P(None, dp, tensor),
            P(None, tensor),
            P(None, tensor, dp),
            P(),
            P(),
            P(),
        ),
        check_vma=False,
    )
```

```python
import functools

import jax
import jax.numpy as jnp
from jax import lax
from jax.experimental import pallas as pl
from jax.experimental.pallas import tpu as pltpu
from jax.sharding import PartitionSpec as P

HEAD_DIM = 64
ROT = 20
LAYERS = 2
CHUNKS = 4
LANES = 128
EPSILON = 1e-06
LOG2E = 1.4426950408889634
LN2 = 0.6931471805599453
SCALE = HEAD_DIM ** (-0.5)
RSQRT_2PI = 0.3989422804014327
F32, BF16 = jnp.float32, jnp.bfloat16
NN = (((1,), (0,)), ((), ()))
NT = (((1,), (1,)), ((), ()))
TN = (((0,), (0,)), ((), ()))
MESH = pl.DeviceIdType.MESH
ANY = pl.BlockSpec(memory_space=pl.ANY)
VMEM = pl.BlockSpec(memory_space=pltpu.VMEM)
VMEM_LIMIT = 60 * 2**20


def dot(left, right, dims):
    return lax.dot_general(left, right, dims, preferred_element_type=F32)


def tile(index, size):
    return pl.ds(pl.multiple_of(index * size, size), size)


class Place:
    def __init__(self):
        self.dh, self.b, self.th, self.tl = [lax.axis_index(a) for a in ("dh", "b", "th", "tl")]
        self.n = lax.axis_size("dh")
        self.me = (self.dh, self.b, self.th, self.tl)
        self.sib = (self.dh, 1 - self.b, self.th, self.tl)
        self.link = (self.dh, self.b, self.th, 1 - self.tl)
        self.other = (self.dh, self.th, self.b, self.tl)
        self.mine = 2 * self.b + self.tl
        self.links = 2 * self.b + 1 - self.tl
        self.sibs = 2 * (1 - self.b) + self.tl
        self.diags = 2 * (1 - self.b) + 1 - self.tl

    def turn(self, which):
        y, x = self.dh // 2, lax.rem(self.dh, 2)
        across, along = 2 * y + 1 - x, 2 * (1 - y) + x
        first = self.b if which else 1 - self.b
        return first * across + (1 - first) * along

    def opposite(self):
        y, x = self.dh // 2, lax.rem(self.dh, 2)
        return 2 * (1 - y) + 1 - x

    def near(self, dh):
        return (dh, self.b, self.th, self.tl)

    def peer(self, step):
        return (lax.rem(self.dh + step, self.n), self.b, self.th, self.tl)

    def barrier(self):
        sem = pltpu.get_barrier_semaphore()
        greeted = [
            self.sib,
            self.link,
            (self.dh, self.b, 1 - self.th, self.tl),
            (self.dh, 1 - self.b, 1 - self.th, self.tl),
        ] + [self.peer(step) for step in range(1, self.n)]
        for device in greeted:
            pl.semaphore_signal(sem, inc=1, device_id=device, device_id_type=MESH)
        pl.semaphore_wait(sem, len(greeted))


def remote(src, dst, send, recv, device):
    return pltpu.make_async_remote_copy(
        src_ref=src, dst_ref=dst, send_sem=send, recv_sem=recv, device_id=device, device_id_type=MESH
    )


class Swap:
    def __init__(self, at, src, dst, sems):
        self.same = at.b == at.th
        self.far = remote(src, dst, sems.at[0], sems.at[1], at.other)
        self.near = pltpu.make_async_copy(src, dst, sems.at[2])

    def start(self):
        pl.when(self.same)(self.near.start)
        pl.when(jnp.logical_not(self.same))(self.far.start)

    def wait(self):
        pl.when(self.same)(self.near.wait)
        pl.when(jnp.logical_not(self.same))(self.far.wait)


class Gather:
    def __init__(self, at, src, full, zsems, psems):
        self.at, self.src, self.full = at, src, full
        self.zsems, self.psems = zsems, psems
        self.size = src.shape[0]
        self.same = at.b == at.th

    def slot(self, b):
        return self.full.at[tile(self.at.dh * 2 + b, self.size)]

    def block(self, dh):
        return self.full.at[tile(dh, 2 * self.size)]

    def zcopies(self):
        at = self.at
        dst = self.slot(at.b)
        far = remote(
            self.src,
            dst,
            self.zsems.at[0],
            self.zsems.at[4 + at.b],
            (at.dh, at.th, 1 - at.th, at.tl),
        )
        near = remote(self.src, dst, self.zsems.at[1], self.zsems.at[3], at.sib)
        own = pltpu.make_async_copy(self.src, dst, self.zsems.at[2])
        return far, near, own

    def zstart(self):
        far, near, own = self.zcopies()
        far.start()
        pl.when(self.same)(own.start)
        pl.when(jnp.logical_not(self.same))(near.start)

    def arrival(self, b, sem):
        return remote(self.src, self.slot(b), self.zsems.at[0], self.zsems.at[sem], self.at.sib)

    def zwait(self):
        at = self.at
        far, near, own = self.zcopies()
        far.wait_send()

        @pl.when(self.same)
        def _():
            own.wait()
            self.arrival(1 - at.b, 3).wait_recv()

        @pl.when(jnp.logical_not(self.same))
        def _():
            near.wait_send()
            self.arrival(at.b, 4 + at.b).wait_recv()
            self.arrival(1 - at.b, 5 - at.b).wait_recv()

    def pcopy(self, step, dh, device):
        block = self.block(dh)
        return remote(
            block, block, self.psems.at[0, step], self.psems.at[1, step], self.at.near(device)
        )

    def hop(self, which, dh):
        return self.pcopy(which, dh, self.at.turn(which % 2))

    def pstart(self):
        at = self.at
        if at.n == 4:
            self.hop(0, at.dh).start()
            self.hop(1, at.dh).start()
        else:
            for step in range(1, at.n):
                self.pcopy(step, at.dh, lax.rem(at.dh + step, at.n)).start()

    def pforward(self):
        if self.at.n == 4:
            first = self.at.turn(0)
            self.hop(0, first).wait_recv()
            self.pcopy(2, first, self.at.turn(1)).start()

    def pwait(self):
        at = self.at
        if at.n == 4:
            self.hop(0, at.dh).wait_send()
            self.hop(1, at.dh).wait_send()
            self.pcopy(2, at.turn(0), at.turn(1)).wait_send()
            self.hop(1, at.turn(1)).wait_recv()
            self.pcopy(2, at.opposite(), at.turn(1)).wait_recv()
        else:
            for step in range(1, at.n):
                source = lax.rem(at.dh + at.n - step, at.n)
                self.pcopy(step, at.dh, source).wait_send()
                self.pcopy(step, source, source).wait_recv()

    @staticmethod
    def scratch(n):
        return [pltpu.SemaphoreType.DMA((6,)), pltpu.SemaphoreType.DMA((2, n))]


class Scatter:
    def __init__(self, at, grad, out, flip, got, mid, zgot, psems, zsems):
        self.at, self.grad, self.out, self.flip = at, grad, out, flip
        self.got, self.mid, self.zgot = got, mid, zgot
        self.psems, self.zsems = psems, zsems
        self.size = mid.shape[0] // 2
        self.same = at.b == at.th

    @staticmethod
    def scratch(n, rows, columns):
        size = rows // n
        return [
            pltpu.VMEM((n - 1, size, columns), BF16),
            pltpu.VMEM((size, columns), BF16),
        ]

    @staticmethod
    def layer_scratch(n, rows, columns):
        return [
            pltpu.VMEM((2, rows // n // 2, columns), BF16),
            pltpu.SemaphoreType.DMA((2, n)),
            pltpu.SemaphoreType.DMA((6,)),
        ]

    def part(self, dh):
        return self.grad.at[tile(dh, 2 * self.size)]

    def pcopy(self, step, src, device):
        return remote(
            src,
            self.got.at[step],
            self.psems.at[0, step],
            self.psems.at[1, step],
            self.at.near(device),
        )

    def hop(self, index):
        at = self.at
        if index == 2:
            return self.pcopy(2, self.mid, at.turn(1))
        return self.pcopy(index, self.part(at.opposite() if index else at.turn(0)), at.turn(0))

    def pstart(self):
        at = self.at
        if at.n == 4:
            self.hop(1).start()
            self.hop(0).start()
        else:
            for step in range(1, at.n):
                target = lax.rem(at.dh + step, at.n)
                self.pcopy(step - 1, self.part(target), target).start()

    def pforward(self):
        at = self.at
        if at.n == 4:
            self.hop(1).wait()
            total = self.grad[tile(at.turn(1), 2 * self.size), :].astype(F32)
            self.mid[...] = (total + self.got[1].astype(F32)).astype(BF16)
            self.hop(2).start()

    def psum(self):
        at = self.at
        total = self.grad[tile(at.dh, 2 * self.size), :].astype(F32)
        if at.n == 4:
            self.hop(0).wait()
            self.hop(2).wait()
            total = total + self.got[0].astype(F32) + self.got[2].astype(F32)
        else:
            for step in range(1, at.n):
                target = lax.rem(at.dh + step, at.n)
                self.pcopy(step - 1, self.part(target), target).wait()
                total = total + self.got[step - 1].astype(F32)
        self.mid[...] = total.astype(BF16)

    def piece(self, b):
        return self.mid.at[tile(b, self.size)]

    def zcopies(self):
        at, sems = self.at, self.zsems
        dst = self.zgot.at[at.th]
        own = pltpu.make_async_copy(self.piece(at.b), dst, sems.at[0])
        near = remote(self.piece(1 - at.b), dst, sems.at[1], sems.at[4], at.sib)
        first = remote(
            self.piece(at.b), dst, sems.at[2], sems.at[5], (at.dh, at.b, 1 - at.th, at.tl)
        )
        second = remote(
            self.piece(1 - at.b), dst, sems.at[3], sems.at[5], (at.dh, 1 - at.b, 1 - at.th, at.tl)
        )
        return own, near, first, second

    def zstart(self):
        own, near, first, second = self.zcopies()

        @pl.when(self.same)
        def _():
            near.start()
            own.start()

        @pl.when(jnp.logical_not(self.same))
        def _():
            first.start()
            second.start()

    def arrival(self, th, sem):
        return remote(
            self.piece(0), self.zgot.at[th], self.zsems.at[0], self.zsems.at[sem], self.at.sib
        )

    def zsum(self):
        at = self.at
        own, near, first, second = self.zcopies()

        @pl.when(self.same)
        def _():
            near.wait_send()
            own.wait()

        @pl.when(jnp.logical_not(self.same))
        def _():
            first.wait_send()
            second.wait_send()
            self.arrival(at.th, 4).wait_recv()

        self.arrival(1 - at.th, 5).wait_recv()
        total = self.zgot[0].astype(F32) + self.zgot[1].astype(F32)
        if self.flip is None:
            for kind in range(3):
                self.out[kind][...] = total[:, kind * LANES : (kind + 1) * LANES]
        else:
            self.out[...] = total.T if self.flip else total


class Rows:
    def __init__(self, at, count):
        self.at, self.R = at, count // CHUNKS

    def at_(self, chunk, owner):
        return tile(chunk * 4 + owner, self.R)

    def whole(self, chunk):
        return pl.ds(chunk * 4 * self.R, 4 * self.R)

    def own(self, chunk):
        return pl.ds(chunk * self.R, self.R)


class Spread:
    def __init__(self, at, rows, buf, sems):
        self.at, self.rows, self.buf, self.sems = at, rows, buf, sems

    @staticmethod
    def scratch(width):
        return [pltpu.SemaphoreType.DMA((6, CHUNKS))]

    def copy(self, chunk, kind, owner):
        ref = self.buf.at[self.rows.at_(chunk, owner)]
        device = self.at.link if kind == 0 else self.at.sib
        return remote(ref, ref, self.sems.at[kind, chunk], self.sems.at[3 + kind, chunk], device)

    def start(self, chunk):
        self.copy(chunk, 0, self.at.mine).start()
        self.copy(chunk, 1, self.at.mine).start()

    def forward(self, chunk):
        self.copy(chunk, 0, self.at.links).wait_recv()
        self.copy(chunk, 2, self.at.links).start()

    def wait(self, chunk):
        self.copy(chunk, 1, self.at.sibs).wait_recv()
        self.copy(chunk, 2, self.at.diags).wait_recv()

    def finish(self):
        for chunk in range(CHUNKS):
            self.copy(chunk, 0, self.at.mine).wait_send()
            self.copy(chunk, 1, self.at.mine).wait_send()
            self.copy(chunk, 2, self.at.links).wait_send()


class Collect:
    def __init__(self, at, rows, part, sent, got, sent_far, got_far, sems):
        self.at, self.R, self.part = at, rows.R, part
        self.sent, self.got, self.sent_far, self.got_far, self.sems = sent, got, sent_far, got_far, sems

    @staticmethod
    def scratch(count, width):
        R = count // CHUNKS
        return [
            pltpu.VMEM((CHUNKS, 2 * R, width), BF16),
            pltpu.VMEM((CHUNKS, 2 * R, width), BF16),
            pltpu.VMEM((CHUNKS, R, width), BF16),
            pltpu.VMEM((CHUNKS, R, width), BF16),
        ]

    SEMS = pltpu.SemaphoreType.DMA((4, CHUNKS))

    def near(self, chunk):
        return remote(
            self.sent.at[chunk],
            self.got.at[chunk],
            self.sems.at[0, chunk],
            self.sems.at[1, chunk],
            self.at.sib,
        )

    def far(self, chunk):
        return remote(
            self.sent_far.at[chunk],
            self.got_far.at[chunk],
            self.sems.at[2, chunk],
            self.sems.at[3, chunk],
            self.at.link,
        )

    def left(self, ref, chunk):
        halves = [ref[tile(2 * chunk + b, 2 * self.R), :] for b in (self.at.b, 1 - self.at.b)]
        return jnp.concatenate(halves, axis=0)

    def put(self, chunk, span, values):
        self.part[chunk, :, span] = values[: 2 * self.R]
        self.sent[chunk, :, span] = values[2 * self.R :].astype(BF16)

    def start(self, chunk):
        self.near(chunk).start()

    def half(self, chunk, tl):
        mine = self.part[chunk, tile(tl, self.R), :]
        return mine + self.got[chunk, tile(tl, self.R), :].astype(F32)

    def forward(self, chunk):
        self.near(chunk).wait_recv()
        self.sent_far[chunk] = self.half(chunk, 1 - self.at.tl).astype(BF16)
        self.far(chunk).start()

    def take(self, chunk):
        self.far(chunk).wait_recv()
        return self.half(chunk, self.at.tl) + self.got_far[chunk].astype(F32)

    def finish(self):
        for chunk in range(CHUNKS):
            self.near(chunk).wait_send()
            self.far(chunk).wait_send()


class Take:
    def __init__(self, refs):
        self.refs = list(refs)

    def __call__(self, count=None):
        if count is None:
            return self.refs.pop(0)
        return [self.refs.pop(0) for _ in range(count)]


class Local:
    def __init__(self, sems):
        self.sems, self.used = sems, 0

    def start(self, src, dst):
        copy = pltpu.make_async_copy(src, dst, self.sems.at[self.used])
        self.used += 1
        copy.start()
        return copy


def stats(values):
    center = values - jnp.mean(values, axis=-1, keepdims=True)
    inverse = lax.rsqrt(jnp.mean(center * center, axis=-1, keepdims=True) + EPSILON)
    return center * inverse, inverse


def norm(values, gain, shift):
    return stats(values)[0] * gain + shift


def norm_back(upstream, scaled, inverse, gain):
    weighted = upstream * gain
    first_mean = jnp.mean(weighted, axis=-1, keepdims=True)
    second_mean = jnp.mean(weighted * scaled, axis=-1, keepdims=True)
    return inverse * (weighted - first_mean - scaled * second_mean)


def lane():
    return lax.broadcasted_iota(jnp.int32, (1, LANES), 1)


def turned(values, cosines, sines):
    within = lax.rem(lane(), HEAD_DIM)
    former = lax.rem(within, ROT) < ROT // 2
    half = ROT // 2
    moved = jnp.where(former, pltpu.roll(values, LANES - half, 1), pltpu.roll(values, half, 1))
    return values * cosines + moved * sines


def of_head(values, head):
    keep = (lane() // HEAD_DIM) == head % 2
    return jnp.where(keep, values, jnp.zeros_like(values))


def gelu_and_slope(u):
    size = jnp.abs(u) * 0.7071067811865476
    t = 1.0 / (1.0 + 0.3275911 * size)
    bell = jnp.exp(-0.5 * u * u)
    poly = t * (
        0.127414796
        + t * (-0.142248368 + t * (0.7107068705 + t * (-0.7265760135 + t * 0.5307027145)))
    )
    tail = poly * bell
    phi = jnp.where(u < 0, tail, 1.0 - tail)
    return u * phi, phi + u * bell * RSQRT_2PI


def tables(places, cosines, sines, rows):
    row = lax.broadcasted_iota(jnp.int32, (HEAD_DIM, places.shape[1]), 0)
    which = row // ROT
    place = jnp.where(
        which == 0, places[0:1, :], jnp.where(which == 1, places[1:2, :], places[2:3, :])
    )
    step = lax.rem(row, ROT // 2).astype(F32) / (ROT // 2)
    frequency = jnp.where(which < 3, jnp.exp(step * -9.210340371976184), 0.0)
    angle = place * frequency
    sign = jnp.where(lax.rem(row, ROT) < ROT // 2, -1.0, 1.0)
    for table, values in ((cosines, jnp.cos(angle)), (sines, jnp.sin(angle) * sign)):
        turned_values = jnp.concatenate([values, values], axis=0).T
        for k in range(CHUNKS):
            for owner in range(4):
                start = (owner * CHUNKS + k) * rows.R
                table[pl.ds((k * 4 + owner) * rows.R, rows.R), :] = turned_values[
                    start : start + rows.R, :
                ]


def forward_kernel(n, refs):
    take = Take(refs)
    tokens, cotangent, clip_mask, positions = take(4)
    triple_in, triple_bias, exit_in, expand_in, expand_bias, shrink_in = take(6)
    norm_gain, norm_shift, branch_bias = take(3)
    upstream, cosines_out, sines_out, small_out, em_out = take(5)
    outs = [take(15) for _ in range(LAYERS)]
    x, smalls, small, parameters, turned_tokens, turned_cotangent, cosines, sines = take(8)
    exit_turned, shrink_turned, triple_turned, em = take(4)
    weights = [take(4) for _ in range(LAYERS)]
    n1, n2, qp, kp, vp, vt, o, g, slope, lse, ot, part = take(12)
    spread_sems = take(2 * LAYERS)
    one_buffers, two_buffers = take(4), take(4)
    collect_sems = take(2 * LAYERS)
    gather_sems = [[take(2) for _ in range(4)] for _ in range(LAYERS)]
    em_sems, token_sems, small_sems, cotangent_sems, local_sems = take(5)

    at = Place()
    local = Local(local_sems)
    rows = Rows(at, x.shape[0])
    slices = [
        [source.at[l] for source in (triple_turned, exit_turned, expand_in, shrink_turned)]
        for l in range(LAYERS)
    ]
    gathers = [
        [Gather(at, *triple) for triple in zip(slices[l], weights[l], *zip(*gather_sems[l]))]
        for l in range(LAYERS)
    ]
    smalls[...] = jnp.zeros_like(smalls)
    smalls[0:3, :] = positions[...].astype(F32)
    smalls[3:4, :] = jnp.broadcast_to(clip_mask[...].astype(F32), (1, smalls.shape[1]))
    for l in range(LAYERS):
        for kind in range(3):
            width = triple_bias.shape[2]
            columns = slice(kind * width, (kind + 1) * width)
            smalls[4 + l : 5 + l, columns] = triple_bias[kind, l : l + 1, :].astype(F32)
            triple_turned[l, :, columns] = triple_in[l, kind]
        smalls[6 + l : 7 + l, :] = expand_bias[l : l + 1, :].astype(F32)
    swap_small = Swap(at, smalls, small, small_sems)
    swap_tokens = [
        Swap(
            at,
            tokens.at[rows.own(k)],
            turned_tokens.at[rows.own(k)],
            token_sems.at[k],
        )
        for k in range(CHUNKS)
    ]
    swap_cotangent = Swap(at, cotangent, turned_cotangent, cotangent_sems)

    at.barrier()
    gathers[0][0].zstart()
    swap_small.start()
    for swap in swap_tokens:
        swap.start()
    for l in range(LAYERS):
        exit_turned[l] = exit_in[l].T
        shrink_turned[l] = shrink_in[l].T
        for index, source in enumerate((norm_gain, norm_shift, branch_bias)):
            parameters[8 * l + 2 * index : 8 * l + 2 * index + 2, :] = source[l].astype(F32)
    swap_small.wait()
    tables(small, cosines, sines, rows)
    saves = [
        local.start(*pair)
        for pair in ((cosines, cosines_out), (sines, sines_out), (small, small_out))
    ]
    spread_em = Spread(at, rows, em, em_sems)

    def begin(l):
        spread = [Spread(at, rows, buf, spread_sems[2 * l + i]) for i, buf in enumerate((n1, n2))]
        collect = [
            Collect(at, rows, part, *buffers, collect_sems[2 * l + i])
            for i, buffers in enumerate((one_buffers, two_buffers))
        ]
        return spread + collect

    stages = [begin(l) for l in range(LAYERS)]

    def row(l, index):
        return parameters[8 * l + index : 8 * l + index + 1, :]

    def first_norm(l, k):
        n1[rows.at_(k, at.mine), :] = norm(x[rows.own(k), :], row(l, 0), row(l, 2)).astype(BF16)
        stages[l][0].start(k)

    def project(l, k):
        stages[l][0].wait(k)
        whole = rows.whole(k)
        wa = weights[l][0]
        for kind in range(3):
            columns = slice(2 * kind * LANES, 2 * (kind + 1) * LANES)
            bias = small[4 + l : 5 + l, columns]
            both = dot(n1[whole, :], wa[:, columns], NN) + bias
            for pair in range(2):
                t = both[:, pair * LANES : (pair + 1) * LANES]
                if kind < 2:
                    t = turned(t, cosines[whole, :], sines[whole, :])
                if kind == 0:
                    qp[pair, whole, :] = (t * (SCALE * LOG2E)).astype(BF16)
                elif kind == 1:
                    kp[pair, whole, :] = t.astype(BF16)
                else:
                    vp[pair, whole, :] = t.astype(BF16)
                    vt[pl.ds(pair * LANES, LANES), whole] = t.T.astype(BF16)

    def attention(k):
        whole = rows.whole(k)

        def head(h, carry):
            scores = dot(kp[h // 2], of_head(qp[h // 2, whole, :], h), NT)
            highest = jnp.max(scores, axis=0, keepdims=True)
            weights = jnp.exp2(scores - highest)
            total = jnp.sum(weights, axis=0, keepdims=True)
            spans = tile(h, HEAD_DIM)
            ot[spans, :] = dot(vt[spans, :], weights.astype(BF16), NN) / total
            lse[pl.ds(h, 1), whole] = highest + jnp.log2(total)
            return carry

        lax.fori_loop(0, 4, head, 0)
        o[whole, :] = ot[...].T.astype(BF16)

    def leave(l, k):
        wb, collect = weights[l][1], stages[l][2]
        left = collect.left(o, k)

        def columns(j, carry):
            span = tile(j, 256)
            collect.put(k, span, dot(left, wb[span, :], NT))
            return carry

        lax.fori_loop(0, part.shape[2] // 256, columns, 0, unroll=True)
        collect.start(k)

    def second_norm(l, k):
        own = rows.own(k)
        x[own, :] = x[own, :] + (stages[l][2].take(k) + row(l, 4))
        n2[rows.at_(k, at.mine), :] = norm(x[own, :], row(l, 1), row(l, 3)).astype(BF16)
        stages[l][1].start(k)

    def up(l, k):
        whole = rows.whole(k)
        wc = weights[l][2]
        stages[l][1].wait(k)

        def columns(j, carry):
            span = tile(j, 256)
            u = dot(n2[whole, :], wc[:, span], NN) + small[pl.ds(6 + l, 1), span]
            active, grade = gelu_and_slope(u)
            g[whole, span] = active.astype(BF16)
            slope[whole, span] = grade.astype(BF16)
            return carry

        lax.fori_loop(0, wc.shape[1] // 256, columns, 0, unroll=True)

    def down(l, k):
        wd, collect = weights[l][3], stages[l][3]
        left = collect.left(g, k)

        def outputs(j, carry):
            span = tile(j, 256)
            collect.put(k, span, dot(left, wd[span, :], NT))
            return carry

        lax.fori_loop(0, part.shape[2] // 256, outputs, 0, unroll=True)
        collect.start(k)

    def end(l, k):
        own = rows.own(k)
        x[own, :] = x[own, :] + (stages[l][3].take(k) + row(l, 5))
        if l + 1 < LAYERS:
            first_norm(l + 1, k)

    A, B, C, D = range(4)

    def begin_plane(gather):
        gather.zwait()
        gather.pstart()

    begin_plane(gathers[0][A])
    for k in range(CHUNKS):
        swap_tokens[k].wait()
        x[rows.own(k), :] = turned_tokens[rows.own(k), :].astype(F32)
        first_norm(0, k)
    for gather in gathers[0][B:]:
        gather.zstart()
    gathers[0][A].pforward()
    pending = []
    for l in range(LAYERS):
        hidden_out, middle_out, *full_outs = outs[l][:6]
        n1_out, n2_out, qp_out, kp_out, vp_out, o_out, g_out, slope_out, lse_out = outs[l][6:]
        spread_one, spread_two, collect_one, collect_two = stages[l]
        now = gathers[l]
        following = gathers[l + 1] if l + 1 < LAYERS else None
        save_x = local.start(x, hidden_out)
        for k in range(CHUNKS):
            spread_one.forward(k)
        now[A].pwait()
        if l == 0:
            begin_plane(now[B])
        else:
            now[B].pforward()
            begin_plane(now[C])
        for save in pending:
            save.wait()
        for k in range(CHUNKS):
            project(l, k)
        spread_one.finish()
        save_n1 = local.start(n1, n1_out)
        pending = [
            local.start(*pair) for pair in ((qp, qp_out), (kp, kp_out), (vp, vp_out))
        ]
        if l == 0:
            now[B].pforward()
        attention(0)
        now[B].pwait()
        leave(l, 0)
        if l == 0:
            begin_plane(now[C])
            following[A].zstart()
            following[B].zstart()
        attention(1)
        collect_one.forward(0)
        leave(l, 1)
        if l:
            begin_plane(now[D])
            now[C].pforward()
        save_x.wait()
        attention(2)
        collect_one.forward(1)
        leave(l, 2)
        second_norm(l, 0)
        attention(3)
        collect_one.forward(2)
        leave(l, 3)
        if l == 0:
            now[C].pforward()
            begin_plane(now[D])
        if not following:
            swap_cotangent.wait()
            upstream[...] = turned_cotangent[...].astype(F32) * small[3:4, :]
            for k in range(CHUNKS):
                em[rows.at_(k, at.mine), :] = upstream[rows.own(k), :].astype(BF16)
        second_norm(l, 1)
        collect_one.forward(3)
        second_norm(l, 2)
        second_norm(l, 3)
        if following:
            following[C].zstart()
        else:
            for k in range(CHUNKS):
                spread_em.start(k)
        save_x = local.start(x, middle_out)
        pending += [local.start(o, o_out), local.start(lse, lse_out)]
        save_n1.wait()
        spread_two.forward(0)
        now[C].pwait()
        for k in range(CHUNKS):
            up(l, k)
            if k == 1 and following:
                begin_plane(following[A])
            if k == 1 and not following:
                now[D].pforward()
            if k + 1 < CHUNKS:
                spread_two.forward(k + 1)
        if following:
            now[D].pforward()
        else:
            for k in range(CHUNKS):
                spread_em.forward(k)
        pending += [local.start(*pair) for pair in ((n2, n2_out), (g, g_out), (slope, slope_out))]
        save_x.wait()
        spread_two.finish()
        now[D].pwait()
        pending += [local.start(*pair) for pair in zip(weights[l], full_outs)]
        if not following:
            collect_one.finish()
            for k in range(CHUNKS):
                spread_em.wait(k)
            spread_em.finish()
            pending.append(local.start(em, em_out))
            continue
        for k in range(CHUNKS):
            down(l, k)
            if k:
                collect_two.forward(k - 1)
            if k == 1:
                begin_plane(following[B])
            if k > 1:
                end(l, k - 2)
        collect_two.forward(CHUNKS - 1)
        end(l, CHUNKS - 2)
        following[A].pforward()
        end(l, CHUNKS - 1)
        following[D].zstart()
        swap_cotangent.start()
        collect_one.finish()
        collect_two.finish()
    for save in saves + pending:
        save.wait()


def backward_kernel(n, refs):
    take = Take(refs)
    upstream, gain_in, bias_in, small, em_in = take(5)
    ins = [take(15) for _ in range(LAYERS)]
    cosines_in, sines_in = take(2)
    mixed_out, grad_out, triple_out, triple_bias_out, exit_out, expand_out = take(6)
    expand_bias_out, shrink_out, gain_out, shift_out, bias_out = take(5)
    e, xs, wa, wb, wc, wd = take(6)
    em, ea, n2, qp, kp, vp, kt, o, g, du, lse = take(11)
    dk, dv, dqt, do, part, gd, ge, vectors, cosines, sines = take(10)
    dt, gt = take(2), take(2)
    mixed, turned_mixed, low_grad_own, turned_grad = take(4)
    part_last, last_got, last_sems = take(), take(2), take()
    spread_sems = take(2 * LAYERS)
    one_buffers, two_buffers = take(4), take(4)
    collect_sems = take(2 * LAYERS)
    scatter_buffers = [take(2) for _ in range(5)]
    scatter_layers = [[take(3) for _ in range(5)] for _ in range(LAYERS)]
    mixed_sems, grad_sems = take(2)
    plane, column, plane_sems, column_sems = take(4)
    local_sems = take()

    at = Place()
    local = Local(local_sems)
    rows = Rows(at, e.shape[0])

    def load(l, name):
        where = {
            "hidden": (0, xs),
            "middle": (1, xs),
            "a": (2, wa),
            "b": (3, wb),
            "c": (4, wc),
            "d": (5, wd),
            "n1": (6, g),
            "n2": (7, n2),
            "q": (8, qp),
            "k": (9, kp),
            "v": (10, vp),
            "o": (11, o),
            "g": (12, g),
            "slope": (13, du),
            "lse": (14, lse),
        }
        index, target = where[name]
        loads[(l, name)] = local.start(ins[l][index], target)

    def ready(l, *names):
        for name in names:
            loads.pop((l, name)).wait()

    loads = {}
    top = LAYERS - 1
    load_em = local.start(em_in, em)
    load_e = local.start(upstream, e)
    for name in ("d", "slope", "c", "middle", "g", "n2", "b", "q", "k", "v", "o", "lse", "a"):
        load(top, name)
    load_tables = [local.start(cosines_in, cosines), local.start(sines_in, sines)]

    cubes = [(db, dth, dtl) for db in range(2) for dth in range(2) for dtl in range(2)][1:]

    def flipped(flips):
        return [jnp.abs(coordinate - flip) for coordinate, flip in zip(at.me[1:], flips)]

    barrier = pltpu.get_barrier_semaphore()
    greeted = [(at.dh, *flipped(flips)) for flips in cubes]
    greeted += [at.peer(step) for step in range(1, n)]
    for device in greeted:
        pl.semaphore_signal(barrier, inc=1, device_id=device, device_id_type=MESH)
    pl.semaphore_wait(barrier, len(greeted))

    spreads = [
        [Spread(at, rows, buf, spread_sems[2 * l + i]) for i, buf in enumerate((em, ea))]
        for l in range(LAYERS)
    ]
    collects = [
        [
            Collect(at, rows, part, *buffers, collect_sems[2 * l + i])
            for i, buffers in enumerate((one_buffers, two_buffers))
        ]
        for l in range(LAYERS)
    ]
    def triple_columns(l, pair):
        return [triple_out.at[l, kind, :, pl.ds(pair * LANES, LANES)] for kind in range(3)]

    def pieces(l):
        return (
            (gt[0], triple_columns(l, 0), None),
            (gt[1], triple_columns(l, 1), None),
            (ge, exit_out.at[l], True),
            (wd, expand_out.at[l], False),
            (gd, shrink_out.at[l], True),
        )

    scatters = [
        [
            Scatter(at, *piece, *buffers, *own)
            for piece, buffers, own in zip(pieces(l), scatter_buffers, scatter_layers[l])
        ]
        for l in range(LAYERS)
    ]
    collect_last = Collect(
        at, rows, part_last, two_buffers[0], last_got[0], two_buffers[2], last_got[1], last_sems
    )
    swap_mixed = Swap(at, mixed, turned_mixed, mixed_sems)
    swap_grads = [
        Swap(
            at, low_grad_own.at[rows.own(k)], turned_grad.at[rows.own(k)], grad_sems.at[k]
        )
        for k in range(CHUNKS)
    ]
    vectors[...] = jnp.zeros_like(vectors)

    def add(l, row, values):
        vectors[8 * l + row : 8 * l + row + 1, : values.shape[1]] += jnp.sum(
            values.astype(F32), axis=0, keepdims=True
        )

    def weight_grad(left, right, out):
        def block(j, carry):
            span = tile(j, 256)
            out[span, :] = dot(left[:, span], right[...], TN).astype(BF16)
            return carry

        lax.fori_loop(0, left.shape[1] // 256, block, 0, unroll=True)

    def send_branch(l, k):
        low = e[rows.own(k), :].astype(BF16)
        em[rows.at_(k, at.mine), :] = low
        spreads[l][0].start(k)
        add(l, 5, low)

    def shrink_back(l, k):
        if l < top:
            spreads[l][0].forward(k)
            spreads[l][0].wait(k)
        whole = rows.whole(k)
        collect = collects[l][0]

        def columns(j, carry):
            span = tile(j, 256)
            active_grad = dot(em[whole, :], wd[:, span], NN)
            du[whole, span] = (active_grad * du[whole, span].astype(F32)).astype(BF16)
            return carry

        lax.fori_loop(0, wd.shape[1] // 256, columns, 0, unroll=True)
        add(l, 6, du[whole, :])
        left = collect.left(du, k)

        def outputs(j, carry):
            span = tile(j, 256)
            collect.put(k, span, dot(left, wc[span, :], NT))
            return carry

        lax.fori_loop(0, part.shape[2] // 256, outputs, 0, unroll=True)
        collect.start(k)

    def norm_step(l, k, which):
        own = rows.own(k)
        scaled, inverse = stats(xs[own, :])
        grads = collects[l][1 - which].take(k)
        add(l, which, grads * scaled)
        add(l, 2 + which, grads)
        gain = gain_in[l, which : which + 1, :].astype(F32)
        e[own, :] = e[own, :] + norm_back(grads, scaled, inverse, gain)

    def middle_step(l, k):
        norm_step(l, k, 1)
        low = e[rows.own(k), :].astype(BF16)
        ea[rows.at_(k, at.mine), :] = low
        spreads[l][1].start(k)
        add(l, 4, low)

    def first_step(l, k):
        norm_step(l, k, 0)
        if l:
            send_branch(l - 1, k)
        else:
            low_grad_own[rows.own(k), :] = e[rows.own(k), :].astype(BF16)
            swap_grads[k].start()

    def branch_last(k):
        left = collect_last.left(g, k)

        def outputs(j, carry):
            span = tile(j, 256)
            collect_last.put(k, span, dot(left, wd[span, :], NT))
            return carry

        lax.fori_loop(0, part.shape[2] // 256, outputs, 0, unroll=True)
        collect_last.start(k)

    def end_last(k):
        own = rows.own(k)
        bias = bias_in[top, 1:2, :].astype(F32)
        hidden = xs[own, :] + (collect_last.take(k) + bias)
        mixed[own, :] = (hidden * small[3:4, :]).astype(BF16)

    def attention_back(l, pair, k):
        whole = rows.whole(k)
        if pair == 0:
            spreads[l][1].wait(k)
            do[whole, :] = dot(ea[whole, :], wb[...], NN).astype(BF16)
        lanes = slice(pair * LANES, (pair + 1) * LANES)
        dop = do[whole, lanes]
        product = dop.astype(F32) * o[whole, lanes].astype(F32)
        high = product.astype(BF16)
        rest = (product - high.astype(F32)).astype(BF16)
        kept = []
        for half in range(2):
            h = 2 * pair + half
            pick = jnp.broadcast_to(((lane() // HEAD_DIM) == half).astype(BF16), (8, LANES))
            center = dot(pick, high, NT) + dot(pick, rest, NT)
            qh = of_head(qp[pair, whole, :], half)
            doh = of_head(dop, half)
            scores = dot(kp[pair], qh, NT)
            chances = jnp.exp2(scores - lse[h : h + 1, whole])
            chance_grad = dot(vp[pair], doh, NT)
            score_grad = (chances * (chance_grad - center[0:1, :])).astype(BF16)
            kept.append((chances.astype(BF16), doh, score_grad, qh))
            spans = slice(h * HEAD_DIM, (h + 1) * HEAD_DIM)
            dqt[half * HEAD_DIM : (half + 1) * HEAD_DIM, :] = dot(kt[spans, :], score_grad, NN)
        low_chances, dohs, score_grads, qhs = [
            jnp.concatenate(two, axis=axis) for two, axis in zip(zip(*kept), (1, 0, 1, 0))
        ]
        dv[pair] += dot(low_chances, dohs, NN)
        dk[pair] += dot(score_grads, qhs, NN)
        dq = dqt[...].T * SCALE
        dt[pair][whole, :LANES] = turned(dq, cosines[whole, :], -sines[whole, :]).astype(BF16)

    def pair_done(l, pair):
        dt[pair][:, LANES : 2 * LANES] = turned(
            dk[pair] * LN2, cosines[...], -sines[...]
        ).astype(BF16)
        dt[pair][:, 2 * LANES :] = dv[pair].astype(BF16)
        weight_grad(g, dt[pair], gt[pair])
        scatters[l][pair].pstart()

    def triple_sum(l):
        width = 2 * LANES
        for pair in range(2):
            sums = jnp.sum(dt[pair][...].astype(F32), axis=0, keepdims=True)
            for kind in range(3):
                start = kind * width + pair * LANES
                vectors[8 * l + 7 : 8 * l + 8, start : start + LANES] = sums[
                    :, kind * LANES : (kind + 1) * LANES
                ]

    def projection_back(l, k):
        collect = collects[l][1]
        left = jnp.concatenate(
            [
                collect.left(dt[pair], k)[:, kind * LANES : (kind + 1) * LANES]
                for kind in range(3)
                for pair in range(2)
            ],
            axis=1,
        )

        def outputs(j, carry):
            span = tile(j, 256)
            collect.put(k, span, dot(left, wa[span, :], NT))
            return carry

        lax.fori_loop(0, part.shape[2] // 256, outputs, 0, unroll=True)
        collect.start(k)

    load_e.wait()
    load_em.wait()
    for k in range(CHUNKS):
        add(top, 5, em[rows.at_(k, at.mine), :])
    for l in reversed(range(LAYERS)):
        spread_one, spread_two = spreads[l]
        collect_one, collect_two = collects[l]
        st0, st1, se, sc, sd = scatters[l]
        previous = scatters[l + 1] if l < top else None
        ready(l, "d", "slope", "c", "middle")
        for k in range(CHUNKS):
            shrink_back(l, k)
            if k:
                collect_one.forward(k - 1)
            if k > 1:
                middle_step(l, k - 2)
        collect_one.forward(CHUNKS - 1)
        if previous:
            spread_one.finish()
            previous[1].psum()
        ready(l, "g")
        if l == top:
            branch_last(0)
            branch_last(1)
        weight_grad(em, g, gd)
        sd.pstart()
        middle_step(l, CHUNKS - 2)
        middle_step(l, CHUNKS - 1)
        if l == top:
            branch_last(2)
            branch_last(3)
        else:
            load(l, "hidden")
        load(l, "n1")
        ready(l, "n2")
        weight_grad(n2, du, wd)
        sc.pstart()
        if l:
            load(l - 1, "slope")
            load(l - 1, "c")
            load(l - 1, "n2")
        ready(l, "b", "q", "k", "v", "o", "lse")
        for pair in range(2):
            kt[pl.ds(pair * LANES, LANES), :] = kp[pair].astype(F32).T.astype(BF16)
        dk[...] = jnp.zeros_like(dk)
        dv[...] = jnp.zeros_like(dv)
        if l == top:
            for copy in load_tables:
                copy.wait()
        spread_two.forward(0)
        spread_two.forward(1)
        attention_back(l, 0, 0)
        spread_two.forward(2)
        spread_two.forward(3)
        sd.pforward()
        if l == top:
            collect_last.forward(0)
            collect_last.forward(1)
        else:
            previous[1].zstart()
        attention_back(l, 0, 1)
        if l == top:
            collect_last.forward(2)
            collect_last.forward(3)
        sc.pforward()
        attention_back(l, 0, 2)
        sd.psum()
        sd.zstart()
        attention_back(l, 0, 3)
        spread_two.finish()
        weight_grad(ea, o, ge)
        se.pstart()
        ready(l, "n1")
        pair_done(l, 0)
        sc.psum()
        sc.zstart()
        attention_back(l, 1, 0)
        if l == top:
            for k in range(CHUNKS):
                end_last(k)
            load(l, "hidden")
            swap_mixed.start()
        else:
            previous[1].zsum()
        attention_back(l, 1, 1)
        se.pforward()
        st0.pforward()
        attention_back(l, 1, 2)
        se.psum()
        se.zstart()
        attention_back(l, 1, 3)
        st0.psum()
        st0.zstart()
        ready(l, "a")
        if l == top:
            collect_last.finish()
        pair_done(l, 1)
        for k in range(CHUNKS):
            projection_back(l, k)
            if k:
                collect_two.forward(k - 1)
        collect_two.forward(CHUNKS - 1)
        triple_sum(l)
        ready(l, "hidden")
        if l:
            for name in ("d", "g", "b", "q", "k", "v", "o", "lse", "a"):
                load(l - 1, name)
        collect_one.finish()
        sd.zsum()
        first_step(l, 0)
        first_step(l, 1)
        st1.pforward()
        first_step(l, 2)
        first_step(l, 3)
        if l:
            load(l - 1, "middle")
        collect_two.finish()
        for scatter in (sc, se, st0):
            scatter.zsum()

    last = scatters[0][1]
    plane[at.dh] = vectors[...]

    def plane_copy(step, slot):
        ref = plane.at[slot]
        return remote(ref, ref, plane_sems.at[0, step], plane_sems.at[1, step], at.peer(step))

    for step in range(1, n):
        plane_copy(step, at.dh).start()
    last.psum()
    last.zstart()
    for step in range(1, n):
        plane_copy(step, at.dh).wait_send()
        plane_copy(step, lax.rem(at.dh + n - step, n)).wait_recv()
    total = plane[0]
    for index in range(1, n):
        total = total + plane[index]

    def slot(b, th, tl):
        return 4 * b + 2 * th + tl

    mine = slot(*at.me[1:])
    column[mine] = total

    def column_copy(index, flips, where):
        ref = column.at[where]
        device = (at.dh, *flipped(flips))
        return remote(ref, ref, column_sems.at[0, index], column_sems.at[1, index], device)

    for index, flips in enumerate(cubes):
        column_copy(index, flips, mine).start()
    swap_mixed.wait()
    save_mixed = local.start(turned_mixed, mixed_out)
    for index, flips in enumerate(cubes):
        column_copy(index, flips, mine).wait_send()
        column_copy(index, flips, slot(*flipped(flips))).wait_recv()
    total = column[0]
    for index in range(1, 8):
        total = total + column[index]
    own = column[slot(at.th, 0, at.tl)] + column[slot(at.th, 1, at.tl)]
    width = triple_bias_out.shape[2]
    for l in range(LAYERS):
        gain_out[l] = total[8 * l : 8 * l + 2, :]
        shift_out[l] = total[8 * l + 2 : 8 * l + 4, :]
        bias_out[l] = total[8 * l + 4 : 8 * l + 6, :]
        expand_bias_out[l : l + 1, :] = own[8 * l + 6 : 8 * l + 7, :]
        for kind in range(3):
            triple_bias_out[kind, l : l + 1, :] = own[
                8 * l + 7 : 8 * l + 8, kind * width : (kind + 1) * width
            ]
    for k in range(CHUNKS):
        swap_grads[k].wait()
    save_grad = local.start(turned_grad, grad_out)
    last.zsum()
    save_mixed.wait()
    save_grad.wait()


def finish_kernel(*refs):
    half = len(refs) // 2
    for source, target in zip(refs[:half], refs[half:]):
        if len(source.shape) < len(target.shape):
            target[:, 0, :] = source[...].astype(F32)
        else:
            target[...] = source[...]


def call(body, args, vmem_in, outs, vmem_out, scratch, collective_id, name, flops=0):
    def kernel(*refs):
        body(refs)

    in_specs = [VMEM if index in vmem_in else ANY for index in range(len(args))]
    out_specs = [VMEM if index in vmem_out else ANY for index in range(len(outs))]
    return pl.pallas_call(
        kernel,
        out_shape=outs,
        in_specs=in_specs,
        out_specs=out_specs,
        scratch_shapes=scratch,
        compiler_params=pltpu.CompilerParams(
            collective_id=collective_id, has_side_effects=True, vmem_limit_bytes=VMEM_LIMIT
        ),
        name=name,
    )(*args)


def shards(
    n,
    tokens,
    cotangent,
    clip_mask,
    positions,
    triple_weight,
    triple_bias,
    exit_weight,
    expand_weight,
    expand_bias,
    shrink_weight,
    norm_gain,
    norm_shift,
    branch_bias,
):
    count, _, depth = tokens.shape
    seq = 4 * count
    size = triple_weight.shape[1]
    local = triple_weight.shape[3]
    inner = expand_weight.shape[2]
    wide = 3 * local
    pairs = local // LANES
    R = count // CHUNKS
    V, DMA, shape = pltpu.VMEM, pltpu.SemaphoreType.DMA, jax.ShapeDtypeStruct
    wides = (wide, local, inner, inner)
    pair_shape = (pairs, seq, LANES)
    args = [
        tokens[:, 0, :],
        cotangent[:, 0, :],
        clip_mask[:, None],
        positions[:, 0, :],
        triple_weight.transpose(0, 2, 1, 3),
        triple_bias.transpose(1, 0, 2),
        exit_weight,
        expand_weight,
        expand_bias,
        shrink_weight,
        norm_gain,
        norm_shift,
        branch_bias,
    ]
    outs = [
        shape((count, depth), F32),
        shape((seq, LANES), F32),
        shape((seq, LANES), F32),
        shape((8, depth), F32),
        shape((seq, depth), BF16),
    ]
    for _ in range(LAYERS):
        outs += [shape((count, depth), F32)] * 2
        outs += [shape((depth, width), BF16) for width in wides]
        outs += [shape((seq, depth), BF16)] * 2
        outs += [shape(pair_shape, BF16)] * 3
        outs += [shape((seq, local), BF16)]
        outs += [shape((seq, inner), BF16)] * 2
        outs += [shape((8, seq), F32)]
    scratch = [
        V((count, depth), F32),
        V((8, depth), F32),
        V((8, depth), F32),
        V((8 * LAYERS, depth), F32),
        V((count, depth), BF16),
        V((count, depth), BF16),
        V((seq, LANES), F32),
        V((seq, LANES), F32),
        V((LAYERS, size, local), BF16),
        V((LAYERS, size, inner), BF16),
        V((LAYERS, size, wide), BF16),
        V((seq, depth), BF16),
    ]
    for _ in range(LAYERS):
        scratch += [V((depth, width), BF16) for width in wides]
    scratch += [V((seq, depth), BF16)] * 2
    scratch += [V(pair_shape, BF16)] * 3
    scratch += [V((local, seq), BF16), V((seq, local), BF16)]
    scratch += [V((seq, inner), BF16)] * 2
    scratch += [V((8, seq), F32), V((local, 4 * R), F32), V((CHUNKS, 2 * R, depth), F32)]
    scratch += Spread.scratch(depth) * (2 * LAYERS)
    scratch += Collect.scratch(count, depth) * 2
    scratch += [Collect.SEMS] * (2 * LAYERS)
    scratch += Gather.scratch(n) * (4 * LAYERS)
    scratch += Spread.scratch(depth)
    scratch += [DMA((CHUNKS, 3)), DMA((3,)), DMA((3,)), DMA((48,))]
    results = call(
        functools.partial(forward_kernel, n),
        args,
        tuple(range(len(args))),
        outs,
        (0,),
        scratch,
        1,
        "forward",
    )
    upstream, cosines, sines, small, em = results[:5]
    args = [upstream, norm_gain, branch_bias, small, em, *results[5:], cosines, sines]
    outs = [
        shape((count, depth), BF16),
        shape((count, depth), BF16),
        shape((LAYERS, 3, size, local), F32),
        shape((3, LAYERS, local), F32),
        shape(exit_weight.shape, F32),
        shape(expand_weight.shape, F32),
        shape(expand_bias.shape, F32),
        shape(shrink_weight.shape, F32),
        shape(norm_gain.shape, F32),
        shape(norm_shift.shape, F32),
        shape(branch_bias.shape, F32),
    ]
    scratch = [V((count, depth), F32)] * 2
    scratch += [V((depth, width), BF16) for width in wides]
    scratch += [V((seq, depth), BF16)] * 3
    scratch += [V(pair_shape, BF16)] * 3
    scratch += [V((local, seq), BF16), V((seq, local), BF16)]
    scratch += [V((seq, inner), BF16)] * 2
    scratch += [V((8, seq), F32)]
    scratch += [V(pair_shape, F32)] * 2
    scratch += [V((LANES, 4 * R), F32), V((seq, local), BF16), V((CHUNKS, 2 * R, depth), F32)]
    scratch += [V((depth, inner), BF16), V((depth, local), BF16)]
    scratch += [V((8 * LAYERS, depth), F32), V((seq, LANES), F32), V((seq, LANES), F32)]
    scratch += [V((seq, 3 * LANES), BF16)] * 2 + [V((depth, 3 * LANES), BF16)] * 2
    scratch += [V((count, depth), BF16)] * 4
    scratch += [V((CHUNKS, 2 * R, depth), F32)] + Collect.scratch(count, depth)[1::2] + [Collect.SEMS]
    scratch += Spread.scratch(depth) * (2 * LAYERS)
    scratch += Collect.scratch(count, depth) * 2
    scratch += [Collect.SEMS] * (2 * LAYERS)
    widths = (3 * LANES, 3 * LANES, local, inner, inner)
    for width in widths:
        scratch += Scatter.scratch(n, depth, width)
    for _ in range(LAYERS):
        for width in widths:
            scratch += Scatter.layer_scratch(n, depth, width)
    scratch += [DMA((3,)), DMA((CHUNKS, 3))]
    scratch += [V((n, 8 * LAYERS, depth), F32), V((8, 8 * LAYERS, depth), F32)]
    scratch += [DMA((2, n)), DMA((2, 7)), DMA((48,))]
    results = call(
        functools.partial(backward_kernel, n),
        args,
        (1, 2, 3),
        outs,
        tuple(range(2, len(outs))),
        scratch,
        2,
        "backward",
    )
    outs = [shape((count, 1, depth), F32)] * 2 + [shape(r.shape, F32) for r in results[2:]]
    mixed, grad, triple_total, bias_total, *others = pl.pallas_call(
        finish_kernel, out_shape=outs, name="finish"
    )(*results)
    return (
        mixed,
        grad,
        triple_total.transpose(0, 2, 1, 3),
        bias_total.transpose(1, 0, 2),
        *others,
    )


def solution(mesh):
    n = mesh.shape["dp"] // 2
    fine = jax.sharding.Mesh(
        mesh.devices.reshape(n, 2, mesh.shape["tensor"] // 2, 2), ("dh", "b", "th", "tl")
    )
    dp, tensor = ("dh", "b"), ("th", "tl")
    return jax.shard_map(
        functools.partial(shards, n),
        mesh=fine,
        in_specs=(
            P(tensor, dp, None),
            P(tensor, dp, None),
            P(dp),
            P(None, dp, None),
            P(None, dp, None, tensor),
            P(None, None, tensor),
            P(None, tensor, dp),
            P(None, dp, tensor),
            P(None, tensor),
            P(None, tensor, dp),
            P(),
            P(),
            P(),
        ),
        out_specs=(
            P(tensor, dp, None),
            P(tensor, dp, None),
            P(None, dp, None, tensor),
            P(None, None, tensor),
            P(None, tensor, dp),
            P(None, dp, tensor),
            P(None, tensor),
            P(None, tensor, dp),
            P(),
            P(),
            P(),
        ),
        check_vma=False,
    )
```
